512 devices in a mesh: grp: 16 (over y, x_hi, core), blk: 32 (over x_lo, z).
Axes of the slice: x: 4 (x_hi: 2, x_lo: 2; x = x_hi * 2 + x_lo), y: 4, z: 16, core: 2. Of those that a mesh axis runs over, the one named last changes fastest.
Arguments:
- queries: bfloat16 [16384, 5120], P(('grp', 'blk')), may hold values from -8 to 8
- page_table: int32 [16384, 4], P(('grp', 'blk')), may hold values from 0 to 24575, as said below
- suffix_len: int32 [16384], P(('grp', 'blk')), may hold values from 0 to 64
- place: int32 [24576], P('grp'), may hold values from 0 to 24575, as said below
- suffix_keys: bfloat16 [24576, 16, 1024], P(('grp', 'blk')), may hold values from -6 to 6
- suffix_values: bfloat16 [24576, 16, 1024], P(('grp', 'blk')), may hold values from -5 to 5
- prefix_keys: bfloat16 [1024, 1024], P('blk'), may hold values from -5 to 5
- prefix_values: bfloat16 [1024, 1024], P('blk'), may hold values from -5 to 5
Outputs:
- attention: bfloat16 [16384, 5120], P(('grp', 'blk'))
The draws below stay inside these ranges and needn't reach their ends.
Inputs may be any that keep to these rules, and one draw needn't show every extreme that they name: `page_table`: only the first ceil(suffix_len[r] / 16) entries of row r are used, and used entries name distinct pages. The requests and pool rows held on one index of grp form a group; every entry of a request names a page number whose pool row place puts in its own group. Among the used entries of one device's requests, at most 2 name pages whose rows lie on any one other device of the group; in every draw some device has exactly 2 such pages on every other device of its group. `place`: A permutation of the page numbers that maps each group's page numbers onto that group's pool rows.
All inputs are finite; a program needn't handle non-finite values.
Results may differ from the reference program's by a relative error of at most 0.02.
Values may be sent and summed in bfloat16 or wider, within the bound.
No kernel may reach another device: no remote copies, remote signals or barrier semaphores. Data moves between devices by JAX's collectives and lax.ppermute only.
A program may use at most 128 MiB of HBM per device.

```python
import jax
import jax.numpy as jnp
from jax import lax

QH = 40
KVH = 8
HD = 128
PAGE = 16
MAXP = 4
CAP = 2
POOL_DEV = 48
REQ_DEV = 32
PRE_DEV = 32
PREFIX = 1024
REQUESTS = 16384
PAGES = 24576
N_GRP = 16
N_BLK = 32


def draw_queries(key, part):
    key = jax.random.fold_in(key, 11)
    base_key = jax.random.fold_in(key, 0)
    group = QH // KVH
    base = jnp.clip(2.0 * jax.random.normal(base_key, (REQUESTS, KVH, group, HD), jnp.float32), -8.0, 8.0)
    return base.reshape(REQUESTS, QH * HD).astype(jnp.bfloat16)


def draw_prefix_keys(key, part):
    key = jax.random.fold_in(key, 12)
    keys_all = jnp.clip(jax.random.normal(key, (PRE_DEV * N_BLK, KVH, HD), jnp.float32), -5.0, 5.0)
    return keys_all.reshape(PRE_DEV * N_BLK, KVH * HD).astype(jnp.bfloat16)


def shuffled(key, rows, length):

    def single(sub):
        return jax.random.permutation(sub, length)
    return jax.vmap(single)(jax.random.split(key, rows))


def group_layout(key, group_id):
    nblk = N_BLK
    cells = REQ_DEV * MAXP
    parts = jax.random.split(key, 12)
    ranking = jax.random.permutation(parts[0], nblk)
    heavy_count = jax.random.randint(parts[1], (), 1, nblk // 4 + 1)
    heavy = ranking < heavy_count
    fullest = ranking == 0
    heavy_loads = jax.random.randint(parts[2], (nblk, nblk), 1, CAP + 1)
    light_loads = jax.random.randint(parts[3], (nblk, nblk), 0, 2)
    loads = jnp.where(heavy[:, None], heavy_loads, light_loads)
    loads = jnp.where(fullest[:, None], CAP, loads)
    loads = loads * (1 - jnp.eye(nblk, dtype=jnp.int32))
    incoming = jnp.sum(loads, axis=0)
    spare = jax.random.randint(parts[4], (nblk,), 0, 4)
    local_count = POOL_DEV - incoming - spare
    totals = local_count + jnp.sum(loads, axis=1)
    chosen_req = jax.random.randint(parts[5], (), 0, REQ_DEV)
    cell_req = jnp.arange(cells, dtype=jnp.int32) // MAXP
    priority = shuffled(parts[6], nblk, cells)
    forced = fullest[:, None] & (cell_req[None, :] == chosen_req)
    priority = jnp.where(forced, priority - cells, priority)
    order = jnp.argsort(jnp.argsort(priority, axis=1), axis=1)
    chosen = order < totals[:, None]
    counts = jnp.sum(chosen.reshape(nblk, REQ_DEV, MAXP).astype(jnp.int32), axis=2)
    live = jnp.arange(MAXP, dtype=jnp.int32)[None, None, :] < counts[:, :, None]
    live_flat = live.reshape(nblk, cells)
    mixing = shuffled(parts[7], nblk, cells)
    page_rank = jnp.argsort(jnp.argsort(jnp.where(live_flat, mixing, mixing + cells), axis=1), axis=1)
    remote_index = page_rank - local_count[:, None]
    inclusive = jnp.cumsum(loads, axis=1)
    holder_remote = jnp.sum((remote_index[:, :, None] >= inclusive[:, None, :]).astype(jnp.int32), axis=2)
    holder_remote = jnp.minimum(holder_remote, nblk - 1)
    before = inclusive - loads
    within = remote_index - jnp.take_along_axis(before, holder_remote, axis=1)
    prior_owners = jnp.cumsum(loads, axis=0) - loads
    owner_ids = jnp.broadcast_to(jnp.arange(nblk, dtype=jnp.int32)[:, None], (nblk, cells))
    remote_offset = local_count[holder_remote] + prior_owners[owner_ids, holder_remote] + within
    is_local = page_rank < local_count[:, None]
    holder = jnp.where(is_local, owner_ids, holder_remote)
    offset = jnp.clip(jnp.where(is_local, page_rank, remote_offset), 0, POOL_DEV - 1)
    slot_order = shuffled(parts[8], nblk, POOL_DEV)
    physical = holder * POOL_DEV + slot_order[holder, offset]
    mapping = jax.random.permutation(parts[9], nblk * POOL_DEV)
    inverse = jnp.argsort(mapping)
    logical = inverse[physical]
    filler = jax.random.randint(parts[10], (nblk, cells), 0, nblk * POOL_DEV)
    logical = jnp.where(live_flat, logical, filler)
    last_fill = jax.random.randint(parts[11], (nblk, REQ_DEV), 1, PAGE + 1)
    last_fill = jnp.where(fullest[:, None] & (jnp.arange(REQ_DEV, dtype=jnp.int32)[None, :] == chosen_req), PAGE, last_fill)
    lengths = jnp.where(counts > 0, (counts - 1) * PAGE + last_fill, 0)
    offset_base = group_id * nblk * POOL_DEV
    return ((logical + offset_base).reshape(nblk * REQ_DEV, MAXP), lengths.reshape(nblk * REQ_DEV), mapping + offset_base)


def layout(key):
    key = jax.random.fold_in(key, 101)

    def single(group_id):
        return group_layout(jax.random.fold_in(key, group_id), group_id)
    tables, lengths, places = jax.vmap(single)(jnp.arange(N_GRP, dtype=jnp.int32))
    return (tables.reshape(REQ_DEV * N_BLK * N_GRP, MAXP).astype(jnp.int32), lengths.reshape(REQ_DEV * N_BLK * N_GRP).astype(jnp.int32), places.reshape(POOL_DEV * N_BLK * N_GRP).astype(jnp.int32))


def draw_page_table(key, part):
    tables, lengths, places = layout(key)
    return tables


def draw_suffix_len(key, part):
    tables, lengths, places = layout(key)
    return lengths


def draw_place(key, part):
    tables, lengths, places = layout(key)
    return places


def levels(own_key, extent, cuts, low, largest):
    def one(axis_at, blocks):
        steps = jax.random.uniform(jax.random.fold_in(jax.random.fold_in(own_key, 6), axis_at), (blocks,), jnp.float32, low / len(cuts), largest / len(cuts))
        return jnp.repeat(jnp.exp(steps), extent[axis_at] // blocks).reshape((-1,) + (1,) * (len(extent) - axis_at - 1))

    loudness = one(*cuts[0])
    for cut in cuts[1:]:
        loudness = loudness * one(*cut)
    return loudness


def bell_draw(key, dims, width, limit, pieces=(), kind=jnp.bfloat16):
    entries = width * jax.random.normal(key, dims, jnp.float32)
    if pieces:
        entries = entries * levels(key, dims, pieces, -0.22, 0.18)
    return jnp.clip(entries, -limit, limit).astype(kind)


def setup_inputs(seed: int = 0) -> dict:
    splits = jax.random.split(jax.random.key(seed), 9)
    queries = draw_queries(jax.random.fold_in(splits[8], 71), 0)
    page_table = draw_page_table(jax.random.fold_in(splits[8], 71), 0)
    suffix_len = draw_suffix_len(jax.random.fold_in(splits[8], 71), 0)
    place = draw_place(jax.random.fold_in(splits[8], 71), 0)
    suffix_keys = bell_draw(splits[4], (PAGES, PAGE, KVH * HD), 1.5, 6.0, ((0, 512),))
    suffix_values = bell_draw(splits[5], (PAGES, PAGE, KVH * HD), 1.0, 5.0, ((0, 512),))
    prefix_keys = draw_prefix_keys(jax.random.fold_in(splits[8], 71), 0)
    prefix_values = bell_draw(splits[7], (PREFIX, KVH * HD), 1.0, 5.0, ((0, 32),))
    return dict(queries=queries, page_table=page_table, suffix_len=suffix_len, place=place, suffix_keys=suffix_keys, suffix_values=suffix_values, prefix_keys=prefix_keys, prefix_values=prefix_values)


def reference(queries, page_table, suffix_len, place, suffix_keys, suffix_values, prefix_keys, prefix_values):
    group = QH // KVH
    scale = HD ** -0.5
    blocks = REQUESTS // REQ_DEV
    prefix_k = prefix_keys.reshape(PREFIX, KVH, HD).astype(jnp.float32)
    prefix_v = prefix_values.reshape(PREFIX, KVH, HD).astype(jnp.float32)
    positions = jnp.arange(MAXP * PAGE, dtype=jnp.int32)
    highest = lax.Precision.HIGHEST

    def one_block(items):
        block_queries, block_table, block_len = items
        heads = block_queries.reshape(REQ_DEV, KVH, group, HD).astype(jnp.float32)
        rows = place[block_table]
        keys = suffix_keys[rows].reshape(REQ_DEV, MAXP * PAGE, KVH, HD).astype(jnp.float32)
        values = suffix_values[rows].reshape(REQ_DEV, MAXP * PAGE, KVH, HD).astype(jnp.float32)
        valid = positions[None, :] < block_len[:, None]
        pre_scores = jnp.einsum("rkgd,nkd->rkgn", heads, prefix_k, precision=highest) * scale
        suf_scores = jnp.einsum("rkgd,rnkd->rkgn", heads, keys, precision=highest) * scale
        suf_scores = jnp.where(valid[:, None, None, :], suf_scores, -jnp.inf)
        top = jnp.maximum(jnp.max(pre_scores, axis=-1), jnp.max(suf_scores, axis=-1))
        pre_weights = jnp.exp(pre_scores - top[..., None])
        suf_weights = jnp.exp(suf_scores - top[..., None])
        total = jnp.sum(pre_weights, axis=-1) + jnp.sum(suf_weights, axis=-1)
        pre_round = lax.optimization_barrier(pre_weights.astype(jnp.bfloat16)).astype(jnp.float32)
        suf_round = lax.optimization_barrier(suf_weights.astype(jnp.bfloat16)).astype(jnp.float32)
        mixture = jnp.einsum("rkgn,nkd->rkgd", pre_round, prefix_v, precision=highest)
        mixture = mixture + jnp.einsum("rkgn,rnkd->rkgd", suf_round, values, precision=highest)
        return (mixture / total[..., None]).astype(jnp.bfloat16).reshape(REQ_DEV, QH * HD)

    result = lax.map(one_block, (queries.reshape(blocks, REQ_DEV, QH * HD), page_table.reshape(blocks, REQ_DEV, MAXP), suffix_len.reshape(blocks, REQ_DEV)))
    return result.reshape(REQUESTS, QH * HD)
```

```python
import functools

import jax
import jax.numpy as jnp
from jax import lax
from jax.experimental import pallas as pl
from jax.experimental.pallas import tpu as pltpu
from jax.sharding import PartitionSpec as P

QH = 40
KVH = 8
HD = 128
PAGE = 16
MAXP = 4
CAP = 2
GROUP = QH // KVH
QCOLS = QH * HD
SIDE = 128
ROW = QCOLS + SIDE
SHARE = 4
HEADS = QH // SHARE
BLOCK = HEADS * HD
KV = KVH // SHARE * HD
SCALE = HD ** (-0.5)
VERY_LOW = -1e30
F32 = jnp.float32
BF16 = jnp.bfloat16
MIB = 1 << 20


def iota(shape, axis):
    return lax.broadcasted_iota(jnp.int32, shape, axis)


def dot(a, b):
    return lax.dot_general(a, b, (((1,), (0,)), ((), ())), preferred_element_type=F32)


def dot_t(a, b):
    return lax.dot_general(a, b, (((1,), (1,)), ((), ())), preferred_element_type=F32)


def three_parts(x):
    hi = x.astype(BF16).astype(F32)
    mid = (x - hi).astype(BF16).astype(F32)
    lo = (x - hi - mid).astype(BF16).astype(F32)
    return hi, mid, lo


def route_kernel(
    pool, q_ref, table_ref, len_ref, place_ref, pk_ref, pv_ref,
    send_ref, local_ref, where_ref, *share_refs,
):
    requests = q_ref.shape[0]
    entries = requests * MAXP
    cells = send_ref.shape[0]
    devices = cells // CAP
    mine = lax.axis_index("blk")
    group = lax.axis_index("grp")
    base = group * (devices * pool)
    table = table_ref[...] - base
    page = jnp.concatenate([table[:, j : j + 1] for j in range(MAXP)], axis=0)
    place = (place_ref[...] - base).astype(F32)
    lane = iota((entries, 128), 1)
    found = jnp.zeros((entries, 128), F32)
    for k in range(place.shape[0]):
        found = found + jnp.where(page == lane + 128 * k, place[k : k + 1, :], 0.0)
    physical = jnp.sum(found, axis=1, keepdims=True)
    holder = jnp.floor((physical + 0.5) * (1.0 / pool))
    slot = physical - holder * pool
    row = jnp.broadcast_to(len_ref[...], (requests, requests)).astype(F32)
    square = iota((requests, requests), 0) == iota((requests, requests), 1)
    length = jnp.sum(jnp.where(square, row, 0.0), axis=1, keepdims=True)
    tokens = jnp.concatenate(
        [jnp.clip(length - PAGE * j, 0.0, PAGE) for j in range(MAXP)], axis=0
    )
    used = tokens > 0.0
    at_home = holder == mine.astype(F32)
    remote = jnp.where(used & jnp.logical_not(at_home), 1.0, 0.0)
    lane_f = lane.astype(F32)
    member = jnp.where(holder == lane_f, remote, 0.0)
    below = jnp.where(iota((entries, entries), 1) < iota((entries, entries), 0), 1.0, 0.0)
    before = dot(below.astype(BF16), member.astype(BF16))
    rank = jnp.sum(before * member, axis=1, keepdims=True)
    where = jnp.where(remote > 0.0, holder * CAP + rank, cells + slot)
    where = jnp.where(used, where, -1.0)
    where_ref[...] = jnp.broadcast_to(where, where_ref.shape)
    pick = jnp.where(where == lane_f, 1.0, 0.0).T
    picked = functools.reduce(
        jnp.add, [pick[:, requests * j : requests * (j + 1)] for j in range(MAXP)]
    ).astype(BF16)
    facts = jnp.where(lane == 0, slot, jnp.where(lane == 1, tokens, 0.0))
    side = dot(pick.astype(BF16), facts.astype(BF16)).astype(BF16)
    send_ref[:, QCOLS:ROW] = side[:cells]
    local_ref[:, QCOLS:ROW] = side[cells : cells + pool]
    for k in range(KVH):
        cols = slice(k * GROUP * HD, (k + 1) * GROUP * HD)
        rows = dot(picked, q_ref[:, cols]).astype(BF16)
        send_ref[:, cols] = rows[:cells]
        local_ref[:, cols] = rows[cells : cells + pool]
    turn, part = lax.rem(group, SHARE), lax.div(group, SHARE)
    kv_at = pl.ds(pl.multiple_of(turn * KV, KV), KV)
    prefix = jnp.concatenate([pk_ref[:, kv_at], pv_ref[:, kv_at]], axis=1)
    depth = prefix.shape[0] // (lax.axis_size("grp") // SHARE) // CAP
    at = iota((cells, prefix.shape[0]), 1)
    want = part * (CAP * depth) + depth * lax.rem(iota((cells, prefix.shape[0]), 0), CAP)
    for p in range(depth):
        one = jnp.where(at == want + p, 1.0, 0.0).astype(BF16)
        send_ref[:, ROW + 2 * KV * p : ROW + 2 * KV * (p + 1)] = dot(one, prefix).astype(BF16)
    for o, share_ref in enumerate(share_refs):
        turned = turn ^ o
        share_ref[...] = q_ref[:, pl.ds(pl.multiple_of(turned * BLOCK, 128), BLOCK)]


def pages_kernel(got_ref, local_ref, k_ref, v_ref, answer_ref, own_ref):
    cells = got_ref.shape[0]
    pool = k_ref.shape[0]
    step = 16
    facts = got_ref[:, QCOLS:ROW].astype(F32)
    lane = iota((cells, 128), 1).astype(F32)
    pick = jnp.where((facts[:, 0:1] == lane) & (facts[:, 1:2] > 0.0), 1.0, 0.0)
    fetch = pick.T[:pool].astype(BF16)
    pick = pick[:, :pool].astype(BF16)
    tokens = (dot(fetch, got_ref[:, QCOLS:ROW]) + local_ref[:, QCOLS:ROW].astype(F32))[:, 1:2]
    wide = (step, step * PAGE)
    column = iota(wide, 1)
    sums = [jnp.zeros((step, SIDE), F32) for _ in range(pool // step)]
    side_lane = iota((step, SIDE), 1)
    masks = []
    for g in range(pool // step):
        ok = (lax.div(column, PAGE) == iota(wide, 0)) & (
            lax.rem(column, PAGE).astype(F32) < tokens[step * g : step * (g + 1)]
        )
        bias = jnp.where(ok, 0.0, VERY_LOW)
        masks.append(jnp.concatenate([bias] * GROUP, axis=0))
    for k in range(KVH):
        base = k * GROUP * HD
        cols = slice(base, base + GROUP * HD)
        rows = (dot(fetch, got_ref[:, cols]) + local_ref[:, cols].astype(F32)).astype(BF16)
        for g in range(pool // step):
            span = slice(step * g, step * (g + 1))
            heads = jnp.concatenate(
                [rows[span, i * HD : (i + 1) * HD] for i in range(GROUP)], axis=0
            )
            keys = k_ref[span, :, k * HD : (k + 1) * HD].reshape(step * PAGE, HD)
            values = v_ref[span, :, k * HD : (k + 1) * HD].reshape(step * PAGE, HD)
            scores = dot_t(heads, keys) * SCALE + masks[g]
            top = jnp.max(scores, axis=1, keepdims=True)
            weights = jnp.exp(scores - top)
            total = jnp.sum(weights, axis=1, keepdims=True)
            mixture = (dot(weights.astype(BF16), values) / total).astype(BF16)
            log_sum = top + jnp.log(total)
            for i in range(GROUP):
                own_ref[span, base + i * HD : base + (i + 1) * HD] = mixture[step * i : step * (i + 1)]
                here = lax.rem(side_lane, QH) == k * GROUP + i
                sums[g] = jnp.where(here, log_sum[step * i : step * (i + 1)], sums[g])
    for g in range(pool // step):
        hi, mid, lo = three_parts(sums[g])
        side = jnp.where(side_lane < QH, hi, jnp.where(side_lane < 2 * QH, mid, lo))
        own_ref[step * g : step * (g + 1), QCOLS:ROW] = side.astype(BF16)
    for k in range(KVH):
        cols = slice(k * GROUP * HD, (k + 1) * GROUP * HD)
        answer_ref[:, cols] = dot(pick, own_ref[:, cols]).astype(BF16)
    answer_ref[:, QCOLS:ROW] = dot(pick, own_ref[:, QCOLS:ROW]).astype(BF16)


def prefix_kernel(q0, q1, q2, q3, kv_ref, o0, o1, o2, o3):
    requests = q0.shape[0]
    rows = requests * SHARE
    chunks = kv_ref.shape[1] // (2 * KV)
    lane = iota((rows, SIDE), 1)
    sums = jnp.zeros((rows, SIDE), F32)
    outs = (o0, o1, o2, o3)
    for h in range(HEADS):
        head = h // GROUP
        cols = slice(h * HD, (h + 1) * HD)
        heads = jnp.concatenate([q[:, cols] for q in (q0, q1, q2, q3)], axis=0)
        scores = [
            dot_t(heads, kv_ref[:, 2 * KV * p + head * HD : 2 * KV * p + (head + 1) * HD]) * SCALE
            for p in range(chunks)
        ]
        top = functools.reduce(jnp.maximum, scores)
        top = jnp.max(top, axis=1, keepdims=True)
        weights = [jnp.exp(s - top) for s in scores]
        total = jnp.sum(functools.reduce(jnp.add, weights), axis=1, keepdims=True)
        mixture = functools.reduce(
            jnp.add,
            [
                dot(
                    w.astype(BF16),
                    kv_ref[:, 2 * KV * p + KV + head * HD : 2 * KV * p + KV + (head + 1) * HD],
                )
                for p, w in enumerate(weights)
            ],
        )
        mixture = (mixture / total).astype(BF16)
        sums = jnp.where(lax.rem(lane, HEADS) == h, top + jnp.log(total), sums)
        for o, out in enumerate(outs):
            out[:, cols] = mixture[requests * o : requests * (o + 1)]
    hi, mid, lo = three_parts(sums)
    side = jnp.where(lane < HEADS, hi, jnp.where(lane < 2 * HEADS, mid, lo)).astype(BF16)
    for o, out in enumerate(outs):
        out[:, BLOCK:] = side[requests * o : requests * (o + 1)]


def join_kernel(got_ref, own_ref, where_ref, p0, p1, p2, p3, out_ref):
    entries = where_ref.shape[0]
    requests = p0.shape[0]
    cells = got_ref.shape[0]
    pool = own_ref.shape[0]
    lane = iota((entries, 128), 1)
    where = where_ref[...]
    pick = jnp.where(where == lane.astype(F32), 1.0, 0.0).astype(BF16)
    far, near = pick[:, :cells], pick[:, cells : cells + pool]
    side = dot(far, got_ref[:, QCOLS:ROW]) + dot(near, own_ref[:, QCOLS:ROW])
    sums = side + pltpu.roll(side, SIDE - QH, 1) + pltpu.roll(side, SIDE - 2 * QH, 1)
    sums = jnp.where(where >= 0.0, sums, VERY_LOW)
    turn = lax.rem(lax.axis_index("grp"), SHARE)
    for o, p_ref in enumerate((p0, p1, p2, p3)):
        turned = turn ^ o
        at = pl.multiple_of(turned * BLOCK, 128)
        cols = pl.ds(at, BLOCK)
        rows = dot(far, got_ref[:, cols]) + dot(near, own_ref[:, cols])
        moved = pltpu.roll(sums, lax.rem(SIDE - turned * HEADS, SIDE), 1)
        pre = p_ref[:, BLOCK:].astype(F32)
        pre = pre + pltpu.roll(pre, SIDE - HEADS, 1) + pltpu.roll(pre, SIDE - 2 * HEADS, 1)
        logs = [moved[requests * j : requests * (j + 1)] for j in range(MAXP)]
        top = functools.reduce(jnp.maximum, logs, pre)
        parts = [jnp.exp(x - top) for x in logs]
        part = jnp.exp(pre - top)
        total = functools.reduce(jnp.add, parts, part)
        parts = [x / total for x in parts]
        part = part / total
        for h in range(HEADS):
            here = slice(h * HD, (h + 1) * HD)
            mixture = part[:, h : h + 1] * p_ref[:, here].astype(F32)
            for j in range(MAXP):
                mixture = mixture + parts[j][:, h : h + 1] * rows[requests * j : requests * (j + 1), here]
            out_ref[:, pl.ds(pl.multiple_of(at + h * HD, 128), HD)] = mixture.astype(BF16)


def call(kernel, out_shape, flops, *args):
    return pl.pallas_call(
        kernel,
        out_shape=[jax.ShapeDtypeStruct(s, d) for s, d in out_shape],
        compiler_params=pltpu.CompilerParams(vmem_limit_bytes=40 * MIB),
        cost_estimate=pl.CostEstimate(flops=flops, bytes_accessed=4 * MIB, transcendentals=0),
    )(*args)


def body(
    queries, page_table, suffix_len, place, suffix_keys, suffix_values, prefix_keys, prefix_values
):
    requests = queries.shape[0]
    pool = suffix_keys.shape[0]
    devices = lax.axis_size("blk")
    group = lax.axis_size("grp")
    cells = devices * CAP
    rest = 2 * prefix_keys.shape[0] * KV // (group // SHARE) // CAP
    send, local, where, *shares = call(
        functools.partial(route_kernel, pool),
        [((cells, ROW + rest), BF16), ((pool, ROW), BF16), ((requests * MAXP, 128), F32)]
        + [((requests, BLOCK), BF16)] * SHARE,
        10**8,
        queries,
        page_table,
        suffix_len.reshape(1, requests),
        place.reshape(-1, 128),
        prefix_keys,
        prefix_values,
    )
    swap = lambda x, o: lax.ppermute(x, "grp", [(i, i ^ o) for i in range(group)]) if o else x
    got = lax.all_to_all(send, "blk", split_axis=0, concat_axis=0, tiled=True)
    strips = [[SHARE * y + t for y in range(group // SHARE)] for t in range(SHARE)]
    kv = lax.all_gather(got[:, ROW:], "grp", axis=0, tiled=True, axis_index_groups=strips)
    asked = [swap(x, o) for o, x in enumerate(shares)]
    answer, own = call(
        pages_kernel,
        [((cells, ROW), BF16), ((pool, ROW), BF16)],
        10**9,
        got,
        local,
        suffix_keys,
        suffix_values,
    )
    back = lax.all_to_all(answer, "blk", split_axis=0, concat_axis=0, tiled=True)
    served = call(
        prefix_kernel, [((requests, BLOCK + SIDE), BF16)] * SHARE, 10**9, *asked, kv
    )
    served = [swap(x, o) for o, x in enumerate(served)]
    (out,) = call(
        join_kernel, [((requests, QCOLS), BF16)], 10**8, back, own, where, *served
    )
    return out


def solution(mesh):
    return jax.shard_map(
        body,
        mesh=mesh,
        in_specs=(
            P(("grp", "blk"), None),
            P(("grp", "blk"), None),
            P(("grp", "blk")),
            P("grp"),
            P(("grp", "blk"), None, None),
            P(("grp", "blk"), None, None),
            P("blk", None),
            P("blk", None),
        ),
        out_specs=P(("grp", "blk"), None),
        check_vma=False,
    )
```

```python
import functools

import jax
import jax.numpy as jnp
from jax import lax
from jax.experimental import pallas as pl
from jax.experimental.pallas import tpu as pltpu
from jax.sharding import PartitionSpec as P

QH = 40
KVH = 8
HD = 128
PAGE = 16
MAXP = 4
CAP = 2
GROUP = QH // KVH
QCOLS = QH * HD
SIDE = 128
ROW = QCOLS + SIDE
SHARE = 2
HEADS = QH // SHARE
BLOCK = HEADS * HD
KV = KVH // SHARE * HD
SCALE = HD ** (-0.5)
VERY_LOW = -1e30
F32 = jnp.float32
BF16 = jnp.bfloat16


def iota(shape, axis):
    return lax.broadcasted_iota(jnp.int32, shape, axis)


def dot(a, b):
    return lax.dot_general(a, b, (((1,), (0,)), ((), ())), preferred_element_type=F32)


def dot_t(a, b):
    return lax.dot_general(a, b, (((1,), (1,)), ((), ())), preferred_element_type=F32)


def three_parts(x):
    hi = x.astype(BF16).astype(F32)
    mid = (x - hi).astype(BF16).astype(F32)
    lo = (x - hi - mid).astype(BF16).astype(F32)
    return hi, mid, lo


def load(refs, scratch, sems):
    copies = [
        pltpu.make_async_copy(ref, buf, sems.at[i])
        for i, (ref, buf) in enumerate(zip(refs, scratch, strict=True))
    ]
    for copy in copies:
        copy.start()
    return copies


def my_turn():
    return lax.rem(lax.div(lax.axis_index("grp"), 2), SHARE)


def share_kernel(pk_hbm, pv_hbm, q_hbm, prefix_ref, mine_ref, away_ref, rows, q_ref, sems):
    group = lax.axis_index("grp")
    turn, part, core = my_turn(), lax.div(group, 2 * SHARE), lax.rem(group, 2)
    kv_at = pl.ds(pl.multiple_of(turn * KV, KV), KV)
    fetch_q = pltpu.make_async_copy(q_hbm, q_ref, sems.at[0])
    fetch_q.start()

    def fetch_rows(source):
        copy = pltpu.make_async_copy(source.at[:, kv_at], rows, sems.at[1])
        copy.start()
        copy.wait()

    @pl.when(core == 0)
    def _():
        fetch_rows(pk_hbm)

    @pl.when(core == 1)
    def _():
        fetch_rows(pv_hbm)

    shape = (prefix_ref.shape[0], rows.shape[0])
    each = rows.shape[0] // (lax.axis_size("grp") // (2 * SHARE))
    one = iota(shape, 1) == part * each + lax.rem(iota(shape, 0), each)
    prefix_ref[...] = dot(jnp.where(one, 1.0, 0.0).astype(BF16), rows[...]).astype(BF16)
    fetch_q.wait()
    for o, ref in enumerate((mine_ref, away_ref)):
        at = pl.multiple_of((turn ^ o) * BLOCK, BLOCK)
        ref[...] = q_ref[:, pl.ds(at, BLOCK)]


def route_kernel(
    pool, q_hbm, table_hbm, len_hbm, place_hbm, send_ref, local_ref, where_ref,
    q_ref, table_ref, len_ref, place_ref, sems,
):
    copies = load(
        (place_hbm, table_hbm, len_hbm, q_hbm), (place_ref, table_ref, len_ref, q_ref), sems
    )
    requests = q_ref.shape[0]
    entries = requests * MAXP
    devices = send_ref.shape[0]
    cells = devices * CAP
    mine = lax.axis_index("blk")
    group = lax.axis_index("grp")
    base = group * (devices * pool)
    square = iota((requests, requests), 0) == iota((requests, requests), 1)

    def column(row):
        row = jnp.broadcast_to(row, (requests, requests)).astype(F32)
        return jnp.sum(jnp.where(square, row, 0.0), axis=1, keepdims=True)

    for copy in copies[:3]:
        copy.wait()
    table = table_ref[...] - base
    page = jnp.concatenate([column(table[j : j + 1]) for j in range(MAXP)], axis=0)
    place = (place_ref[...] - base).astype(F32)
    lane = iota((entries, 128), 1).astype(F32)
    found = jnp.zeros((entries, 128), F32)
    for k in range(place.shape[0]):
        found = found + jnp.where(page == lane + 128.0 * k, place[k : k + 1, :], 0.0)
    physical = jnp.sum(found, axis=1, keepdims=True)
    holder = jnp.floor((physical + 0.5) * (1.0 / pool))
    slot = physical - holder * pool
    length = column(len_ref[...])
    tokens = jnp.concatenate(
        [jnp.clip(length - PAGE * j, 0.0, PAGE) for j in range(MAXP)], axis=0
    )
    used = tokens > 0.0
    at_home = holder == mine.astype(F32)
    remote = jnp.where(used & jnp.logical_not(at_home), 1.0, 0.0)
    member = jnp.where(holder == lane, remote, 0.0)
    below = jnp.where(iota((entries, entries), 1) < iota((entries, entries), 0), 1.0, 0.0)
    before = dot(below.astype(BF16), member.astype(BF16))
    rank = jnp.sum(before * member, axis=1, keepdims=True)
    where = jnp.where(remote > 0.0, holder * CAP + rank, cells + slot)
    where = jnp.where(used, where, -1.0)
    where_ref[...] = jnp.broadcast_to(where, where_ref.shape)
    pick = jnp.where(where == lane, 1.0, 0.0).T
    picked = functools.reduce(
        jnp.add, [pick[:, requests * j : requests * (j + 1)] for j in range(MAXP)]
    ).astype(BF16)
    facts = jnp.where(lane == 0.0, slot, jnp.where(lane == 1.0, tokens, 0.0))
    side = dot(pick.astype(BF16), facts.astype(BF16)).astype(BF16)
    send_ref[:, :, QCOLS:ROW] = side[:cells].reshape(devices, CAP, SIDE)
    local_ref[:, QCOLS:ROW] = side[cells : cells + pool]
    copies[3].wait()
    for k in range(KVH):
        cols = slice(k * GROUP * HD, (k + 1) * GROUP * HD)
        rows = dot(picked, q_ref[:, cols]).astype(BF16)
        send_ref[:, :, cols] = rows[:cells].reshape(devices, CAP, GROUP * HD)
        local_ref[:, cols] = rows[cells : cells + pool]


def pages_kernel(
    got_hbm, local_hbm, k_hbm, v_hbm, answer_ref, own_ref, got_ref, local_ref, k_ref, v_ref, sems
):
    devices = got_ref.shape[0]
    first = load((got_hbm, local_hbm), (got_ref, local_ref), sems.at[pl.ds(KVH, 2)])
    cells = devices * CAP
    pool = k_ref.shape[0]
    step = 16
    pair = 2 * HD
    copies = []
    for c in range(KVH // 2):
        at = (slice(None), slice(None), pl.ds(c * pair, pair))
        for i, (hbm, ref) in enumerate(((k_hbm, k_ref), (v_hbm, v_ref))):
            copy = pltpu.make_async_copy(hbm.at[at], ref.at[at], sems.at[2 * c + i])
            copy.start()
            copies.append(copy)
    for copy in first:
        copy.wait()
    facts = got_ref[:, :, QCOLS:ROW].reshape(cells, SIDE)
    plain = facts
    facts = facts.astype(F32)
    lane = iota((cells, 128), 1).astype(F32)
    pick = jnp.where((facts[:, 0:1] == lane) & (facts[:, 1:2] > 0.0), 1.0, 0.0)
    fetch = pick.T[:pool].astype(BF16)
    pick = pick[:, :pool].astype(BF16)
    tokens = (dot(fetch, plain) + local_ref[:, QCOLS:ROW].astype(F32))[:, 1:2]
    wide = (step, step * PAGE)
    column = iota(wide, 1)
    sums = [jnp.zeros((step, SIDE), F32) for _ in range(pool // step)]
    side_lane = iota((step, SIDE), 1)
    masks = []
    for g in range(pool // step):
        ok = (lax.div(column, PAGE) == iota(wide, 0)) & (
            lax.rem(column, PAGE).astype(F32) < tokens[step * g : step * (g + 1)]
        )
        bias = jnp.where(ok, 0.0, VERY_LOW)
        masks.append(jnp.concatenate([bias] * GROUP, axis=0))
    for k in range(KVH):
        base = k * GROUP * HD
        cols = slice(base, base + GROUP * HD)
        asked = got_ref[:, :, cols].reshape(cells, GROUP * HD)
        rows = (dot(fetch, asked) + local_ref[:, cols].astype(F32)).astype(BF16)
        if k % 2 == 0:
            copies[k].wait()
            copies[k + 1].wait()
        for g in range(pool // step):
            span = slice(step * g, step * (g + 1))
            heads = jnp.concatenate(
                [rows[span, i * HD : (i + 1) * HD] for i in range(GROUP)], axis=0
            )
            keys = k_ref[span, :, k * HD : (k + 1) * HD].reshape(step * PAGE, HD)
            values = v_ref[span, :, k * HD : (k + 1) * HD].reshape(step * PAGE, HD)
            scores = dot_t(heads, keys) * SCALE + masks[g]
            top = jnp.max(scores, axis=1, keepdims=True)
            weights = jnp.exp(scores - top)
            total = jnp.sum(weights, axis=1, keepdims=True)
            mixture = (dot(weights.astype(BF16), values) / total).astype(BF16)
            log_sum = top + jnp.log(total)
            for i in range(GROUP):
                own_ref[span, base + i * HD : base + (i + 1) * HD] = mixture[step * i : step * (i + 1)]
                here = lax.rem(side_lane, QH) == k * GROUP + i
                sums[g] = jnp.where(here, log_sum[step * i : step * (i + 1)], sums[g])
    for g in range(pool // step):
        hi, mid, lo = three_parts(sums[g])
        side = jnp.where(side_lane < QH, hi, jnp.where(side_lane < 2 * QH, mid, lo))
        own_ref[step * g : step * (g + 1), QCOLS:ROW] = side.astype(BF16)
    for k in range(KVH):
        cols = slice(k * GROUP * HD, (k + 1) * GROUP * HD)
        rows = dot(pick, own_ref[:, cols]).astype(BF16)
        answer_ref[:, :, cols] = rows.reshape(devices, CAP, GROUP * HD)
    rows = dot(pick, own_ref[:, QCOLS:ROW]).astype(BF16)
    answer_ref[:, :, QCOLS:ROW] = rows.reshape(devices, CAP, SIDE)


def prefix_kernel(q0, q1, kv_mine, kv_other, o0, o1):
    requests = q0.shape[0]
    rows = requests * SHARE
    step = 256
    chunks = [slice(c, c + step) for c in range(0, kv_mine.shape[0], step)]
    core = lax.rem(lax.axis_index("grp"), 2)
    lane = iota((rows, SIDE), 1)
    outs = (o0, o1)

    def attend(k_ref, v_ref):
        sums = jnp.zeros((rows, SIDE), F32)
        for k in range(KVH // SHARE):
            kv = slice(k * HD, (k + 1) * HD)
            heads = jnp.concatenate(
                [
                    q[:, (k * GROUP + i) * HD : (k * GROUP + i + 1) * HD]
                    for i in range(GROUP)
                    for q in (q0, q1)
                ],
                axis=0,
            )
            scores = [dot_t(heads, k_ref[c, kv]) * SCALE for c in chunks]
            top = jnp.max(functools.reduce(jnp.maximum, scores), axis=1, keepdims=True)
            weights = [jnp.exp(s - top) for s in scores]
            total = jnp.sum(functools.reduce(jnp.add, weights), axis=1, keepdims=True)
            mixture = functools.reduce(
                jnp.add, [dot(w.astype(BF16), v_ref[c, kv]) for c, w in zip(chunks, weights)]
            )
            mixture = (mixture / total).astype(BF16)
            log_sum = top + jnp.log(total)
            for i in range(GROUP):
                h = k * GROUP + i
                here = lax.rem(lane, HEADS) == h
                sums = jnp.where(here, log_sum[rows * i : rows * (i + 1)], sums)
                for o, out in enumerate(outs):
                    at = rows * i + requests * o
                    out[:, h * HD : (h + 1) * HD] = mixture[at : at + requests]
        hi, mid, lo = three_parts(sums)
        side = jnp.where(lane < HEADS, hi, jnp.where(lane < 2 * HEADS, mid, lo)).astype(BF16)
        for o, out in enumerate(outs):
            out[:, BLOCK:] = side[requests * o : requests * (o + 1)]

    @pl.when(core == 0)
    def _():
        attend(kv_mine, kv_other)

    @pl.when(core == 1)
    def _():
        attend(kv_other, kv_mine)


def join_kernel(
    got_hbm, own_hbm, where_hbm, p0_hbm, p1_hbm, out_ref, got_ref, own_ref, where_ref, p0, p1, sems
):
    hbm, vmem = (got_hbm, own_hbm, where_hbm, p0_hbm, p1_hbm), (got_ref, own_ref, where_ref, p0, p1)
    for copy in load(hbm, vmem, sems):
        copy.wait()
    entries = where_ref.shape[0]
    requests = p0.shape[0]
    cells = got_ref.shape[0] * CAP
    pool = own_ref.shape[0]
    lane = iota((entries, 128), 1)
    where = where_ref[...]
    pick = jnp.where(where == lane.astype(F32), 1.0, 0.0).astype(BF16)
    far, near = pick[:, :cells], pick[:, cells : cells + pool]
    side = dot(far, got_ref[:, :, QCOLS:ROW].reshape(cells, SIDE)) + dot(near, own_ref[:, QCOLS:ROW])
    sums = side + pltpu.roll(side, SIDE - QH, 1) + pltpu.roll(side, SIDE - 2 * QH, 1)
    sums = jnp.where(where >= 0.0, sums, VERY_LOW)
    turn = my_turn()
    for o, p_ref in enumerate((p0, p1)):
        turned = turn ^ o
        at = pl.multiple_of(turned * BLOCK, 128)
        cols = pl.ds(at, BLOCK)
        got = got_ref[:, :, cols].reshape(cells, BLOCK)
        rows = dot(far, got) + dot(near, own_ref[:, cols])
        moved = pltpu.roll(sums, lax.rem(SIDE - turned * HEADS, SIDE), 1)
        pre = p_ref[:, BLOCK:].astype(F32)
        pre = pre + pltpu.roll(pre, SIDE - HEADS, 1) + pltpu.roll(pre, SIDE - 2 * HEADS, 1)
        logs = [moved[requests * j : requests * (j + 1)] for j in range(MAXP)]
        top = functools.reduce(jnp.maximum, logs, pre)
        parts = [jnp.exp(x - top) for x in logs]
        part = jnp.exp(pre - top)
        total = functools.reduce(jnp.add, parts, part)
        parts = [x / total for x in parts]
        part = part / total
        for h in range(HEADS):
            here = slice(h * HD, (h + 1) * HD)
            mixture = part[:, h : h + 1] * p_ref[:, here].astype(F32)
            for j in range(MAXP):
                mixture = mixture + parts[j][:, h : h + 1] * rows[requests * j : requests * (j + 1), here]
            out_ref[:, pl.ds(pl.multiple_of(at + h * HD, 128), HD)] = mixture.astype(BF16)


def call(kernel, out_shape, flops, *args, in_hbm=(), scratch=(), room=62_150_000):
    specs = [
        pl.BlockSpec(memory_space=pl.ANY if i in in_hbm else pltpu.VMEM) for i in range(len(args))
    ]
    return pl.pallas_call(
        kernel,
        out_shape=[jax.ShapeDtypeStruct(s, d) for s, d in out_shape],
        in_specs=specs,
        scratch_shapes=list(scratch),
        compiler_params=pltpu.CompilerParams(vmem_limit_bytes=room),
        cost_estimate=pl.CostEstimate(flops=flops, bytes_accessed=1 << 22, transcendentals=0),
    )(*args)


def like(x):
    return pltpu.VMEM(x.shape, x.dtype)


def body(
    queries, page_table, suffix_len, place, suffix_keys, suffix_values, prefix_keys, prefix_values
):
    requests = queries.shape[0]
    pool = suffix_keys.shape[0]
    devices = lax.axis_size("blk")
    group = lax.axis_size("grp")
    depth = prefix_keys.shape[0]
    each = depth // (group // (2 * SHARE))
    share, mine, away = call(
        share_kernel,
        [((devices * each, KV), BF16), ((requests, BLOCK), BF16), ((requests, BLOCK), BF16)],
        10**7,
        prefix_keys,
        prefix_values,
        queries,
        in_hbm=range(3),
        scratch=(pltpu.VMEM((depth, KV), BF16), like(queries), pltpu.SemaphoreType.DMA((2,))),
    )
    swap = lambda x: lax.ppermute(x, "grp", [(i, i ^ 2) for i in range(group)])
    exchange = lambda x: lax.all_to_all(x, "blk", split_axis=0, concat_axis=0, tiled=True)
    part = exchange(share.reshape(devices, each, KV)).reshape(devices * each, KV)
    tables, lengths, places = (
        page_table.T, suffix_len.reshape(1, requests), place.reshape(-1, 128)
    )
    send, local, where = call(
        functools.partial(route_kernel, pool),
        [((devices, CAP, ROW), BF16), ((pool, ROW), BF16), ((requests * MAXP, 128), F32)],
        10**8,
        queries,
        tables,
        lengths,
        places,
        in_hbm=range(4),
        scratch=(*map(like, (queries, tables, lengths, places)), pltpu.SemaphoreType.DMA((4,))),
    )
    send, part = lax.optimization_barrier((send, part))
    got = exchange(send)
    around = [
        lax.ppermute(part, "grp", [(i, (i + 2 * SHARE * y) % group) for i in range(group)])
        for y in range(1, group // (2 * SHARE))
    ]
    kv_mine = jnp.concatenate([part, *around], axis=0)
    kv_other = lax.ppermute(kv_mine, "grp", [(i, i ^ 1) for i in range(group)])
    asked = swap(away)
    local, kv_mine, kv_other, asked = lax.optimization_barrier((local, kv_mine, kv_other, asked))
    served, away = call(
        prefix_kernel,
        [((requests, BLOCK + SIDE), BF16)] * SHARE,
        10**9,
        mine,
        asked,
        kv_mine,
        kv_other,
        room=40 << 20,
    )
    away = swap(away)
    answer, own = call(
        pages_kernel,
        [((devices, CAP, ROW), BF16), ((pool, ROW), BF16)],
        10**9,
        got,
        local,
        suffix_keys,
        suffix_values,
        in_hbm=range(4),
        scratch=(
            *map(like, (got, local, suffix_keys, suffix_values)),
            pltpu.SemaphoreType.DMA((KVH + 2,)),
        ),
    )
    back = exchange(answer)
    last = (back, own, where, served, away)
    (out,) = call(
        join_kernel,
        [((requests, QCOLS), BF16)],
        10**8,
        *last,
        in_hbm=range(5),
        scratch=(*map(like, last), pltpu.SemaphoreType.DMA((5,))),
        room=32 << 20,
    )
    return out


def solution(mesh):
    return jax.shard_map(
        body,
        mesh=mesh,
        in_specs=(
            P(("grp", "blk"), None),
            P(("grp", "blk"), None),
            P(("grp", "blk")),
            P("grp"),
            P(("grp", "blk"), None, None),
            P(("grp", "blk"), None, None),
            P("blk", None),
            P("blk", None),
        ),
        out_specs=P(("grp", "blk"), None),
        check_vma=False,
    )
```

```python
import functools

import jax
import jax.numpy as jnp
from jax import lax
from jax.experimental import pallas as pl
from jax.experimental.pallas import tpu as pltpu
from jax.sharding import PartitionSpec as P

QH = 40
KVH = 8
HD = 128
PAGE = 16
MAXP = 4
CAP = 2
GROUP = QH // KVH
QCOLS = QH * HD
SIDE = 128
ROW = QCOLS + SIDE
SHARE = 4
HEADS = QH // SHARE
BLOCK = HEADS * HD
KV = KVH // SHARE * HD
SCALE = HD ** (-0.5)
VERY_LOW = -1e30
F32 = jnp.float32
BF16 = jnp.bfloat16


def iota(shape, axis):
    return lax.broadcasted_iota(jnp.int32, shape, axis)


def dot(a, b):
    return lax.dot_general(a, b, (((1,), (0,)), ((), ())), preferred_element_type=F32)


def dot_t(a, b):
    return lax.dot_general(a, b, (((1,), (1,)), ((), ())), preferred_element_type=F32)


def three_parts(x):
    hi = x.astype(BF16).astype(F32)
    mid = (x - hi).astype(BF16).astype(F32)
    lo = (x - hi - mid).astype(BF16).astype(F32)
    return hi, mid, lo


def load(refs, scratch, sems):
    copies = [
        pltpu.make_async_copy(ref, buf, sems.at[i])
        for i, (ref, buf) in enumerate(zip(refs, scratch, strict=True))
    ]
    for copy in copies:
        copy.start()
    return copies


def my_turn():
    group = lax.axis_index("grp")
    return lax.rem(lax.div(group, 2), 2) + 2 * lax.div(group, 8)


def route_kernel(
    pool, q_hbm, table_hbm, len_hbm, place_hbm, pk_hbm, pv_hbm,
    send_ref, local_ref, where_ref, s0, s1, s2, s3,
    q_ref, table_ref, len_ref, place_ref, rows_ref, sems,
):
    requests = q_ref.shape[0]
    entries = requests * MAXP
    devices = send_ref.shape[0]
    cells = devices * CAP
    mine = lax.axis_index("blk")
    group = lax.axis_index("grp")
    turn = my_turn()
    copies = load(
        (place_hbm, table_hbm, len_hbm, q_hbm), (place_ref, table_ref, len_ref, q_ref), sems
    )
    kv_at = pl.ds(pl.multiple_of(turn * KV, KV), KV)

    def fetch_rows(source):
        return pltpu.make_async_copy(source.at[:, kv_at], rows_ref, sems.at[4])

    @pl.when(lax.rem(group, 2) == 0)
    def _():
        fetch_rows(pk_hbm).start()

    @pl.when(lax.rem(group, 2) == 1)
    def _():
        fetch_rows(pv_hbm).start()

    base = group * (devices * pool)
    square = iota((requests, requests), 0) == iota((requests, requests), 1)

    def column(row):
        row = jnp.broadcast_to(row, (requests, requests)).astype(F32)
        return jnp.sum(jnp.where(square, row, 0.0), axis=1, keepdims=True)

    for copy in copies[:3]:
        copy.wait()
    table = table_ref[...] - base
    page = jnp.concatenate([column(table[j : j + 1]) for j in range(MAXP)], axis=0)
    place = (place_ref[...] - base).astype(F32)
    lane = iota((entries, 128), 1).astype(F32)
    found = jnp.zeros((entries, 128), F32)
    for k in range(place.shape[0]):
        found = found + jnp.where(page == lane + 128.0 * k, place[k : k + 1, :], 0.0)
    physical = jnp.sum(found, axis=1, keepdims=True)
    holder = jnp.floor((physical + 0.5) * (1.0 / pool))
    slot = physical - holder * pool
    length = column(len_ref[...])
    tokens = jnp.concatenate(
        [jnp.clip(length - PAGE * j, 0.0, PAGE) for j in range(MAXP)], axis=0
    )
    used = tokens > 0.0
    at_home = holder == mine.astype(F32)
    remote = jnp.where(used & jnp.logical_not(at_home), 1.0, 0.0)
    member = jnp.where(holder == lane, remote, 0.0)
    below = jnp.where(iota((entries, entries), 1) < iota((entries, entries), 0), 1.0, 0.0)
    before = dot(below.astype(BF16), member.astype(BF16))
    rank = jnp.sum(before * member, axis=1, keepdims=True)
    where = jnp.where(remote > 0.0, holder * CAP + rank, cells + slot)
    where = jnp.where(used, where, -1.0)
    where_ref[...] = jnp.broadcast_to(where, where_ref.shape)
    pick = jnp.where(where == lane, 1.0, 0.0).T
    picked = functools.reduce(
        jnp.add, [pick[:, requests * j : requests * (j + 1)] for j in range(MAXP)]
    ).astype(BF16)
    facts = jnp.where(lane == 0.0, slot, jnp.where(lane == 1.0, tokens, 0.0))
    side = dot(pick.astype(BF16), facts.astype(BF16)).astype(BF16)
    send_ref[:, :, QCOLS:ROW] = side[:cells].reshape(devices, CAP, SIDE)
    local_ref[:, QCOLS:ROW] = side[cells : cells + pool]
    copies[3].wait()
    for k in range(KVH):
        cols = slice(k * GROUP * HD, (k + 1) * GROUP * HD)
        rows = dot(picked, q_ref[:, cols]).astype(BF16)
        send_ref[:, :, cols] = rows[:cells].reshape(devices, CAP, GROUP * HD)
        local_ref[:, cols] = rows[cells : cells + pool]
    for o, ref in enumerate((s0, s1, s2, s3)):
        at = pl.multiple_of((turn ^ o) * BLOCK, BLOCK)
        ref[...] = q_ref[:, pl.ds(at, BLOCK)]
    fetch_rows(pk_hbm).wait()
    shape = (cells, rows_ref.shape[0])
    deep = rows_ref.shape[0] // 2
    half = deep * lax.rem(lax.div(group, 4), 2)
    for p in range(deep // CAP):
        one = iota(shape, 1) == half + deep // CAP * lax.rem(iota(shape, 0), CAP) + p
        rows = dot(jnp.where(one, 1.0, 0.0).astype(BF16), rows_ref[...]).astype(BF16)
        send_ref[:, :, ROW + KV * p : ROW + KV * (p + 1)] = rows.reshape(devices, CAP, KV)


def pages_kernel(
    got_hbm, local_hbm, k_hbm, v_hbm, answer_ref, own_ref, got_ref, local_ref, k_ref, v_ref, sems
):
    devices = got_ref.shape[0]
    here = got_hbm.at[:, :, pl.ds(0, ROW)]
    first = load((here, local_hbm), (got_ref, local_ref), sems.at[pl.ds(KVH, 2)])
    cells = devices * CAP
    pool = k_ref.shape[0]
    step = 16
    pair = 2 * HD
    copies = []
    for c in range(KVH // 2):
        at = (slice(None), slice(None), pl.ds(c * pair, pair))
        for i, (hbm, ref) in enumerate(((k_hbm, k_ref), (v_hbm, v_ref))):
            copy = pltpu.make_async_copy(hbm.at[at], ref.at[at], sems.at[2 * c + i])
            copy.start()
            copies.append(copy)
    for copy in first:
        copy.wait()
    facts = got_ref[:, :, QCOLS:ROW].reshape(cells, SIDE)
    plain = facts
    facts = facts.astype(F32)
    lane = iota((cells, 128), 1).astype(F32)
    pick = jnp.where((facts[:, 0:1] == lane) & (facts[:, 1:2] > 0.0), 1.0, 0.0)
    fetch = pick.T[:pool].astype(BF16)
    pick = pick[:, :pool].astype(BF16)
    tokens = (dot(fetch, plain) + local_ref[:, QCOLS:ROW].astype(F32))[:, 1:2]
    wide = (step, step * PAGE)
    column = iota(wide, 1)
    sums = [jnp.zeros((step, SIDE), F32) for _ in range(pool // step)]
    side_lane = iota((step, SIDE), 1)
    masks = []
    for g in range(pool // step):
        ok = (lax.div(column, PAGE) == iota(wide, 0)) & (
            lax.rem(column, PAGE).astype(F32) < tokens[step * g : step * (g + 1)]
        )
        bias = jnp.where(ok, 0.0, VERY_LOW)
        masks.append(jnp.concatenate([bias] * GROUP, axis=0))
    for k in range(KVH):
        base = k * GROUP * HD
        cols = slice(base, base + GROUP * HD)
        asked = got_ref[:, :, cols].reshape(cells, GROUP * HD)
        rows = (dot(fetch, asked) + local_ref[:, cols].astype(F32)).astype(BF16)
        if k % 2 == 0:
            copies[k].wait()
            copies[k + 1].wait()
        for g in range(pool // step):
            span = slice(step * g, step * (g + 1))
            heads = jnp.concatenate(
                [rows[span, i * HD : (i + 1) * HD] for i in range(GROUP)], axis=0
            )
            keys = k_ref[span, :, k * HD : (k + 1) * HD].reshape(step * PAGE, HD)
            values = v_ref[span, :, k * HD : (k + 1) * HD].reshape(step * PAGE, HD)
            scores = dot_t(heads, keys) * SCALE + masks[g]
            top = jnp.max(scores, axis=1, keepdims=True)
            weights = jnp.exp(scores - top)
            total = jnp.sum(weights, axis=1, keepdims=True)
            mixture = (dot(weights.astype(BF16), values) / total).astype(BF16)
            log_sum = top + jnp.log(total)
            for i in range(GROUP):
                own_ref[span, base + i * HD : base + (i + 1) * HD] = mixture[step * i : step * (i + 1)]
                here = lax.rem(side_lane, QH) == k * GROUP + i
                sums[g] = jnp.where(here, log_sum[step * i : step * (i + 1)], sums[g])
    for g in range(pool // step):
        hi, mid, lo = three_parts(sums[g])
        side = jnp.where(side_lane < QH, hi, jnp.where(side_lane < 2 * QH, mid, lo))
        own_ref[step * g : step * (g + 1), QCOLS:ROW] = side.astype(BF16)
    for k in range(KVH):
        cols = slice(k * GROUP * HD, (k + 1) * GROUP * HD)
        rows = dot(pick, own_ref[:, cols]).astype(BF16)
        answer_ref[:, :, cols] = rows.reshape(devices, CAP, GROUP * HD)
    rows = dot(pick, own_ref[:, QCOLS:ROW]).astype(BF16)
    answer_ref[:, :, QCOLS:ROW] = rows.reshape(devices, CAP, SIDE)


def prefix_kernel(q0, q1, q2, q3, kv_mine, kv_other, o0, o1, o2, o3):
    requests = q0.shape[0]
    rows = requests * SHARE
    step = 256
    chunks = [slice(c, c + step) for c in range(0, kv_mine.shape[0], step)]
    core = lax.rem(lax.axis_index("grp"), 2)
    lane = iota((rows, SIDE), 1)
    outs = (o0, o1, o2, o3)

    def attend(k_ref, v_ref):
        sums = jnp.zeros((rows, SIDE), F32)
        for k in range(KVH // SHARE):
            kv = slice(k * HD, (k + 1) * HD)
            heads = jnp.concatenate(
                [
                    q[:, (k * GROUP + i) * HD : (k * GROUP + i + 1) * HD]
                    for i in range(GROUP)
                    for q in (q0, q1, q2, q3)
                ],
                axis=0,
            )
            scores = [dot_t(heads, k_ref[c, kv]) * SCALE for c in chunks]
            top = jnp.max(functools.reduce(jnp.maximum, scores), axis=1, keepdims=True)
            weights = [jnp.exp(s - top) for s in scores]
            total = jnp.sum(functools.reduce(jnp.add, weights), axis=1, keepdims=True)
            mixture = functools.reduce(
                jnp.add, [dot(w.astype(BF16), v_ref[c, kv]) for c, w in zip(chunks, weights)]
            )
            mixture = (mixture / total).astype(BF16)
            log_sum = top + jnp.log(total)
            for i in range(GROUP):
                h = k * GROUP + i
                here = lax.rem(lane, HEADS) == h
                sums = jnp.where(here, log_sum[rows * i : rows * (i + 1)], sums)
                for o, out in enumerate(outs):
                    at = rows * i + requests * o
                    out[:, h * HD : (h + 1) * HD] = mixture[at : at + requests]
        hi, mid, lo = three_parts(sums)
        side = jnp.where(lane < HEADS, hi, jnp.where(lane < 2 * HEADS, mid, lo)).astype(BF16)
        for o, out in enumerate(outs):
            out[:, BLOCK:] = side[requests * o : requests * (o + 1)]

    @pl.when(core == 0)
    def _():
        attend(kv_mine, kv_other)

    @pl.when(core == 1)
    def _():
        attend(kv_other, kv_mine)


def join_kernel(*refs):
    hbm, out_ref, vmem, sems = refs[:7], refs[7], refs[8:15], refs[15]
    for copy in load(hbm, vmem, sems):
        copy.wait()
    got_ref, own_ref, where_ref, *served = vmem
    entries = where_ref.shape[0]
    requests = served[0].shape[0]
    cells = got_ref.shape[0] * CAP
    pool = own_ref.shape[0]
    lane = iota((entries, 128), 1)
    where = where_ref[...]
    pick = jnp.where(where == lane.astype(F32), 1.0, 0.0).astype(BF16)
    far, near = pick[:, :cells], pick[:, cells : cells + pool]
    side = dot(far, got_ref[:, :, QCOLS:ROW].reshape(cells, SIDE)) + dot(near, own_ref[:, QCOLS:ROW])
    sums = side + pltpu.roll(side, SIDE - QH, 1) + pltpu.roll(side, SIDE - 2 * QH, 1)
    sums = jnp.where(where >= 0.0, sums, VERY_LOW)
    turn = my_turn()
    for o, p_ref in enumerate(served):
        turned = turn ^ o
        at = pl.multiple_of(turned * BLOCK, 128)
        cols = pl.ds(at, BLOCK)
        got = got_ref[:, :, cols].reshape(cells, BLOCK)
        rows = dot(far, got) + dot(near, own_ref[:, cols])
        moved = pltpu.roll(sums, lax.rem(SIDE - turned * HEADS, SIDE), 1)
        pre = p_ref[:, BLOCK:].astype(F32)
        pre = pre + pltpu.roll(pre, SIDE - HEADS, 1) + pltpu.roll(pre, SIDE - 2 * HEADS, 1)
        logs = [moved[requests * j : requests * (j + 1)] for j in range(MAXP)]
        top = functools.reduce(jnp.maximum, logs, pre)
        parts = [jnp.exp(x - top) for x in logs]
        part = jnp.exp(pre - top)
        total = functools.reduce(jnp.add, parts, part)
        parts = [x / total for x in parts]
        part = part / total
        for h in range(HEADS):
            here = slice(h * HD, (h + 1) * HD)
            mixture = part[:, h : h + 1] * p_ref[:, here].astype(F32)
            for j in range(MAXP):
                mixture = mixture + parts[j][:, h : h + 1] * rows[requests * j : requests * (j + 1), here]
            out_ref[:, pl.ds(pl.multiple_of(at + h * HD, 128), HD)] = mixture.astype(BF16)


def call(kernel, out_shape, flops, *args, in_hbm=(), scratch=(), room=62_150_000):
    specs = [
        pl.BlockSpec(memory_space=pl.ANY if i in in_hbm else pltpu.VMEM) for i in range(len(args))
    ]
    return pl.pallas_call(
        kernel,
        out_shape=[jax.ShapeDtypeStruct(s, d) for s, d in out_shape],
        in_specs=specs,
        scratch_shapes=list(scratch),
        compiler_params=pltpu.CompilerParams(vmem_limit_bytes=room),
        cost_estimate=pl.CostEstimate(flops=flops, bytes_accessed=1 << 22, transcendentals=0),
    )(*args)


def like(x):
    return pltpu.VMEM(x.shape, x.dtype)


def body(
    queries, page_table, suffix_len, place, suffix_keys, suffix_values, prefix_keys, prefix_values
):
    requests = queries.shape[0]
    pool = suffix_keys.shape[0]
    devices = lax.axis_size("blk")
    group = lax.axis_size("grp")
    depth = prefix_keys.shape[0]
    each = depth // 2
    tables, lengths, places = (
        page_table.T, suffix_len.reshape(1, requests), place.reshape(-1, 128)
    )
    wide = ROW + each // CAP * KV
    send, local, where, *asked = call(
        functools.partial(route_kernel, pool),
        [((devices, CAP, wide), BF16), ((pool, ROW), BF16), ((requests * MAXP, 128), F32)]
        + [((requests, BLOCK), BF16)] * SHARE,
        10**8,
        queries,
        tables,
        lengths,
        places,
        prefix_keys,
        prefix_values,
        in_hbm=range(6),
        scratch=(
            *map(like, (queries, tables, lengths, places)),
            pltpu.VMEM((depth, KV), BF16),
            pltpu.SemaphoreType.DMA((5,)),
        ),
    )
    flip = lambda x, bits: lax.ppermute(x, "grp", [(i, i ^ bits) for i in range(group)])
    turned = lambda xs: [flip(x, (0, 2, 8, 10)[o]) if o else x for o, x in enumerate(xs)]
    exchange = lambda x: lax.all_to_all(x, "blk", split_axis=0, concat_axis=0, tiled=True)
    got = exchange(send)
    asked = turned(asked)
    local, *asked = lax.optimization_barrier((local, *asked))
    answer, own = call(
        pages_kernel,
        [((devices, CAP, ROW), BF16), ((pool, ROW), BF16)],
        10**9,
        got,
        local,
        suffix_keys,
        suffix_values,
        in_hbm=range(4),
        scratch=(
            pltpu.VMEM((devices, CAP, ROW), BF16),
            *map(like, (local, suffix_keys, suffix_values)),
            pltpu.SemaphoreType.DMA((KVH + 2,)),
        ),
    )
    back = exchange(answer)
    part, own = lax.optimization_barrier((got[:, :, ROW:], own))
    part = part.reshape(devices * each, KV)
    kv_mine = jnp.concatenate([part, flip(part, 4)], axis=0)
    kv_other = flip(kv_mine, 1)
    served = call(
        prefix_kernel,
        [((requests, BLOCK + SIDE), BF16)] * SHARE,
        10**9,
        *asked,
        kv_mine,
        kv_other,
        room=40 << 20,
    )
    last = (back, own, where, *turned(served))
    (out,) = call(
        join_kernel,
        [((requests, QCOLS), BF16)],
        10**8,
        *last,
        in_hbm=range(len(last)),
        scratch=(*map(like, last), pltpu.SemaphoreType.DMA((len(last),))),
        room=32 << 20,
    )
    return out


def solution(mesh):
    return jax.shard_map(
        body,
        mesh=mesh,
        in_specs=(
            P(("grp", "blk"), None),
            P(("grp", "blk"), None),
            P(("grp", "blk")),
            P("grp"),
            P(("grp", "blk"), None, None),
            P(("grp", "blk"), None, None),
            P("blk", None),
            P("blk", None),
        ),
        out_specs=P(("grp", "blk"), None),
        check_vma=False,
    )
```

```python
import functools

import jax
import jax.numpy as jnp
from jax import lax
from jax.experimental import pallas as pl
from jax.experimental.pallas import tpu as pltpu
from jax.sharding import PartitionSpec as P

QH = 40
KVH = 8
HD = 128
PAGE = 16
MAXP = 4
CAP = 2
GROUP = QH // KVH
QCOLS = QH * HD
SIDE = 128
ROW = QCOLS + SIDE
SHARE = 4
HEADS = QH // SHARE
BLOCK = HEADS * HD
KV = KVH // SHARE * HD
SCALE = HD ** (-0.5)
VERY_LOW = -1e30
F32 = jnp.float32
BF16 = jnp.bfloat16


def iota(shape, axis):
    return lax.broadcasted_iota(jnp.int32, shape, axis)


def dot(a, b):
    return lax.dot_general(a, b, (((1,), (0,)), ((), ())), preferred_element_type=F32)


def dot_t(a, b):
    return lax.dot_general(a, b, (((1,), (1,)), ((), ())), preferred_element_type=F32)


def three_parts(x):
    hi = x.astype(BF16).astype(F32)
    mid = (x - hi).astype(BF16).astype(F32)
    lo = (x - hi - mid).astype(BF16).astype(F32)
    return hi, mid, lo


def load(refs, scratch, sems):
    copies = [
        pltpu.make_async_copy(ref, buf, sems.at[i])
        for i, (ref, buf) in enumerate(zip(refs, scratch, strict=True))
    ]
    for copy in copies:
        copy.start()
    return copies


def my_turn():
    group = lax.axis_index("grp")
    return lax.rem(lax.div(group, 2), 2) + 2 * lax.div(group, 8)


def route_kernel(
    pool, q_hbm, table_hbm, len_hbm, place_hbm, pk_hbm, pv_hbm,
    send_ref, local_ref, where_ref, s0, s1, s2, s3,
    q_ref, table_ref, len_ref, place_ref, rows_ref, sems,
):
    requests = q_ref.shape[0]
    entries = requests * MAXP
    devices = send_ref.shape[0]
    cells = devices * CAP
    mine = lax.axis_index("blk")
    group = lax.axis_index("grp")
    turn = my_turn()
    copies = load(
        (place_hbm, table_hbm, len_hbm, q_hbm), (place_ref, table_ref, len_ref, q_ref), sems
    )
    kv_at = pl.ds(pl.multiple_of(turn * KV, KV), KV)

    def fetch_rows(source):
        return pltpu.make_async_copy(source.at[:, kv_at], rows_ref, sems.at[4])

    @pl.when(lax.rem(group, 2) == 0)
    def _():
        fetch_rows(pk_hbm).start()

    @pl.when(lax.rem(group, 2) == 1)
    def _():
        fetch_rows(pv_hbm).start()

    base = group * (devices * pool)
    square = iota((requests, requests), 0) == iota((requests, requests), 1)

    def column(row):
        row = jnp.broadcast_to(row, (requests, requests)).astype(F32)
        return jnp.sum(jnp.where(square, row, 0.0), axis=1, keepdims=True)

    for copy in copies[:3]:
        copy.wait()
    table = table_ref[...] - base
    page = jnp.concatenate([column(table[j : j + 1]) for j in range(MAXP)], axis=0)
    place = (place_ref[...] - base).astype(F32)
    lane = iota((entries, 128), 1).astype(F32)
    found = jnp.zeros((entries, 128), F32)
    for k in range(place.shape[0]):
        found = found + jnp.where(page == lane + 128.0 * k, place[k : k + 1, :], 0.0)
    physical = jnp.sum(found, axis=1, keepdims=True)
    holder = jnp.floor((physical + 0.5) * (1.0 / pool))
    slot = physical - holder * pool
    length = column(len_ref[...])
    tokens = jnp.concatenate(
        [jnp.clip(length - PAGE * j, 0.0, PAGE) for j in range(MAXP)], axis=0
    )
    used = tokens > 0.0
    at_home = holder == mine.astype(F32)
    remote = jnp.where(used & jnp.logical_not(at_home), 1.0, 0.0)
    member = jnp.where(holder == lane, remote, 0.0)
    below = jnp.where(iota((entries, entries), 1) < iota((entries, entries), 0), 1.0, 0.0)
    before = dot(below.astype(BF16), member.astype(BF16))
    rank = jnp.sum(before * member, axis=1, keepdims=True)
    where = jnp.where(remote > 0.0, holder * CAP + rank, cells + slot)
    where = jnp.where(used, where, -1.0)
    where_ref[...] = jnp.broadcast_to(where, where_ref.shape)
    pick = jnp.where(where == lane, 1.0, 0.0).T
    picked = functools.reduce(
        jnp.add, [pick[:, requests * j : requests * (j + 1)] for j in range(MAXP)]
    ).astype(BF16)
    facts = jnp.where(lane == 0.0, slot, jnp.where(lane == 1.0, tokens, 0.0))
    side = dot(pick.astype(BF16), facts.astype(BF16)).astype(BF16)
    send_ref[:, :, QCOLS:ROW] = side[:cells].reshape(devices, CAP, SIDE)
    local_ref[:, QCOLS:ROW] = side[cells : cells + pool]
    copies[3].wait()
    for k in range(KVH):
        cols = slice(k * GROUP * HD, (k + 1) * GROUP * HD)
        rows = dot(picked, q_ref[:, cols]).astype(BF16)
        send_ref[:, :, cols] = rows[:cells].reshape(devices, CAP, GROUP * HD)
        local_ref[:, cols] = rows[cells : cells + pool]
    for o, ref in enumerate((s0, s1, s2, s3)):
        at = pl.multiple_of((turn ^ o) * BLOCK, BLOCK)
        ref[...] = q_ref[:, pl.ds(at, BLOCK)]
    fetch_rows(pk_hbm).wait()
    depth = rows_ref.shape[0]
    shape = (cells, depth)
    cell = iota(shape, 0)
    each = depth // 4 // CAP
    first = depth // 2 * lax.rem(lax.div(group, 4), 2) + depth // 4 * lax.div(cell, cells // 2)
    for p in range(each):
        one = iota(shape, 1) == first + each * lax.rem(cell, CAP) + p
        rows = dot(jnp.where(one, 1.0, 0.0).astype(BF16), rows_ref[...]).astype(BF16)
        send_ref[:, :, ROW + KV * p : ROW + KV * (p + 1)] = rows.reshape(devices, CAP, KV)


def pages_kernel(
    got_hbm, local_hbm, k_hbm, v_hbm, answer_ref, own_ref, got_ref, local_ref, k_ref, v_ref, sems
):
    devices = got_ref.shape[0]
    here = got_hbm.at[:, :, pl.ds(0, ROW)]
    first = load((here, local_hbm), (got_ref, local_ref), sems.at[pl.ds(KVH, 2)])
    cells = devices * CAP
    pool = k_ref.shape[0]
    step = 16
    pair = 2 * HD
    copies = []
    for c in range(KVH // 2):
        at = (slice(None), slice(None), pl.ds(c * pair, pair))
        for i, (hbm, ref) in enumerate(((k_hbm, k_ref), (v_hbm, v_ref))):
            copy = pltpu.make_async_copy(hbm.at[at], ref.at[at], sems.at[2 * c + i])
            copy.start()
            copies.append(copy)
    for copy in first:
        copy.wait()
    facts = got_ref[:, :, QCOLS:ROW].reshape(cells, SIDE)
    plain = facts
    facts = facts.astype(F32)
    lane = iota((cells, 128), 1).astype(F32)
    pick = jnp.where((facts[:, 0:1] == lane) & (facts[:, 1:2] > 0.0), 1.0, 0.0)
    fetch = pick.T[:pool].astype(BF16)
    pick = pick[:, :pool].astype(BF16)
    tokens = (dot(fetch, plain) + local_ref[:, QCOLS:ROW].astype(F32))[:, 1:2]
    wide = (step, step * PAGE)
    column = iota(wide, 1)
    sums = [jnp.zeros((step, SIDE), F32) for _ in range(pool // step)]
    side_lane = iota((step, SIDE), 1)
    masks = []
    for g in range(pool // step):
        ok = (lax.div(column, PAGE) == iota(wide, 0)) & (
            lax.rem(column, PAGE).astype(F32) < tokens[step * g : step * (g + 1)]
        )
        bias = jnp.where(ok, 0.0, VERY_LOW)
        masks.append(jnp.concatenate([bias] * GROUP, axis=0))
    for k in range(KVH):
        base = k * GROUP * HD
        cols = slice(base, base + GROUP * HD)
        asked = got_ref[:, :, cols].reshape(cells, GROUP * HD)
        rows = (dot(fetch, asked) + local_ref[:, cols].astype(F32)).astype(BF16)
        if k % 2 == 0:
            copies[k].wait()
            copies[k + 1].wait()
        for g in range(pool // step):
            span = slice(step * g, step * (g + 1))
            heads = jnp.concatenate(
                [rows[span, i * HD : (i + 1) * HD] for i in range(GROUP)], axis=0
            )
            keys = k_ref[span, :, k * HD : (k + 1) * HD].reshape(step * PAGE, HD)
            values = v_ref[span, :, k * HD : (k + 1) * HD].reshape(step * PAGE, HD)
            scores = dot_t(heads, keys) * SCALE + masks[g]
            top = jnp.max(scores, axis=1, keepdims=True)
            weights = jnp.exp(scores - top)
            total = jnp.sum(weights, axis=1, keepdims=True)
            mixture = (dot(weights.astype(BF16), values) / total).astype(BF16)
            log_sum = top + jnp.log(total)
            for i in range(GROUP):
                own_ref[span, base + i * HD : base + (i + 1) * HD] = mixture[step * i : step * (i + 1)]
                here = lax.rem(side_lane, QH) == k * GROUP + i
                sums[g] = jnp.where(here, log_sum[step * i : step * (i + 1)], sums[g])
    for g in range(pool // step):
        hi, mid, lo = three_parts(sums[g])
        side = jnp.where(side_lane < QH, hi, jnp.where(side_lane < 2 * QH, mid, lo))
        own_ref[step * g : step * (g + 1), QCOLS:ROW] = side.astype(BF16)
    for k in range(KVH):
        cols = slice(k * GROUP * HD, (k + 1) * GROUP * HD)
        rows = dot(pick, own_ref[:, cols]).astype(BF16)
        answer_ref[:, :, cols] = rows.reshape(devices, CAP, GROUP * HD)
    rows = dot(pick, own_ref[:, QCOLS:ROW]).astype(BF16)
    answer_ref[:, :, QCOLS:ROW] = rows.reshape(devices, CAP, SIDE)


def prefix_kernel(q0, q1, q2, q3, kv_mine, kv_other, o0, o1, o2, o3):
    requests = q0.shape[0]
    rows = requests * SHARE
    step = 256
    chunks = [slice(c, c + step) for c in range(0, kv_mine.shape[0], step)]
    core = lax.rem(lax.axis_index("grp"), 2)
    lane = iota((rows, SIDE), 1)
    outs = (o0, o1, o2, o3)

    def attend(k_ref, v_ref):
        sums = jnp.zeros((rows, SIDE), F32)
        for k in range(KVH // SHARE):
            kv = slice(k * HD, (k + 1) * HD)
            heads = jnp.concatenate(
                [
                    q[:, (k * GROUP + i) * HD : (k * GROUP + i + 1) * HD]
                    for i in range(GROUP)
                    for q in (q0, q1, q2, q3)
                ],
                axis=0,
            )
            scores = [dot_t(heads, k_ref[c, kv]) * SCALE for c in chunks]
            top = jnp.max(functools.reduce(jnp.maximum, scores), axis=1, keepdims=True)
            weights = [jnp.exp(s - top) for s in scores]
            total = jnp.sum(functools.reduce(jnp.add, weights), axis=1, keepdims=True)
            mixture = functools.reduce(
                jnp.add, [dot(w.astype(BF16), v_ref[c, kv]) for c, w in zip(chunks, weights)]
            )
            mixture = (mixture / total).astype(BF16)
            log_sum = top + jnp.log(total)
            for i in range(GROUP):
                h = k * GROUP + i
                here = lax.rem(lane, HEADS) == h
                sums = jnp.where(here, log_sum[rows * i : rows * (i + 1)], sums)
                for o, out in enumerate(outs):
                    at = rows * i + requests * o
                    out[:, h * HD : (h + 1) * HD] = mixture[at : at + requests]
        hi, mid, lo = three_parts(sums)
        side = jnp.where(lane < HEADS, hi, jnp.where(lane < 2 * HEADS, mid, lo)).astype(BF16)
        for o, out in enumerate(outs):
            out[:, BLOCK:] = side[requests * o : requests * (o + 1)]

    @pl.when(core == 0)
    def _():
        attend(kv_mine, kv_other)

    @pl.when(core == 1)
    def _():
        attend(kv_other, kv_mine)


def join_kernel(*refs):
    hbm, out_ref, vmem, sems = refs[:7], refs[7], refs[8:15], refs[15]
    for copy in load(hbm, vmem, sems):
        copy.wait()
    got_ref, own_ref, where_ref, *served = vmem
    entries = where_ref.shape[0]
    requests = served[0].shape[0]
    cells = got_ref.shape[0] * CAP
    pool = own_ref.shape[0]
    lane = iota((entries, 128), 1)
    where = where_ref[...]
    pick = jnp.where(where == lane.astype(F32), 1.0, 0.0).astype(BF16)
    far, near = pick[:, :cells], pick[:, cells : cells + pool]
    side = dot(far, got_ref[:, :, QCOLS:ROW].reshape(cells, SIDE)) + dot(near, own_ref[:, QCOLS:ROW])
    sums = side + pltpu.roll(side, SIDE - QH, 1) + pltpu.roll(side, SIDE - 2 * QH, 1)
    sums = jnp.where(where >= 0.0, sums, VERY_LOW)
    turn = my_turn()
    for o, p_ref in enumerate(served):
        turned = turn ^ o
        at = pl.multiple_of(turned * BLOCK, 128)
        cols = pl.ds(at, BLOCK)
        got = got_ref[:, :, cols].reshape(cells, BLOCK)
        rows = dot(far, got) + dot(near, own_ref[:, cols])
        moved = pltpu.roll(sums, lax.rem(SIDE - turned * HEADS, SIDE), 1)
        pre = p_ref[:, BLOCK:].astype(F32)
        pre = pre + pltpu.roll(pre, SIDE - HEADS, 1) + pltpu.roll(pre, SIDE - 2 * HEADS, 1)
        logs = [moved[requests * j : requests * (j + 1)] for j in range(MAXP)]
        top = functools.reduce(jnp.maximum, logs, pre)
        parts = [jnp.exp(x - top) for x in logs]
        part = jnp.exp(pre - top)
        total = functools.reduce(jnp.add, parts, part)
        parts = [x / total for x in parts]
        part = part / total
        for h in range(HEADS):
            here = slice(h * HD, (h + 1) * HD)
            mixture = part[:, h : h + 1] * p_ref[:, here].astype(F32)
            for j in range(MAXP):
                mixture = mixture + parts[j][:, h : h + 1] * rows[requests * j : requests * (j + 1), here]
            out_ref[:, pl.ds(pl.multiple_of(at + h * HD, 128), HD)] = mixture.astype(BF16)


def call(kernel, out_shape, flops, *args, in_hbm=(), scratch=(), room=62_150_000):
    specs = [
        pl.BlockSpec(memory_space=pl.ANY if i in in_hbm else pltpu.VMEM) for i in range(len(args))
    ]
    return pl.pallas_call(
        kernel,
        out_shape=[jax.ShapeDtypeStruct(s, d) for s, d in out_shape],
        in_specs=specs,
        scratch_shapes=list(scratch),
        compiler_params=pltpu.CompilerParams(vmem_limit_bytes=room),
        cost_estimate=pl.CostEstimate(flops=flops, bytes_accessed=1 << 22, transcendentals=0),
    )(*args)


def like(x):
    return pltpu.VMEM(x.shape, x.dtype)


def body(
    queries, page_table, suffix_len, place, suffix_keys, suffix_values, prefix_keys, prefix_values
):
    requests = queries.shape[0]
    pool = suffix_keys.shape[0]
    devices = lax.axis_size("blk")
    group = lax.axis_size("grp")
    depth = prefix_keys.shape[0]
    each = depth // 4
    tables, lengths, places = (
        page_table.T, suffix_len.reshape(1, requests), place.reshape(-1, 128)
    )
    wide = ROW + each // CAP * KV
    send, local, where, *asked = call(
        functools.partial(route_kernel, pool),
        [((devices, CAP, wide), BF16), ((pool, ROW), BF16), ((requests * MAXP, 128), F32)]
        + [((requests, BLOCK), BF16)] * SHARE,
        10**8,
        queries,
        tables,
        lengths,
        places,
        prefix_keys,
        prefix_values,
        in_hbm=range(6),
        scratch=(
            *map(like, (queries, tables, lengths, places)),
            pltpu.VMEM((depth, KV), BF16),
            pltpu.SemaphoreType.DMA((5,)),
        ),
    )
    flip = lambda x, bits: lax.ppermute(x, "grp", [(i, i ^ bits) for i in range(group)])
    turned = lambda xs: [flip(x, (0, 2, 8, 10)[o]) if o else x for o, x in enumerate(xs)]
    exchange = lambda x: lax.all_to_all(x, "blk", split_axis=0, concat_axis=0, tiled=True)
    got = exchange(send)
    asked = turned(asked)
    local, *asked = lax.optimization_barrier((local, *asked))
    answer, own = call(
        pages_kernel,
        [((devices, CAP, ROW), BF16), ((pool, ROW), BF16)],
        10**9,
        got,
        local,
        suffix_keys,
        suffix_values,
        in_hbm=range(4),
        scratch=(
            pltpu.VMEM((devices, CAP, ROW), BF16),
            *map(like, (local, suffix_keys, suffix_values)),
            pltpu.SemaphoreType.DMA((KVH + 2,)),
        ),
    )
    back = exchange(answer)
    part, own = lax.optimization_barrier((got[:, :, ROW:], own))
    part = part.reshape(devices * each, KV)
    pairs = [(i, i ^ (devices // 2)) for i in range(devices)]
    both = [
        (g * devices + i, (g ^ 4) * devices + j) for g in range(group) for i, j in pairs
    ]
    around = [
        flip(part, 4), lax.ppermute(part, "blk", pairs), lax.ppermute(part, ("grp", "blk"), both)
    ]
    kv_mine = jnp.concatenate([part, *around], axis=0)
    kv_other = flip(kv_mine, 1)
    served = call(
        prefix_kernel,
        [((requests, BLOCK + SIDE), BF16)] * SHARE,
        10**9,
        *asked,
        kv_mine,
        kv_other,
        room=40 << 20,
    )
    last = (back, own, where, *turned(served))
    (out,) = call(
        join_kernel,
        [((requests, QCOLS), BF16)],
        10**8,
        *last,
        in_hbm=range(len(last)),
        scratch=(*map(like, last), pltpu.SemaphoreType.DMA((len(last),))),
        room=32 << 20,
    )
    return out


def solution(mesh):
    return jax.shard_map(
        body,
        mesh=mesh,
        in_specs=(
            P(("grp", "blk"), None),
            P(("grp", "blk"), None),
            P(("grp", "blk")),
            P("grp"),
            P(("grp", "blk"), None, None),
            P(("grp", "blk"), None, None),
            P("blk", None),
            P("blk", None),
        ),
        out_specs=P(("grp", "blk"), None),
        check_vma=False,
    )
```

```python
import functools

import jax
import jax.numpy as jnp
from jax import lax
from jax.experimental import pallas as pl
from jax.experimental.pallas import tpu as pltpu
from jax.sharding import PartitionSpec as P

QH = 40
KVH = 8
HD = 128
PAGE = 16
MAXP = 4
CAP = 2
GROUP = QH // KVH
QCOLS = QH * HD
SIDE = 128
ROW = QCOLS + SIDE
SHARE = 4
HEADS = QH // SHARE
BLOCK = HEADS * HD
KV = KVH // SHARE * HD
SCALE = HD ** (-0.5)
VERY_LOW = -1e30
F32 = jnp.float32
BF16 = jnp.bfloat16


def iota(shape, axis):
    return lax.broadcasted_iota(jnp.int32, shape, axis)


def dot(a, b):
    return lax.dot_general(a, b, (((1,), (0,)), ((), ())), preferred_element_type=F32)


def dot_t(a, b):
    return lax.dot_general(a, b, (((1,), (1,)), ((), ())), preferred_element_type=F32)


def three_parts(x):
    hi = x.astype(BF16).astype(F32)
    mid = (x - hi).astype(BF16).astype(F32)
    lo = (x - hi - mid).astype(BF16).astype(F32)
    return hi, mid, lo


def load(refs, scratch, sems):
    copies = [
        pltpu.make_async_copy(ref, buf, sems.at[i])
        for i, (ref, buf) in enumerate(zip(refs, scratch, strict=True))
    ]
    for copy in copies:
        copy.start()
    return copies


def my_turn():
    return lax.div(lax.axis_index("grp"), 4)


def route_kernel(
    pool, q_hbm, table_hbm, len_hbm, place_hbm, pk_hbm, pv_hbm,
    send_ref, local_ref, where_ref, s0, s1, s2, s3,
    q_ref, table_ref, len_ref, place_ref, rows_ref, sems,
):
    requests = q_ref.shape[0]
    entries = requests * MAXP
    devices = send_ref.shape[0]
    cells = devices * CAP
    mine = lax.axis_index("blk")
    group = lax.axis_index("grp")
    turn = my_turn()
    copies = load(
        (place_hbm, table_hbm, len_hbm, q_hbm), (place_ref, table_ref, len_ref, q_ref), sems
    )
    kv_at = pl.ds(pl.multiple_of(turn * KV, KV), KV)

    def fetch_rows(source):
        return pltpu.make_async_copy(source.at[:, kv_at], rows_ref, sems.at[4])

    @pl.when(lax.rem(group, 2) == 0)
    def _():
        fetch_rows(pk_hbm).start()

    @pl.when(lax.rem(group, 2) == 1)
    def _():
        fetch_rows(pv_hbm).start()

    base = group * (devices * pool)
    square = iota((requests, requests), 0) == iota((requests, requests), 1)

    def column(row):
        row = jnp.broadcast_to(row, (requests, requests)).astype(F32)
        return jnp.sum(jnp.where(square, row, 0.0), axis=1, keepdims=True)

    for copy in copies[:3]:
        copy.wait()
    table = table_ref[...] - base
    page = jnp.concatenate([column(table[j : j + 1]) for j in range(MAXP)], axis=0)
    place = (place_ref[...] - base).astype(F32)
    lane = iota((entries, 128), 1).astype(F32)
    found = jnp.zeros((entries, 128), F32)
    for k in range(place.shape[0]):
        found = found + jnp.where(page == lane + 128.0 * k, place[k : k + 1, :], 0.0)
    physical = jnp.sum(found, axis=1, keepdims=True)
    holder = jnp.floor((physical + 0.5) * (1.0 / pool))
    slot = physical - holder * pool
    length = column(len_ref[...])
    tokens = jnp.concatenate(
        [jnp.clip(length - PAGE * j, 0.0, PAGE) for j in range(MAXP)], axis=0
    )
    used = tokens > 0.0
    at_home = holder == mine.astype(F32)
    remote = jnp.where(used & jnp.logical_not(at_home), 1.0, 0.0)
    member = jnp.where(holder == lane, remote, 0.0)
    below = jnp.where(iota((entries, entries), 1) < iota((entries, entries), 0), 1.0, 0.0)
    before = dot(below.astype(BF16), member.astype(BF16))
    rank = jnp.sum(before * member, axis=1, keepdims=True)
    where = jnp.where(remote > 0.0, holder * CAP + rank, cells + slot)
    where = jnp.where(used, where, -1.0)
    where_ref[...] = jnp.broadcast_to(where, where_ref.shape)
    pick = jnp.where(where == lane, 1.0, 0.0).T
    picked = functools.reduce(
        jnp.add, [pick[:, requests * j : requests * (j + 1)] for j in range(MAXP)]
    ).astype(BF16)
    facts = jnp.where(lane == 0.0, slot, jnp.where(lane == 1.0, tokens, 0.0))
    side = dot(pick.astype(BF16), facts.astype(BF16)).astype(BF16)
    send_ref[:, :, QCOLS:ROW] = side[:cells].reshape(devices, CAP, SIDE)
    local_ref[:, QCOLS:ROW] = side[cells : cells + pool]
    copies[3].wait()
    for k in range(KVH):
        cols = slice(k * GROUP * HD, (k + 1) * GROUP * HD)
        rows = dot(picked, q_ref[:, cols]).astype(BF16)
        send_ref[:, :, cols] = rows[:cells].reshape(devices, CAP, GROUP * HD)
        local_ref[:, cols] = rows[cells : cells + pool]
    for o, ref in enumerate((s0, s1, s2, s3)):
        at = pl.multiple_of((turn ^ o) * BLOCK, BLOCK)
        ref[...] = q_ref[:, pl.ds(at, BLOCK)]
    fetch_rows(pk_hbm).wait()
    depth = rows_ref.shape[0]
    shape = (cells, depth)
    cell = iota(shape, 0)
    each = depth // 4 // CAP
    first = depth // 2 * lax.rem(lax.div(group, 2), 2) + depth // 4 * lax.div(cell, cells // 2)
    for p in range(each):
        one = iota(shape, 1) == first + each * lax.rem(cell, CAP) + p
        rows = dot(jnp.where(one, 1.0, 0.0).astype(BF16), rows_ref[...]).astype(BF16)
        send_ref[:, :, ROW + KV * p : ROW + KV * (p + 1)] = rows.reshape(devices, CAP, KV)


def pages_kernel(
    got_hbm, local_hbm, k_hbm, v_hbm, answer_ref, own_ref, got_ref, local_ref, k_ref, v_ref, sems
):
    devices = got_ref.shape[0]
    here = got_hbm.at[:, :, pl.ds(0, ROW)]
    first = load((here, local_hbm), (got_ref, local_ref), sems.at[pl.ds(KVH, 2)])
    cells = devices * CAP
    pool = k_ref.shape[0]
    step = 16
    pair = 2 * HD
    copies = []
    for c in range(KVH // 2):
        at = (slice(None), slice(None), pl.ds(c * pair, pair))
        for i, (hbm, ref) in enumerate(((k_hbm, k_ref), (v_hbm, v_ref))):
            copy = pltpu.make_async_copy(hbm.at[at], ref.at[at], sems.at[2 * c + i])
            copy.start()
            copies.append(copy)
    for copy in first:
        copy.wait()
    facts = got_ref[:, :, QCOLS:ROW].reshape(cells, SIDE)
    plain = facts
    facts = facts.astype(F32)
    lane = iota((cells, 128), 1).astype(F32)
    pick = jnp.where((facts[:, 0:1] == lane) & (facts[:, 1:2] > 0.0), 1.0, 0.0)
    fetch = pick.T[:pool].astype(BF16)
    pick = pick[:, :pool].astype(BF16)
    tokens = (dot(fetch, plain) + local_ref[:, QCOLS:ROW].astype(F32))[:, 1:2]
    wide = (step, step * PAGE)
    column = iota(wide, 1)
    sums = [jnp.zeros((step, SIDE), F32) for _ in range(pool // step)]
    side_lane = iota((step, SIDE), 1)
    masks = []
    for g in range(pool // step):
        ok = (lax.div(column, PAGE) == iota(wide, 0)) & (
            lax.rem(column, PAGE).astype(F32) < tokens[step * g : step * (g + 1)]
        )
        bias = jnp.where(ok, 0.0, VERY_LOW)
        masks.append(jnp.concatenate([bias] * GROUP, axis=0))
    for k in range(KVH):
        base = k * GROUP * HD
        cols = slice(base, base + GROUP * HD)
        asked = got_ref[:, :, cols].reshape(cells, GROUP * HD)
        rows = (dot(fetch, asked) + local_ref[:, cols].astype(F32)).astype(BF16)
        if k % 2 == 0:
            copies[k].wait()
            copies[k + 1].wait()
        for g in range(pool // step):
            span = slice(step * g, step * (g + 1))
            heads = jnp.concatenate(
                [rows[span, i * HD : (i + 1) * HD] for i in range(GROUP)], axis=0
            )
            keys = k_ref[span, :, k * HD : (k + 1) * HD].reshape(step * PAGE, HD)
            values = v_ref[span, :, k * HD : (k + 1) * HD].reshape(step * PAGE, HD)
            scores = dot_t(heads, keys) * SCALE + masks[g]
            top = jnp.max(scores, axis=1, keepdims=True)
            weights = jnp.exp(scores - top)
            total = jnp.sum(weights, axis=1, keepdims=True)
            mixture = (dot(weights.astype(BF16), values) / total).astype(BF16)
            log_sum = top + jnp.log(total)
            for i in range(GROUP):
                own_ref[span, base + i * HD : base + (i + 1) * HD] = mixture[step * i : step * (i + 1)]
                here = lax.rem(side_lane, QH) == k * GROUP + i
                sums[g] = jnp.where(here, log_sum[step * i : step * (i + 1)], sums[g])
    for g in range(pool // step):
        hi, mid, lo = three_parts(sums[g])
        side = jnp.where(side_lane < QH, hi, jnp.where(side_lane < 2 * QH, mid, lo))
        own_ref[step * g : step * (g + 1), QCOLS:ROW] = side.astype(BF16)
    for k in range(KVH):
        cols = slice(k * GROUP * HD, (k + 1) * GROUP * HD)
        rows = dot(pick, own_ref[:, cols]).astype(BF16)
        answer_ref[:, :, cols] = rows.reshape(devices, CAP, GROUP * HD)
    rows = dot(pick, own_ref[:, QCOLS:ROW]).astype(BF16)
    answer_ref[:, :, QCOLS:ROW] = rows.reshape(devices, CAP, SIDE)


def prefix_kernel(q0, q1, q2, q3, kv_mine, kv_other, o0, o1, o2, o3):
    requests = q0.shape[0]
    rows = requests * SHARE
    step = 256
    chunks = [slice(c, c + step) for c in range(0, kv_mine.shape[0], step)]
    core = lax.rem(lax.axis_index("grp"), 2)
    lane = iota((rows, SIDE), 1)
    outs = (o0, o1, o2, o3)

    def attend(k_ref, v_ref):
        sums = jnp.zeros((rows, SIDE), F32)
        for k in range(KVH // SHARE):
            kv = slice(k * HD, (k + 1) * HD)
            heads = jnp.concatenate(
                [
                    q[:, (k * GROUP + i) * HD : (k * GROUP + i + 1) * HD]
                    for i in range(GROUP)
                    for q in (q0, q1, q2, q3)
                ],
                axis=0,
            )
            scores = [dot_t(heads, k_ref[c, kv]) * SCALE for c in chunks]
            top = jnp.max(functools.reduce(jnp.maximum, scores), axis=1, keepdims=True)
            weights = [jnp.exp(s - top) for s in scores]
            total = jnp.sum(functools.reduce(jnp.add, weights), axis=1, keepdims=True)
            mixture = functools.reduce(
                jnp.add, [dot(w.astype(BF16), v_ref[c, kv]) for c, w in zip(chunks, weights)]
            )
            mixture = (mixture / total).astype(BF16)
            log_sum = top + jnp.log(total)
            for i in range(GROUP):
                h = k * GROUP + i
                here = lax.rem(lane, HEADS) == h
                sums = jnp.where(here, log_sum[rows * i : rows * (i + 1)], sums)
                for o, out in enumerate(outs):
                    at = rows * i + requests * o
                    out[:, h * HD : (h + 1) * HD] = mixture[at : at + requests]
        hi, mid, lo = three_parts(sums)
        side = jnp.where(lane < HEADS, hi, jnp.where(lane < 2 * HEADS, mid, lo)).astype(BF16)
        for o, out in enumerate(outs):
            out[:, BLOCK:] = side[requests * o : requests * (o + 1)]

    @pl.when(core == 0)
    def _():
        attend(kv_mine, kv_other)

    @pl.when(core == 1)
    def _():
        attend(kv_other, kv_mine)


def join_kernel(got_ref, own_ref, where_ref, *refs):
    *served, out_ref = refs
    entries = where_ref.shape[0]
    requests = served[0].shape[0]
    cells = got_ref.shape[0] * CAP
    pool = own_ref.shape[0]
    lane = iota((entries, 128), 1)
    where = where_ref[...]
    pick = jnp.where(where == lane.astype(F32), 1.0, 0.0).astype(BF16)
    far, near = pick[:, :cells], pick[:, cells : cells + pool]
    side = dot(far, got_ref[:, :, QCOLS:ROW].reshape(cells, SIDE)) + dot(near, own_ref[:, QCOLS:ROW])
    sums = side + pltpu.roll(side, SIDE - QH, 1) + pltpu.roll(side, SIDE - 2 * QH, 1)
    sums = jnp.where(where >= 0.0, sums, VERY_LOW)
    turn = my_turn()
    for o, p_ref in enumerate(served):
        turned = turn ^ o
        at = pl.multiple_of(turned * BLOCK, 128)
        cols = pl.ds(at, BLOCK)
        got = got_ref[:, :, cols].reshape(cells, BLOCK)
        rows = dot(far, got) + dot(near, own_ref[:, cols])
        moved = pltpu.roll(sums, lax.rem(SIDE - turned * HEADS, SIDE), 1)
        pre = p_ref[:, BLOCK:].astype(F32)
        pre = pre + pltpu.roll(pre, SIDE - HEADS, 1) + pltpu.roll(pre, SIDE - 2 * HEADS, 1)
        logs = [moved[requests * j : requests * (j + 1)] for j in range(MAXP)]
        top = functools.reduce(jnp.maximum, logs, pre)
        parts = [jnp.exp(x - top) for x in logs]
        part = jnp.exp(pre - top)
        total = functools.reduce(jnp.add, parts, part)
        parts = [x / total for x in parts]
        part = part / total
        for h in range(HEADS):
            here = slice(h * HD, (h + 1) * HD)
            mixture = part[:, h : h + 1] * p_ref[:, here].astype(F32)
            for j in range(MAXP):
                mixture = mixture + parts[j][:, h : h + 1] * rows[requests * j : requests * (j + 1), here]
            out_ref[:, pl.ds(pl.multiple_of(at + h * HD, 128), HD)] = mixture.astype(BF16)


def call(kernel, out_shape, flops, *args, in_hbm=(), scratch=(), room=62_150_000):
    specs = [
        pl.BlockSpec(memory_space=pl.ANY if i in in_hbm else pltpu.VMEM) for i in range(len(args))
    ]
    return pl.pallas_call(
        kernel,
        out_shape=[jax.ShapeDtypeStruct(s, d) for s, d in out_shape],
        in_specs=specs,
        scratch_shapes=list(scratch),
        compiler_params=pltpu.CompilerParams(vmem_limit_bytes=room),
        cost_estimate=pl.CostEstimate(flops=flops, bytes_accessed=1 << 22, transcendentals=0),
    )(*args)


def like(x):
    return pltpu.VMEM(x.shape, x.dtype)


def body(
    queries, page_table, suffix_len, place, suffix_keys, suffix_values, prefix_keys, prefix_values
):
    requests = queries.shape[0]
    pool = suffix_keys.shape[0]
    devices = lax.axis_size("blk")
    group = lax.axis_size("grp")
    depth = prefix_keys.shape[0]
    each = depth // 4
    tables, lengths, places = (
        page_table.T, suffix_len.reshape(1, requests), place.reshape(-1, 128)
    )
    wide = ROW + each // CAP * KV
    send, local, where, *asked = call(
        functools.partial(route_kernel, pool),
        [((devices, CAP, wide), BF16), ((pool, ROW), BF16), ((requests * MAXP, 128), F32)]
        + [((requests, BLOCK), BF16)] * SHARE,
        10**8,
        queries,
        tables,
        lengths,
        places,
        prefix_keys,
        prefix_values,
        in_hbm=range(6),
        scratch=(
            *map(like, (queries, tables, lengths, places)),
            pltpu.VMEM((depth, KV), BF16),
            pltpu.SemaphoreType.DMA((5,)),
        ),
    )
    flip = lambda x, bits: lax.ppermute(x, "grp", [(i, i ^ bits) for i in range(group)])
    turned = lambda xs: [flip(x, 4 * o) if o else x for o, x in enumerate(xs)]
    exchange = lambda x: lax.all_to_all(x, "blk", split_axis=0, concat_axis=0, tiled=True)
    got = exchange(send)
    asked = turned(asked)
    local, *asked = lax.optimization_barrier((local, *asked))
    answer, own = call(
        pages_kernel,
        [((devices, CAP, ROW), BF16), ((pool, ROW), BF16)],
        10**9,
        got,
        local,
        suffix_keys,
        suffix_values,
        in_hbm=range(4),
        scratch=(
            pltpu.VMEM((devices, CAP, ROW), BF16),
            *map(like, (local, suffix_keys, suffix_values)),
            pltpu.SemaphoreType.DMA((KVH + 2,)),
        ),
    )
    back = exchange(answer)
    part, own = lax.optimization_barrier((got[:, :, ROW:], own))
    part = part.reshape(devices * each, KV)
    pairs = [(i, i ^ (devices // 2)) for i in range(devices)]
    both = [
        (g * devices + i, (g ^ 2) * devices + j) for g in range(group) for i, j in pairs
    ]
    around = [
        flip(part, 2), lax.ppermute(part, "blk", pairs), lax.ppermute(part, ("grp", "blk"), both)
    ]
    kv_mine = jnp.concatenate([part, *around], axis=0)
    kv_other = flip(kv_mine, 1)
    served = call(
        prefix_kernel,
        [((requests, BLOCK + SIDE), BF16)] * SHARE,
        10**9,
        *asked,
        kv_mine,
        kv_other,
        room=40 << 20,
    )
    last = (back, own, where, *turned(served))
    (out,) = call(
        join_kernel,
        [((requests, QCOLS), BF16)],
        10**8,
        *last,
        room=32 << 20,
    )
    return out


def solution(mesh):
    return jax.shard_map(
        body,
        mesh=mesh,
        in_specs=(
            P(("grp", "blk"), None),
            P(("grp", "blk"), None),
            P(("grp", "blk")),
            P("grp"),
            P(("grp", "blk"), None, None),
            P(("grp", "blk"), None, None),
            P("blk", None),
            P("blk", None),
        ),
        out_specs=P(("grp", "blk"), None),
        check_vma=False,
    )
```

```python
import functools

import jax
import jax.numpy as jnp
from jax import lax
from jax.experimental import pallas as pl
from jax.experimental.pallas import tpu as pltpu
from jax.sharding import PartitionSpec as P

QH = 40
KVH = 8
HD = 128
PAGE = 16
MAXP = 4
CAP = 2
GROUP = QH // KVH
QCOLS = QH * HD
SIDE = 128
ROW = QCOLS + SIDE
SHARE = 4
HEADS = QH // SHARE
BLOCK = HEADS * HD
KV = KVH // SHARE * HD
CHUNKS = 4
CHUNK = QCOLS // CHUNKS
TOKENS_AT = 64
SCALE = HD ** (-0.5)
VERY_LOW = -1e30
F32 = jnp.float32
BF16 = jnp.bfloat16


def iota(shape, axis):
    return lax.broadcasted_iota(jnp.int32, shape, axis)


def dot(a, b):
    return lax.dot_general(a, b, (((1,), (0,)), ((), ())), preferred_element_type=F32)


def dot_t(a, b):
    return lax.dot_general(a, b, (((1,), (1,)), ((), ())), preferred_element_type=F32)


def three_parts(x):
    hi = x.astype(BF16).astype(F32)
    mid = (x - hi).astype(BF16).astype(F32)
    lo = (x - hi - mid).astype(BF16).astype(F32)
    return hi, mid, lo


def load(refs, scratch, sems):
    copies = [
        pltpu.make_async_copy(ref, buf, sems.at[i])
        for i, (ref, buf) in enumerate(zip(refs, scratch, strict=True))
    ]
    for copy in copies:
        copy.start()
    return copies


def my_turn():
    return lax.div(lax.axis_index("grp"), 4)


def route_kernel(
    pool, q_hbm, table_hbm, len_hbm, place_hbm, pk_hbm, pv_hbm, send_ref, where_ref,
    q_ref, table_ref, len_ref, place_ref, rows_ref, sems,
):
    requests = q_ref.shape[0]
    entries = requests * MAXP
    devices = send_ref.shape[0]
    cells = devices * CAP
    mine = lax.axis_index("blk")
    group = lax.axis_index("grp")
    turn = my_turn()
    kv_at = pl.ds(pl.multiple_of(turn * KV, KV), KV)

    def fetch_rows(source):
        return pltpu.make_async_copy(source.at[:, kv_at], rows_ref, sems.at[4])

    @pl.when(lax.rem(group, 2) == 0)
    def _():
        fetch_rows(pk_hbm).start()

    @pl.when(lax.rem(group, 2) == 1)
    def _():
        fetch_rows(pv_hbm).start()

    copies = load(
        (place_hbm, table_hbm, len_hbm, q_hbm), (place_ref, table_ref, len_ref, q_ref), sems
    )
    fetch_rows(pk_hbm).wait()
    depth = rows_ref.shape[0]
    shape = (cells, depth)
    cell = iota(shape, 0)
    each = depth // 4 // CAP
    first = depth // 2 * lax.rem(lax.div(group, 2), 2) + depth // 4 * lax.div(cell, cells // 2)
    for p in range(each):
        one = iota(shape, 1) == first + each * lax.rem(cell, CAP) + p
        rows = dot(jnp.where(one, 1.0, 0.0).astype(BF16), rows_ref[...]).astype(BF16)
        send_ref[:, :, ROW + KV * p : ROW + KV * (p + 1)] = rows.reshape(devices, CAP, KV)

    base = group * (devices * pool)
    square = iota((requests, requests), 0) == iota((requests, requests), 1)

    def column(row):
        row = jnp.broadcast_to(row, (requests, requests)).astype(F32)
        return jnp.sum(jnp.where(square, row, 0.0), axis=1, keepdims=True)

    for copy in copies[:3]:
        copy.wait()
    table = table_ref[...] - base
    page = jnp.concatenate([column(table[j : j + 1]) for j in range(MAXP)], axis=0)
    place = (place_ref[...] - base).astype(F32)
    lane = iota((entries, 128), 1).astype(F32)
    found = jnp.zeros((entries, 128), F32)
    for k in range(place.shape[0]):
        found = found + jnp.where(page == lane + 128.0 * k, place[k : k + 1, :], 0.0)
    physical = jnp.sum(found, axis=1, keepdims=True)
    holder = jnp.floor((physical + 0.5) * (1.0 / pool))
    slot = physical - holder * pool
    length = column(len_ref[...])
    tokens = jnp.concatenate(
        [jnp.clip(length - PAGE * j, 0.0, PAGE) for j in range(MAXP)], axis=0
    )
    used = tokens > 0.0
    at_home = holder == mine.astype(F32)
    remote = jnp.where(used & jnp.logical_not(at_home), 1.0, 0.0)
    member = jnp.where(holder == lane, remote, 0.0)
    below = jnp.where(iota((entries, entries), 1) < iota((entries, entries), 0), 1.0, 0.0)
    before = dot(below.astype(BF16), member.astype(BF16))
    rank = jnp.sum(before * member, axis=1, keepdims=True)
    where = jnp.where(remote > 0.0, holder * CAP + rank, cells + slot)
    where = jnp.where(used, where, -1.0)
    where_ref[...] = jnp.where(lane < TOKENS_AT, where, tokens)
    pick = jnp.where(where == lane, 1.0, 0.0).T[:cells]
    facts = jnp.where(lane == 0.0, slot, jnp.where(lane == 1.0, tokens, 0.0))
    side = dot(pick.astype(BF16), facts.astype(BF16)).astype(BF16)
    send_ref[:, :, QCOLS:ROW] = side.reshape(devices, CAP, SIDE)
    picked = over_entries(pick, requests)
    copies[3].wait()
    for c in range(CHUNKS):
        begin = c * CHUNK
        rows = dot(picked, q_ref[:, begin : begin + CHUNK]).astype(BF16)
        send_ref[:, :, begin : begin + CHUNK] = rows.reshape(devices, CAP, CHUNK)


def over_entries(pick, requests):
    parts = [pick[:, requests * j : requests * (j + 1)] for j in range(MAXP)]
    return functools.reduce(jnp.add, parts).astype(BF16)


def home_kernel(q_hbm, where_hbm, local_ref, s0, s1, s2, s3, q_ref, where_ref, sems):
    copies = load((where_hbm, q_hbm), (where_ref, q_ref), sems)
    requests = q_ref.shape[0]
    entries = requests * MAXP
    pool = local_ref.shape[0]
    cells = CAP * lax.axis_size("blk")
    copies[0].wait()
    where, tokens = where_ref[:, 0:1], where_ref[:, TOKENS_AT : TOKENS_AT + 1]
    lane = iota((entries, 128), 1).astype(F32)
    pick = jnp.where(where == lane, 1.0, 0.0).T[cells : cells + pool]
    facts = jnp.where(lane == 0.0, where - cells, jnp.where(lane == 1.0, tokens, 0.0))
    local_ref[:, QCOLS:ROW] = dot(pick.astype(BF16), facts.astype(BF16)).astype(BF16)
    picked = over_entries(pick, requests)
    copies[1].wait()
    for c in range(CHUNKS):
        cols = slice(c * CHUNK, (c + 1) * CHUNK)
        local_ref[:, cols] = dot(picked, q_ref[:, cols]).astype(BF16)
    turn = my_turn()
    for o, ref in enumerate((s0, s1, s2, s3)):
        at = pl.multiple_of((turn ^ o) * BLOCK, BLOCK)
        ref[...] = q_ref[:, pl.ds(at, BLOCK)]


def pages_kernel(
    got_hbm, local_hbm, k_hbm, v_hbm, answer_ref, own_ref,
    got_ref, local_ref, k_ref, v_ref, sems, chunk_sems,
):
    devices = got_ref.shape[0]
    cells = devices * CAP
    pool = k_ref.shape[0]
    step = 16
    pair = 2 * HD
    every = slice(None)
    here = got_hbm.at[:, :, pl.ds(0, ROW)]
    first = load((here, local_hbm), (got_ref, local_ref), sems)
    chunks = []
    for c in range(CHUNKS):
        kv_at = (every, every, pl.ds(c * pair, pair))
        chunks.append(
            load(
                (k_hbm.at[kv_at], v_hbm.at[kv_at]),
                (k_ref.at[kv_at], v_ref.at[kv_at]),
                chunk_sems.at[c],
            )
        )
    wide = (step, step * PAGE)
    column = iota(wide, 1)
    same = lax.div(column, PAGE) == iota(wide, 0)
    token = lax.rem(column, PAGE).astype(F32)
    side_lane = iota((step, SIDE), 1)
    lane = iota((cells, 128), 1).astype(F32)
    for copy in first:
        copy.wait()
    plain = got_ref[:, :, QCOLS:ROW].reshape(cells, SIDE)
    facts = plain.astype(F32)
    pick = jnp.where((facts[:, 0:1] == lane) & (facts[:, 1:2] > 0.0), 1.0, 0.0)
    fetch = pick.T[:pool].astype(BF16)
    pick = pick[:, :pool].astype(BF16)
    tokens = (dot(fetch, plain) + local_ref[:, QCOLS:ROW].astype(F32))[:, 1:2]
    sums = [jnp.zeros((step, SIDE), F32) for _ in range(pool // step)]
    masks = []
    for g in range(pool // step):
        bias = jnp.where(same & (token < tokens[step * g : step * (g + 1)]), 0.0, VERY_LOW)
        masks.append(jnp.concatenate([bias] * (2 * GROUP), axis=0))
    nothing = jnp.zeros((step * GROUP, HD), BF16)
    spans = [slice(step * g, step * (g + 1)) for g in range(pool // step)]

    def score(c, g, rows):
        span = spans[g]
        one, two = (
            jnp.concatenate(
                [rows[span, (GROUP * k + i) * HD : (GROUP * k + i + 1) * HD] for i in range(GROUP)],
                axis=0,
            )
            for k in range(2)
        )
        heads = jnp.concatenate(
            [jnp.concatenate([one, nothing], axis=1), jnp.concatenate([nothing, two], axis=1)], axis=0
        )
        keys = k_ref[span, :, c * pair : (c + 1) * pair].reshape(step * PAGE, pair)
        return dot_t(heads, keys) * SCALE + masks[g]

    def weigh(scores):
        top = jnp.max(scores, axis=1, keepdims=True)
        weights = jnp.exp(scores - top)
        total = jnp.sum(weights, axis=1, keepdims=True)
        return weights.astype(BF16), total, top + jnp.log(total)

    def mix(c, g, weights, total, log_sum):
        span = spans[g]
        values = v_ref[span, :, c * pair : (c + 1) * pair].reshape(step * PAGE, pair)
        mixture = dot(weights, values) / total
        for i in range(2 * GROUP):
            here = slice(step * i, step * (i + 1))
            part = mixture[here, :HD] if i < GROUP else mixture[here, HD:]
            at = c * CHUNK + i * HD
            own_ref[span, at : at + HD] = part.astype(BF16)
            mine = lax.rem(side_lane, QH) == c * 2 * GROUP + i
            sums[g] = jnp.where(mine, log_sum[here], sums[g])

    def ask(c):
        cols = slice(c * CHUNK, (c + 1) * CHUNK)
        asked = got_ref[:, :, cols].reshape(cells, CHUNK)
        return (dot(fetch, asked) + local_ref[:, cols].astype(F32)).astype(BF16)

    for chunk in chunks:
        for copy in chunk:
            copy.wait()
    steps = [(c, g) for c in range(CHUNKS) for g in range(len(spans))]
    rows = {c: ask(c) for c in range(CHUNKS)}
    scores = {s: score(*s, rows[s[0]]) for s in steps[:2]}
    weighed = {}
    for n, s in enumerate(steps + [None]):
        if n + 2 < len(steps):
            t = steps[n + 2]
            scores[t] = score(*t, rows[t[0]])
        if s is not None:
            weighed[s] = weigh(scores.pop(s))
        if n >= 1:
            mix(*steps[n - 1], *weighed.pop(steps[n - 1]))
    for g in range(pool // step):
        hi, mid, lo = three_parts(sums[g])
        side = jnp.where(side_lane < QH, hi, jnp.where(side_lane < 2 * QH, mid, lo))
        own_ref[step * g : step * (g + 1), QCOLS:ROW] = side.astype(BF16)
    for c in range(0, QCOLS, 640):
        cols = slice(c, c + 640)
        rows = dot(pick, own_ref[:, cols]).astype(BF16)
        answer_ref[:, :, cols] = rows.reshape(devices, CAP, 640)
    rows = dot(pick, own_ref[:, QCOLS:ROW]).astype(BF16)
    answer_ref[:, :, QCOLS:ROW] = rows.reshape(devices, CAP, SIDE)


def prefix_kernel(q0, q1, q2, q3, kv_mine, kv_other, o0, o1, o2, o3):
    requests = q0.shape[0]
    rows = requests * SHARE
    step = 256
    chunks = [slice(c, c + step) for c in range(0, kv_mine.shape[0], step)]
    core = lax.rem(lax.axis_index("grp"), 2)
    lane = iota((rows, SIDE), 1)
    asked = (q0, q1, q2, q3)
    outs = (o0, o1, o2, o3)

    def attend(k_ref, v_ref):
        sums = jnp.zeros((rows, SIDE), F32)

        def score(h):
            heads = jnp.concatenate([q[:, h * HD : (h + 1) * HD] for q in asked], axis=0)
            kv = slice(h // GROUP * HD, (h // GROUP + 1) * HD)
            return [dot_t(heads, k_ref[c, kv]) * SCALE for c in chunks]

        def weigh(scores):
            top = jnp.max(functools.reduce(jnp.maximum, scores), axis=1, keepdims=True)
            weights = [jnp.exp(s - top) for s in scores]
            total = jnp.sum(functools.reduce(jnp.add, weights), axis=1, keepdims=True)
            return [w.astype(BF16) for w in weights], total, top + jnp.log(total)

        def mix(h, weights, total):
            kv = slice(h // GROUP * HD, (h // GROUP + 1) * HD)
            parts = [dot(w, v_ref[c, kv]) for c, w in zip(chunks, weights)]
            mixture = (functools.reduce(jnp.add, parts) / total).astype(BF16)
            for o, out in enumerate(outs):
                out[:, h * HD : (h + 1) * HD] = mixture[requests * o : requests * (o + 1)]

        scores, weighed = {0: score(0)}, {}
        for h in range(HEADS + 1):
            if h + 1 < HEADS:
                scores[h + 1] = score(h + 1)
            if h < HEADS:
                *weighed[h], log_sum = weigh(scores.pop(h))
                sums = jnp.where(lax.rem(lane, HEADS) == h, log_sum, sums)
            if h:
                mix(h - 1, *weighed.pop(h - 1))

        hi, mid, lo = three_parts(sums)
        side = jnp.where(lane < HEADS, hi, jnp.where(lane < 2 * HEADS, mid, lo)).astype(BF16)
        for o, out in enumerate(outs):
            out[:, BLOCK:] = side[requests * o : requests * (o + 1)]

    @pl.when(core == 0)
    def _():
        attend(kv_mine, kv_other)

    @pl.when(core == 1)
    def _():
        attend(kv_other, kv_mine)


def join_kernel(got_ref, own_ref, where_ref, *refs):
    *served, out_hbm, out_ref, sems = refs
    entries = where_ref.shape[0]
    requests = served[0].shape[0]
    cells = got_ref.shape[0] * CAP
    pool = own_ref.shape[0]
    lane = iota((entries, 128), 1)
    where = where_ref[:, 0:1]
    pick = jnp.where(where == lane.astype(F32), 1.0, 0.0).astype(BF16)
    far, near = pick[:, :cells], pick[:, cells : cells + pool]
    side = dot(far, got_ref[:, :, QCOLS:ROW].reshape(cells, SIDE)) + dot(near, own_ref[:, QCOLS:ROW])
    sums = side + pltpu.roll(side, SIDE - QH, 1) + pltpu.roll(side, SIDE - 2 * QH, 1)
    sums = jnp.where(where >= 0.0, sums, VERY_LOW)
    turn = my_turn()
    sent = []
    for o, p_ref in enumerate(served):
        turned = turn ^ o
        at = pl.multiple_of(turned * BLOCK, 128)
        cols = pl.ds(at, BLOCK)
        got = got_ref[:, :, cols].reshape(cells, BLOCK)
        rows = dot(far, got) + dot(near, own_ref[:, cols])
        moved = pltpu.roll(sums, lax.rem(SIDE - turned * HEADS, SIDE), 1)
        pre = p_ref[:, BLOCK:].astype(F32)
        pre = pre + pltpu.roll(pre, SIDE - HEADS, 1) + pltpu.roll(pre, SIDE - 2 * HEADS, 1)
        logs = [moved[requests * j : requests * (j + 1)] for j in range(MAXP)]
        top = functools.reduce(jnp.maximum, logs, pre)
        parts = [jnp.exp(x - top) for x in logs]
        part = jnp.exp(pre - top)
        total = functools.reduce(jnp.add, parts, part)
        parts = [x / total for x in parts]
        part = part / total
        for h in range(HEADS):
            here = slice(h * HD, (h + 1) * HD)
            mixture = part[:, h : h + 1] * p_ref[:, here].astype(F32)
            for j in range(MAXP):
                mixture = mixture + parts[j][:, h : h + 1] * rows[requests * j : requests * (j + 1), here]
            out_ref[:, pl.ds(pl.multiple_of(at + h * HD, 128), HD)] = mixture.astype(BF16)
        sent += load((out_ref.at[:, cols],), (out_hbm.at[:, cols],), sems.at[pl.ds(o, 1)])
    for copy in sent:
        copy.wait()


def call(kernel, out_shape, flops, *args, in_hbm=(), out_hbm=(), scratch=(), room=62_150_000):
    specs = [
        [pl.BlockSpec(memory_space=pl.ANY if i in hbm else pltpu.VMEM) for i in range(n)]
        for n, hbm in ((len(args), in_hbm), (len(out_shape), out_hbm))
    ]
    return pl.pallas_call(
        kernel,
        out_shape=[jax.ShapeDtypeStruct(s, d) for s, d in out_shape],
        in_specs=specs[0],
        out_specs=specs[1],
        scratch_shapes=list(scratch),
        compiler_params=pltpu.CompilerParams(vmem_limit_bytes=room),
        cost_estimate=pl.CostEstimate(flops=flops, bytes_accessed=1 << 22, transcendentals=0),
    )(*args)


def like(x):
    return pltpu.VMEM(x.shape, x.dtype)


def semaphores(*shape):
    return pltpu.SemaphoreType.DMA(shape)


def route(queries, tables, lengths, places, prefix_keys, prefix_values, devices, pool):
    requests, depth = queries.shape[0], prefix_keys.shape[0]
    shape = (devices, CAP, ROW + depth // 4 // CAP * KV)
    args = (queries, tables, lengths, places)
    return call(
        functools.partial(route_kernel, pool),
        [(shape, BF16), ((requests * MAXP, 128), F32)],
        10**8,
        *args,
        prefix_keys,
        prefix_values,
        in_hbm=range(6),
        scratch=(
            *map(like, args),
            pltpu.VMEM((depth, KV), BF16),
            semaphores(5),
        ),
    )


def home(queries, where, pool):
    return call(
        home_kernel,
        [((pool, ROW), BF16)] + [((queries.shape[0], BLOCK), BF16)] * SHARE,
        10**8,
        queries,
        where,
        in_hbm=range(2),
        scratch=(like(queries), like(where), semaphores(2)),
    )


def pages(got, local, suffix_keys, suffix_values):
    shape = (got.shape[0], CAP, ROW)
    return call(
        pages_kernel,
        [(shape, BF16), (local.shape, BF16)],
        10**9,
        got,
        local,
        suffix_keys,
        suffix_values,
        in_hbm=range(4),
        scratch=(
            pltpu.VMEM(shape, BF16),
            *map(like, (local, suffix_keys, suffix_values)),
            semaphores(2),
            semaphores(CHUNKS, 2),
        ),
    )


def prefix(asked, kv_mine, kv_other):
    shape = (asked[0].shape[0], BLOCK + SIDE)
    return call(
        prefix_kernel, [(shape, BF16)] * SHARE, 10**9, *asked, kv_mine, kv_other, room=40 << 20
    )


def join(back, own, where, served):
    shape = (served[0].shape[0], QCOLS)
    (out,) = call(
        join_kernel,
        [(shape, BF16)],
        10**8,
        back,
        own,
        where,
        *served,
        out_hbm=(0,),
        scratch=(pltpu.VMEM(shape, BF16), semaphores(SHARE)),
        room=32 << 20,
    )
    return out


def body(
    queries, page_table, suffix_len, place, suffix_keys, suffix_values, prefix_keys, prefix_values
):
    pool = suffix_keys.shape[0]
    devices = lax.axis_size("blk")
    group = lax.axis_size("grp")
    lengths, places = suffix_len.reshape(1, -1), place.reshape(-1, 128)
    send, where = route(
        queries, page_table.T, lengths, places, prefix_keys, prefix_values, devices, pool
    )
    flip = lambda x, bits: lax.ppermute(x, "grp", [(i, i ^ bits) for i in range(group)])
    turned = lambda xs: [flip(x, 4 * o) if o else x for o, x in enumerate(xs)]
    exchange = lambda x: lax.all_to_all(x, "blk", split_axis=0, concat_axis=0, tiled=True)
    got = exchange(send)
    local, *asked = home(queries, where, pool)
    asked = turned(asked)
    local, *asked = lax.optimization_barrier((local, *asked))
    answer, own = pages(got, local, suffix_keys, suffix_values)
    back = exchange(answer)
    part, own = lax.optimization_barrier((got[:, :, ROW:], own))
    part = part.reshape(-1, KV)
    pairs = [(i, i ^ (devices // 2)) for i in range(devices)]
    both = [
        (g * devices + i, (g ^ 2) * devices + j) for g in range(group) for i, j in pairs
    ]
    around = [
        flip(part, 2), lax.ppermute(part, "blk", pairs), lax.ppermute(part, ("grp", "blk"), both)
    ]
    kv_mine = jnp.concatenate([part, *around], axis=0)
    served = prefix(asked, kv_mine, flip(kv_mine, 1))
    return join(back, own, where, turned(served))


def solution(mesh):
    return jax.shard_map(
        body,
        mesh=mesh,
        in_specs=(
            P(("grp", "blk"), None),
            P(("grp", "blk"), None),
            P(("grp", "blk")),
            P("grp"),
            P(("grp", "blk"), None, None),
            P(("grp", "blk"), None, None),
            P("blk", None),
            P("blk", None),
        ),
        out_specs=P(("grp", "blk"), None),
        check_vma=False,
    )
```

```python
import functools

import jax
import jax.numpy as jnp
from jax import lax
from jax.experimental import pallas as pl
from jax.experimental.pallas import tpu as pltpu
from jax.sharding import PartitionSpec as P

QH = 40
KVH = 8
HD = 128
PAGE = 16
MAXP = 4
CAP = 2
GROUP = QH // KVH
QCOLS = QH * HD
SIDE = 128
ROW = QCOLS + SIDE
SHARE = 4
HEADS = QH // SHARE
BLOCK = HEADS * HD
KV = KVH // SHARE * HD
CHUNKS = 4
CHUNK = QCOLS // CHUNKS
TOKENS_AT = 64
SCALE = HD ** (-0.5)
VERY_LOW = -1e30
F32 = jnp.float32
BF16 = jnp.bfloat16


def iota(shape, axis):
    return lax.broadcasted_iota(jnp.int32, shape, axis)


def dot(a, b):
    return lax.dot_general(a, b, (((1,), (0,)), ((), ())), preferred_element_type=F32)


def dot_t(a, b):
    return lax.dot_general(a, b, (((1,), (1,)), ((), ())), preferred_element_type=F32)


def three_parts(x):
    hi = x.astype(BF16).astype(F32)
    mid = (x - hi).astype(BF16).astype(F32)
    lo = (x - hi - mid).astype(BF16).astype(F32)
    return hi, mid, lo


def load(refs, scratch, sems):
    copies = [
        pltpu.make_async_copy(ref, buf, sems.at[i])
        for i, (ref, buf) in enumerate(zip(refs, scratch, strict=True))
    ]
    for copy in copies:
        copy.start()
    return copies


def my_turn():
    return lax.div(lax.axis_index("grp"), 4)


def route_kernel(
    pool, q_hbm, table_hbm, len_hbm, place_hbm, pk_hbm, pv_hbm, send_ref, where_ref,
    q_ref, table_ref, len_ref, place_ref, rows_ref, sems,
):
    requests = q_ref.shape[0]
    entries = requests * MAXP
    devices = send_ref.shape[0]
    cells = devices * CAP
    mine = lax.axis_index("blk")
    group = lax.axis_index("grp")
    turn = my_turn()
    kv_at = pl.ds(pl.multiple_of(turn * KV, KV), KV)

    def fetch_rows(source):
        return pltpu.make_async_copy(source.at[:, kv_at], rows_ref, sems.at[4])

    @pl.when(lax.rem(group, 2) == 0)
    def _():
        fetch_rows(pk_hbm).start()

    @pl.when(lax.rem(group, 2) == 1)
    def _():
        fetch_rows(pv_hbm).start()

    copies = load(
        (place_hbm, table_hbm, len_hbm, q_hbm), (place_ref, table_ref, len_ref, q_ref), sems
    )
    fetch_rows(pk_hbm).wait()
    depth = rows_ref.shape[0]
    shape = (cells, depth)
    cell = iota(shape, 0)
    each = depth // 4 // CAP
    first = depth // 2 * lax.rem(lax.div(group, 2), 2) + depth // 4 * lax.div(cell, cells // 2)
    for p in range(each):
        one = iota(shape, 1) == first + each * lax.rem(cell, CAP) + p
        rows = dot(jnp.where(one, 1.0, 0.0).astype(BF16), rows_ref[...]).astype(BF16)
        send_ref[:, :, ROW + KV * p : ROW + KV * (p + 1)] = rows.reshape(devices, CAP, KV)

    base = group * (devices * pool)
    square = iota((requests, requests), 0) == iota((requests, requests), 1)

    def column(row):
        row = jnp.broadcast_to(row, (requests, requests)).astype(F32)
        return jnp.sum(jnp.where(square, row, 0.0), axis=1, keepdims=True)

    for copy in copies[:3]:
        copy.wait()
    table = table_ref[...] - base
    page = jnp.concatenate([column(table[j : j + 1]) for j in range(MAXP)], axis=0)
    place = (place_ref[...] - base).astype(F32)
    lane = iota((entries, 128), 1).astype(F32)
    found = jnp.zeros((entries, 128), F32)
    for k in range(place.shape[0]):
        found = found + jnp.where(page == lane + 128.0 * k, place[k : k + 1, :], 0.0)
    physical = jnp.sum(found, axis=1, keepdims=True)
    holder = jnp.floor((physical + 0.5) * (1.0 / pool))
    slot = physical - holder * pool
    length = column(len_ref[...])
    tokens = jnp.concatenate(
        [jnp.clip(length - PAGE * j, 0.0, PAGE) for j in range(MAXP)], axis=0
    )
    used = tokens > 0.0
    at_home = holder == mine.astype(F32)
    remote = jnp.where(used & jnp.logical_not(at_home), 1.0, 0.0)
    member = jnp.where(holder == lane, remote, 0.0)
    below = jnp.where(iota((entries, entries), 1) < iota((entries, entries), 0), 1.0, 0.0)
    before = dot(below.astype(BF16), member.astype(BF16))
    rank = jnp.sum(before * member, axis=1, keepdims=True)
    where = jnp.where(remote > 0.0, holder * CAP + rank, cells + slot)
    where = jnp.where(used, where, -1.0)
    where_ref[...] = jnp.where(lane < TOKENS_AT, where, tokens)
    pick = jnp.where(where == lane, 1.0, 0.0).T[:cells]
    facts = jnp.where(lane == 0.0, slot, jnp.where(lane == 1.0, tokens, 0.0))
    side = dot(pick.astype(BF16), facts.astype(BF16)).astype(BF16)
    send_ref[:, :, QCOLS:ROW] = side.reshape(devices, CAP, SIDE)
    picked = over_entries(pick, requests)
    copies[3].wait()
    for c in range(CHUNKS):
        begin = c * CHUNK
        rows = dot(picked, q_ref[:, begin : begin + CHUNK]).astype(BF16)
        send_ref[:, :, begin : begin + CHUNK] = rows.reshape(devices, CAP, CHUNK)


def over_entries(pick, requests):
    parts = [pick[:, requests * j : requests * (j + 1)] for j in range(MAXP)]
    return functools.reduce(jnp.add, parts).astype(BF16)


def home_kernel(q_hbm, where_ref, local_ref, s0, s1, s2, s3, q_ref, sems):
    copies = load((q_hbm,), (q_ref,), sems)
    requests = q_ref.shape[0]
    entries = requests * MAXP
    pool = local_ref.shape[0]
    cells = CAP * lax.axis_size("blk")
    where, tokens = where_ref[:, 0:1], where_ref[:, TOKENS_AT : TOKENS_AT + 1]
    lane = iota((entries, 128), 1).astype(F32)
    pick = jnp.where(where == lane, 1.0, 0.0).T[cells : cells + pool]
    facts = jnp.where(lane == 0.0, where - cells, jnp.where(lane == 1.0, tokens, 0.0))
    local_ref[:, QCOLS:ROW] = dot(pick.astype(BF16), facts.astype(BF16)).astype(BF16)
    picked = over_entries(pick, requests)
    copies[0].wait()
    for c in range(CHUNKS):
        cols = slice(c * CHUNK, (c + 1) * CHUNK)
        local_ref[:, cols] = dot(picked, q_ref[:, cols]).astype(BF16)
    turn = my_turn()
    for o, ref in enumerate((s0, s1, s2, s3)):
        at = pl.multiple_of((turn ^ o) * BLOCK, BLOCK)
        ref[...] = q_ref[:, pl.ds(at, BLOCK)]


def pages_kernel(
    got_ref, local_ref, k_hbm, v_hbm, answer_ref, own_ref, k_ref, v_ref, chunk_sems,
):
    devices = got_ref.shape[0]
    cells = devices * CAP
    pool = k_ref.shape[0]
    step = 16
    pair = 2 * HD
    every = slice(None)
    chunks = []
    for c in range(CHUNKS):
        kv_at = (every, every, pl.ds(c * pair, pair))
        chunks.append(
            load(
                (k_hbm.at[kv_at], v_hbm.at[kv_at]),
                (k_ref.at[kv_at], v_ref.at[kv_at]),
                chunk_sems.at[c],
            )
        )
    wide = (step, step * PAGE)
    column = iota(wide, 1)
    same = lax.div(column, PAGE) == iota(wide, 0)
    token = lax.rem(column, PAGE).astype(F32)
    side_lane = iota((step, SIDE), 1)
    lane = iota((cells, 128), 1).astype(F32)
    plain = got_ref[:, :, QCOLS:ROW].reshape(cells, SIDE)
    facts = plain.astype(F32)
    pick = jnp.where((facts[:, 0:1] == lane) & (facts[:, 1:2] > 0.0), 1.0, 0.0)
    fetch = pick.T[:pool].astype(BF16)
    pick = pick[:, :pool].astype(BF16)
    tokens = (dot(fetch, plain) + local_ref[:, QCOLS:ROW].astype(F32))[:, 1:2]
    sums = [jnp.zeros((step, SIDE), F32) for _ in range(pool // step)]
    masks = []
    for g in range(pool // step):
        bias = jnp.where(same & (token < tokens[step * g : step * (g + 1)]), 0.0, VERY_LOW)
        masks.append(jnp.concatenate([bias] * (2 * GROUP), axis=0))
    nothing = jnp.zeros((step * GROUP, HD), BF16)
    spans = [slice(step * g, step * (g + 1)) for g in range(pool // step)]

    def score(c, g, rows):
        span = spans[g]
        one, two = (
            jnp.concatenate(
                [rows[span, (GROUP * k + i) * HD : (GROUP * k + i + 1) * HD] for i in range(GROUP)],
                axis=0,
            )
            for k in range(2)
        )
        heads = jnp.concatenate(
            [jnp.concatenate([one, nothing], axis=1), jnp.concatenate([nothing, two], axis=1)], axis=0
        )
        keys = k_ref[span, :, c * pair : (c + 1) * pair].reshape(step * PAGE, pair)
        return dot_t(heads, keys) * SCALE + masks[g]

    def weigh(scores):
        top = jnp.max(scores, axis=1, keepdims=True)
        weights = jnp.exp(scores - top)
        total = jnp.sum(weights, axis=1, keepdims=True)
        return weights.astype(BF16), total, top + jnp.log(total)

    def mix(c, g, weights, total, log_sum):
        span = spans[g]
        values = v_ref[span, :, c * pair : (c + 1) * pair].reshape(step * PAGE, pair)
        mixture = dot(weights, values) / total
        for i in range(2 * GROUP):
            here = slice(step * i, step * (i + 1))
            part = mixture[here, :HD] if i < GROUP else mixture[here, HD:]
            at = c * CHUNK + i * HD
            own_ref[span, at : at + HD] = part.astype(BF16)
            mine = lax.rem(side_lane, QH) == c * 2 * GROUP + i
            sums[g] = jnp.where(mine, log_sum[here], sums[g])

    def ask(c):
        cols = slice(c * CHUNK, (c + 1) * CHUNK)
        asked = got_ref[:, :, cols].reshape(cells, CHUNK)
        return (dot(fetch, asked) + local_ref[:, cols].astype(F32)).astype(BF16)

    for chunk in chunks:
        for copy in chunk:
            copy.wait()
    steps = [(c, g) for c in range(CHUNKS) for g in range(len(spans))]
    rows = {c: ask(c) for c in range(CHUNKS)}
    scores = {s: score(*s, rows[s[0]]) for s in steps[:2]}
    weighed = {}
    for n, s in enumerate(steps + [None]):
        if n + 2 < len(steps):
            t = steps[n + 2]
            scores[t] = score(*t, rows[t[0]])
        if s is not None:
            weighed[s] = weigh(scores.pop(s))
        if n >= 1:
            mix(*steps[n - 1], *weighed.pop(steps[n - 1]))
    for g in range(pool // step):
        hi, mid, lo = three_parts(sums[g])
        side = jnp.where(side_lane < QH, hi, jnp.where(side_lane < 2 * QH, mid, lo))
        own_ref[step * g : step * (g + 1), QCOLS:ROW] = side.astype(BF16)
    for c in range(0, QCOLS, 640):
        cols = slice(c, c + 640)
        rows = dot(pick, own_ref[:, cols]).astype(BF16)
        answer_ref[:, :, cols] = rows.reshape(devices, CAP, 640)
    rows = dot(pick, own_ref[:, QCOLS:ROW]).astype(BF16)
    answer_ref[:, :, QCOLS:ROW] = rows.reshape(devices, CAP, SIDE)


def prefix_kernel(q0, q1, q2, q3, kv_mine, kv_other, o0, o1, o2, o3):
    requests = q0.shape[0]
    rows = requests * SHARE
    step = 256
    chunks = [slice(c, c + step) for c in range(0, kv_mine.shape[0], step)]
    core = lax.rem(lax.axis_index("grp"), 2)
    lane = iota((rows, SIDE), 1)
    asked = (q0, q1, q2, q3)
    outs = (o0, o1, o2, o3)

    def attend(k_ref, v_ref):
        sums = jnp.zeros((rows, SIDE), F32)

        def score(h):
            heads = jnp.concatenate([q[:, h * HD : (h + 1) * HD] for q in asked], axis=0)
            kv = slice(h // GROUP * HD, (h // GROUP + 1) * HD)
            return [dot_t(heads, k_ref[c, kv]) * SCALE for c in chunks]

        def weigh(scores):
            top = jnp.max(functools.reduce(jnp.maximum, scores), axis=1, keepdims=True)
            weights = [jnp.exp(s - top) for s in scores]
            total = jnp.sum(functools.reduce(jnp.add, weights), axis=1, keepdims=True)
            return [w.astype(BF16) for w in weights], total, top + jnp.log(total)

        def mix(h, weights, total):
            kv = slice(h // GROUP * HD, (h // GROUP + 1) * HD)
            parts = [dot(w, v_ref[c, kv]) for c, w in zip(chunks, weights)]
            mixture = (functools.reduce(jnp.add, parts) / total).astype(BF16)
            for o, out in enumerate(outs):
                out[:, h * HD : (h + 1) * HD] = mixture[requests * o : requests * (o + 1)]

        scores, weighed = {0: score(0)}, {}
        for h in range(HEADS + 1):
            if h + 1 < HEADS:
                scores[h + 1] = score(h + 1)
            if h < HEADS:
                *weighed[h], log_sum = weigh(scores.pop(h))
                sums = jnp.where(lax.rem(lane, HEADS) == h, log_sum, sums)
            if h:
                mix(h - 1, *weighed.pop(h - 1))

        hi, mid, lo = three_parts(sums)
        side = jnp.where(lane < HEADS, hi, jnp.where(lane < 2 * HEADS, mid, lo)).astype(BF16)
        for o, out in enumerate(outs):
            out[:, BLOCK:] = side[requests * o : requests * (o + 1)]

    @pl.when(core == 0)
    def _():
        attend(kv_mine, kv_other)

    @pl.when(core == 1)
    def _():
        attend(kv_other, kv_mine)


def join_kernel(got_ref, own_ref, where_ref, *refs):
    *served, out_hbm, out_ref, sems = refs
    entries = where_ref.shape[0]
    requests = served[0].shape[0]
    cells = got_ref.shape[0] * CAP
    pool = own_ref.shape[0]
    lane = iota((entries, 128), 1)
    where = where_ref[:, 0:1]
    pick = jnp.where(where == lane.astype(F32), 1.0, 0.0).astype(BF16)
    far, near = pick[:, :cells], pick[:, cells : cells + pool]
    side = dot(far, got_ref[:, :, QCOLS:ROW].reshape(cells, SIDE)) + dot(near, own_ref[:, QCOLS:ROW])
    sums = side + pltpu.roll(side, SIDE - QH, 1) + pltpu.roll(side, SIDE - 2 * QH, 1)
    sums = jnp.where(where >= 0.0, sums, VERY_LOW)
    turn = my_turn()
    sent = []

    def bring(o):
        cols = pl.ds(pl.multiple_of((turn ^ o) * BLOCK, 128), BLOCK)
        got = got_ref[:, :, cols].reshape(cells, BLOCK)
        return dot(far, got) + dot(near, own_ref[:, cols])

    def shares(o):
        moved = pltpu.roll(sums, lax.rem(SIDE - (turn ^ o) * HEADS, SIDE), 1)
        pre = served[o][:, BLOCK:].astype(F32)
        pre = pre + pltpu.roll(pre, SIDE - HEADS, 1) + pltpu.roll(pre, SIDE - 2 * HEADS, 1)
        logs = [moved[requests * j : requests * (j + 1)] for j in range(MAXP)]
        top = functools.reduce(jnp.maximum, logs, pre)
        parts = [jnp.exp(x - top) for x in (*logs, pre)]
        total = functools.reduce(jnp.add, parts)
        return [x / total for x in parts]

    weights = [shares(o) for o in range(SHARE)]
    rows = bring(0)
    for o in range(SHARE):
        ahead = bring(o + 1) if o + 1 < SHARE else None
        *parts, part = weights[o]
        at = pl.multiple_of((turn ^ o) * BLOCK, 128)
        for h in range(HEADS):
            here = slice(h * HD, (h + 1) * HD)
            mixture = part[:, h : h + 1] * served[o][:, here].astype(F32)
            for j in range(MAXP):
                mixture = mixture + parts[j][:, h : h + 1] * rows[requests * j : requests * (j + 1), here]
            out_ref[:, pl.ds(pl.multiple_of(at + h * HD, 128), HD)] = mixture.astype(BF16)
        rows = ahead
        cols = pl.ds(at, BLOCK)
        sent += load((out_ref.at[:, cols],), (out_hbm.at[:, cols],), sems.at[pl.ds(o, 1)])
    for copy in sent:
        copy.wait()


def call(kernel, out_shape, flops, *args, in_hbm=(), out_hbm=(), scratch=(), room=24 << 20):
    args = [
        pltpu.with_memory_space_constraint(x, pltpu.HBM) if i in in_hbm else x
        for i, x in enumerate(args)
    ]
    specs = [
        [pl.BlockSpec(memory_space=pl.ANY if i in hbm else pltpu.VMEM) for i in range(n)]
        for n, hbm in ((len(args), in_hbm), (len(out_shape), out_hbm))
    ]
    return pl.pallas_call(
        kernel,
        out_shape=[jax.ShapeDtypeStruct(s, d) for s, d in out_shape],
        in_specs=specs[0],
        out_specs=specs[1],
        scratch_shapes=list(scratch),
        compiler_params=pltpu.CompilerParams(vmem_limit_bytes=room),
        cost_estimate=pl.CostEstimate(flops=flops, bytes_accessed=1 << 22, transcendentals=0),
    )(*args)


def like(x):
    return pltpu.VMEM(x.shape, x.dtype)


def semaphores(*shape):
    return pltpu.SemaphoreType.DMA(shape)


def route(queries, tables, lengths, places, prefix_keys, prefix_values, devices, pool):
    requests, depth = queries.shape[0], prefix_keys.shape[0]
    shape = (devices, CAP, ROW + depth // 4 // CAP * KV)
    args = (queries, tables, lengths, places)
    return call(
        functools.partial(route_kernel, pool),
        [(shape, BF16), ((requests * MAXP, 128), F32)],
        10**8,
        *args,
        prefix_keys,
        prefix_values,
        in_hbm=range(6),
        scratch=(
            *map(like, args),
            pltpu.VMEM((depth, KV), BF16),
            semaphores(5),
        ),
    )


def home(queries, where, pool):
    return call(
        home_kernel,
        [((pool, ROW), BF16)] + [((queries.shape[0], BLOCK), BF16)] * SHARE,
        10**8,
        queries,
        where,
        in_hbm=(0,),
        scratch=(like(queries), semaphores(1)),
    )


def pages(got, local, suffix_keys, suffix_values):
    shape = (got.shape[0], CAP, ROW)
    return call(
        pages_kernel,
        [(shape, BF16), (local.shape, BF16)],
        10**9,
        got,
        local,
        suffix_keys,
        suffix_values,
        in_hbm=(2, 3),
        scratch=(*map(like, (suffix_keys, suffix_values)), semaphores(CHUNKS, 2)),
    )


def prefix(asked, kv_mine, kv_other):
    shape = (asked[0].shape[0], BLOCK + SIDE)
    return call(
        prefix_kernel, [(shape, BF16)] * SHARE, 10**9, *asked, kv_mine, kv_other
    )


def join(back, own, where, served):
    shape = (served[0].shape[0], QCOLS)
    (out,) = call(
        join_kernel,
        [(shape, BF16)],
        10**8,
        back,
        own,
        where,
        *served,
        out_hbm=(0,),
        scratch=(pltpu.VMEM(shape, BF16), semaphores(SHARE)),
    )
    return out


def body(
    queries, page_table, suffix_len, place, suffix_keys, suffix_values, prefix_keys, prefix_values
):
    pool = suffix_keys.shape[0]
    devices = lax.axis_size("blk")
    group = lax.axis_size("grp")
    lengths, places = suffix_len.reshape(1, -1), place.reshape(-1, 128)
    send, where = route(
        queries, page_table.T, lengths, places, prefix_keys, prefix_values, devices, pool
    )
    flip = lambda x, bits: lax.ppermute(x, "grp", [(i, i ^ bits) for i in range(group)])
    turned = lambda xs: [flip(x, 4 * o) if o else x for o, x in enumerate(xs)]
    exchange = lambda x: lax.all_to_all(x, "blk", split_axis=0, concat_axis=0, tiled=True)
    got = exchange(send)
    local, *asked = home(queries, where, pool)
    asked = turned(asked)
    local, *asked = lax.optimization_barrier((local, *asked))
    answer, own = pages(got, local, suffix_keys, suffix_values)
    back = exchange(answer)
    part, own = lax.optimization_barrier((got[:, :, ROW:], own))
    part = part.reshape(-1, KV)
    pairs = [(i, i ^ (devices // 2)) for i in range(devices)]
    both = [
        (g * devices + i, (g ^ 2) * devices + j) for g in range(group) for i, j in pairs
    ]
    around = [
        flip(part, 2), lax.ppermute(part, "blk", pairs), lax.ppermute(part, ("grp", "blk"), both)
    ]
    kv_mine = jnp.concatenate([part, *around], axis=0)
    served = prefix(asked, kv_mine, flip(kv_mine, 1))
    return join(back, own, where, turned(served))


def solution(mesh):
    return jax.shard_map(
        body,
        mesh=mesh,
        in_specs=(
            P(("grp", "blk"), None),
            P(("grp", "blk"), None),
            P(("grp", "blk")),
            P("grp"),
            P(("grp", "blk"), None, None),
            P(("grp", "blk"), None, None),
            P("blk", None),
            P("blk", None),
        ),
        out_specs=P(("grp", "blk"), None),
        check_vma=False,
    )
```

```python
import functools

import jax
import jax.numpy as jnp
from jax import lax
from jax.experimental import pallas as pl
from jax.experimental.pallas import tpu as pltpu
from jax.sharding import PartitionSpec as P

QH = 40
KVH = 8
HD = 128
PAGE = 16
MAXP = 4
CAP = 2
GROUP = QH // KVH
QCOLS = QH * HD
SIDE = 128
ROW = QCOLS + SIDE
SHARE = 4
HEADS = QH // SHARE
BLOCK = HEADS * HD
KV = KVH // SHARE * HD
CHUNKS = 4
CHUNK = QCOLS // CHUNKS
TOKENS_AT = 64
SCALE = HD ** (-0.5)
VERY_LOW = -1e30
F32 = jnp.float32
BF16 = jnp.bfloat16


def iota(shape, axis):
    return lax.broadcasted_iota(jnp.int32, shape, axis)


def dot(a, b):
    return lax.dot_general(a, b, (((1,), (0,)), ((), ())), preferred_element_type=F32)


def dot_t(a, b):
    return lax.dot_general(a, b, (((1,), (1,)), ((), ())), preferred_element_type=F32)


def three_parts(x):
    hi = x.astype(BF16).astype(F32)
    mid = (x - hi).astype(BF16).astype(F32)
    lo = (x - hi - mid).astype(BF16).astype(F32)
    return hi, mid, lo


def load(refs, scratch, sems):
    copies = [
        pltpu.make_async_copy(ref, buf, sems.at[i])
        for i, (ref, buf) in enumerate(zip(refs, scratch, strict=True))
    ]
    for copy in copies:
        copy.start()
    return copies


def my_turn():
    return lax.div(lax.axis_index("grp"), 4)


def route_kernel(
    pool, q_hbm, table_hbm, len_hbm, place_hbm, pk_hbm, pv_hbm, send_ref, where_ref,
    q_ref, table_ref, len_ref, place_ref, rows_ref, sems,
):
    requests = q_ref.shape[0]
    entries = requests * MAXP
    devices = send_ref.shape[0]
    cells = devices * CAP
    mine = lax.axis_index("blk")
    group = lax.axis_index("grp")
    turn = my_turn()
    kv_at = pl.ds(pl.multiple_of(turn * KV, KV), KV)

    def fetch_rows(source):
        return pltpu.make_async_copy(source.at[:, kv_at], rows_ref, sems.at[4])

    @pl.when(lax.rem(group, 2) == 0)
    def _():
        fetch_rows(pk_hbm).start()

    @pl.when(lax.rem(group, 2) == 1)
    def _():
        fetch_rows(pv_hbm).start()

    copies = load(
        (place_hbm, table_hbm, len_hbm, q_hbm), (place_ref, table_ref, len_ref, q_ref), sems
    )
    fetch_rows(pk_hbm).wait()
    depth = rows_ref.shape[0]
    shape = (cells, depth)
    cell = iota(shape, 0)
    each = depth // 4 // CAP
    first = depth // 2 * lax.rem(lax.div(group, 2), 2) + depth // 4 * lax.div(cell, cells // 2)
    for p in range(each):
        one = iota(shape, 1) == first + each * lax.rem(cell, CAP) + p
        rows = dot(jnp.where(one, 1.0, 0.0).astype(BF16), rows_ref[...]).astype(BF16)
        send_ref[:, :, ROW + KV * p : ROW + KV * (p + 1)] = rows.reshape(devices, CAP, KV)

    base = group * (devices * pool)
    square = iota((requests, requests), 0) == iota((requests, requests), 1)

    def column(row):
        row = jnp.broadcast_to(row, (requests, requests)).astype(F32)
        return jnp.sum(jnp.where(square, row, 0.0), axis=1, keepdims=True)

    for copy in copies[:3]:
        copy.wait()
    table = table_ref[...] - base
    page = jnp.concatenate([column(table[j : j + 1]) for j in range(MAXP)], axis=0)
    place = (place_ref[...] - base).astype(F32)
    lane = iota((entries, 128), 1).astype(F32)
    found = jnp.zeros((entries, 128), F32)
    for k in range(place.shape[0]):
        found = found + jnp.where(page == lane + 128.0 * k, place[k : k + 1, :], 0.0)
    physical = jnp.sum(found, axis=1, keepdims=True)
    holder = jnp.floor((physical + 0.5) * (1.0 / pool))
    slot = physical - holder * pool
    length = column(len_ref[...])
    tokens = jnp.concatenate(
        [jnp.clip(length - PAGE * j, 0.0, PAGE) for j in range(MAXP)], axis=0
    )
    used = tokens > 0.0
    at_home = holder == mine.astype(F32)
    remote = jnp.where(used & jnp.logical_not(at_home), 1.0, 0.0)
    member = jnp.where(holder == lane, remote, 0.0)
    below = jnp.where(iota((entries, entries), 1) < iota((entries, entries), 0), 1.0, 0.0)
    before = dot(below.astype(BF16), member.astype(BF16))
    rank = jnp.sum(before * member, axis=1, keepdims=True)
    where = jnp.where(remote > 0.0, holder * CAP + rank, cells + slot)
    where = jnp.where(used, where, -1.0)
    where_ref[...] = jnp.where(lane < TOKENS_AT, where, tokens)
    pick = jnp.where(where == lane, 1.0, 0.0).T[:cells]
    facts = jnp.where(lane == 0.0, slot, jnp.where(lane == 1.0, tokens, 0.0))
    side = dot(pick.astype(BF16), facts.astype(BF16)).astype(BF16)
    send_ref[:, :, QCOLS:ROW] = side.reshape(devices, CAP, SIDE)
    picked = over_entries(pick, requests)
    copies[3].wait()
    for c in range(CHUNKS):
        begin = c * CHUNK
        rows = dot(picked, q_ref[:, begin : begin + CHUNK]).astype(BF16)
        send_ref[:, :, begin : begin + CHUNK] = rows.reshape(devices, CAP, CHUNK)


def over_entries(pick, requests):
    parts = [pick[:, requests * j : requests * (j + 1)] for j in range(MAXP)]
    return functools.reduce(jnp.add, parts).astype(BF16)


def home_kernel(q_hbm, where_ref, local_ref, s0, s1, s2, s3, q_ref, sems):
    copies = load((q_hbm,), (q_ref,), sems)
    requests = q_ref.shape[0]
    entries = requests * MAXP
    pool = local_ref.shape[0]
    cells = CAP * lax.axis_size("blk")
    where, tokens = where_ref[:, 0:1], where_ref[:, TOKENS_AT : TOKENS_AT + 1]
    lane = iota((entries, 128), 1).astype(F32)
    pick = jnp.where(where == lane, 1.0, 0.0).T[cells : cells + pool]
    facts = jnp.where(lane == 0.0, where - cells, jnp.where(lane == 1.0, tokens, 0.0))
    local_ref[:, QCOLS:ROW] = dot(pick.astype(BF16), facts.astype(BF16)).astype(BF16)
    picked = over_entries(pick, requests)
    copies[0].wait()
    for c in range(CHUNKS):
        cols = slice(c * CHUNK, (c + 1) * CHUNK)
        local_ref[:, cols] = dot(picked, q_ref[:, cols]).astype(BF16)
    turn = my_turn()
    for o, ref in enumerate((s0, s1, s2, s3)):
        at = pl.multiple_of((turn ^ o) * BLOCK, BLOCK)
        ref[...] = q_ref[:, pl.ds(at, BLOCK)]


def pages_kernel(
    got_ref, local_ref, k_ref, v_hbm, answer_ref, own_ref, v_ref, chunk_sems,
):
    devices = got_ref.shape[0]
    cells = devices * CAP
    pool = k_ref.shape[0]
    step = 16
    pair = 2 * HD
    every = slice(None)
    chunks = []
    for c in range(CHUNKS):
        kv_at = (every, every, pl.ds(c * pair, pair))
        chunks.append(
            load(
                (v_hbm.at[kv_at],), (v_ref.at[kv_at],), chunk_sems.at[pl.ds(c, 1)]
            )
        )
    wide = (step, step * PAGE)
    column = iota(wide, 1)
    same = lax.div(column, PAGE) == iota(wide, 0)
    token = lax.rem(column, PAGE).astype(F32)
    side_lane = iota((step, SIDE), 1)
    lane = iota((cells, 128), 1).astype(F32)
    plain = got_ref[:, :, QCOLS:ROW].reshape(cells, SIDE)
    facts = plain.astype(F32)
    pick = jnp.where((facts[:, 0:1] == lane) & (facts[:, 1:2] > 0.0), 1.0, 0.0)
    fetch = pick.T[:pool].astype(BF16)
    pick = pick[:, :pool].astype(BF16)
    tokens = (dot(fetch, plain) + local_ref[:, QCOLS:ROW].astype(F32))[:, 1:2]
    sums = [jnp.zeros((step, SIDE), F32) for _ in range(pool // step)]
    masks = []
    for g in range(pool // step):
        bias = jnp.where(same & (token < tokens[step * g : step * (g + 1)]), 0.0, VERY_LOW)
        masks.append(jnp.concatenate([bias] * (2 * GROUP), axis=0))
    nothing = jnp.zeros((step * GROUP, HD), BF16)
    spans = [slice(step * g, step * (g + 1)) for g in range(pool // step)]

    def score(c, g, rows):
        span = spans[g]
        one, two = (
            jnp.concatenate(
                [rows[span, (GROUP * k + i) * HD : (GROUP * k + i + 1) * HD] for i in range(GROUP)],
                axis=0,
            )
            for k in range(2)
        )
        heads = jnp.concatenate(
            [jnp.concatenate([one, nothing], axis=1), jnp.concatenate([nothing, two], axis=1)], axis=0
        )
        keys = k_ref[span, :, c * pair : (c + 1) * pair].reshape(step * PAGE, pair)
        return dot_t(heads, keys) * SCALE + masks[g]

    def weigh(scores):
        top = jnp.max(scores, axis=1, keepdims=True)
        weights = jnp.exp(scores - top)
        total = jnp.sum(weights, axis=1, keepdims=True)
        return weights.astype(BF16), total, top + jnp.log(total)

    def mix(c, g, weights, total, log_sum):
        span = spans[g]
        values = v_ref[span, :, c * pair : (c + 1) * pair].reshape(step * PAGE, pair)
        mixture = dot(weights, values) / total
        for i in range(2 * GROUP):
            here = slice(step * i, step * (i + 1))
            part = mixture[here, :HD] if i < GROUP else mixture[here, HD:]
            at = c * CHUNK + i * HD
            own_ref[span, at : at + HD] = part.astype(BF16)
            mine = lax.rem(side_lane, QH) == c * 2 * GROUP + i
            sums[g] = jnp.where(mine, log_sum[here], sums[g])

    def ask(c):
        cols = slice(c * CHUNK, (c + 1) * CHUNK)
        asked = got_ref[:, :, cols].reshape(cells, CHUNK)
        return (dot(fetch, asked) + local_ref[:, cols].astype(F32)).astype(BF16)

    steps = [(c, g) for c in range(CHUNKS) for g in range(len(spans))]
    rows = {c: ask(c) for c in range(CHUNKS)}
    scores = {s: score(*s, rows[s[0]]) for s in steps[:2]}
    weighed = {}
    for n, s in enumerate(steps + [None]):
        if n + 2 < len(steps):
            t = steps[n + 2]
            scores[t] = score(*t, rows[t[0]])
        if s is not None:
            weighed[s] = weigh(scores.pop(s))
        if n == 1:
            for copy in chunks[0] + chunks[1]:
                copy.wait()
        if n == 7:
            for copy in chunks[2] + chunks[3]:
                copy.wait()
        if n >= 1:
            mix(*steps[n - 1], *weighed.pop(steps[n - 1]))
    for g in range(pool // step):
        hi, mid, lo = three_parts(sums[g])
        side = jnp.where(side_lane < QH, hi, jnp.where(side_lane < 2 * QH, mid, lo))
        own_ref[step * g : step * (g + 1), QCOLS:ROW] = side.astype(BF16)
    for c in range(0, QCOLS, 640):
        cols = slice(c, c + 640)
        rows = dot(pick, own_ref[:, cols]).astype(BF16)
        answer_ref[:, :, cols] = rows.reshape(devices, CAP, 640)
    rows = dot(pick, own_ref[:, QCOLS:ROW]).astype(BF16)
    answer_ref[:, :, QCOLS:ROW] = rows.reshape(devices, CAP, SIDE)


def prefix_kernel(q0, q1, q2, q3, kv_mine, kv_other, o0, o1, o2, o3):
    requests = q0.shape[0]
    rows = requests * SHARE
    step = 256
    chunks = [slice(c, c + step) for c in range(0, kv_mine.shape[0], step)]
    core = lax.rem(lax.axis_index("grp"), 2)
    lane = iota((rows, SIDE), 1)
    asked = (q0, q1, q2, q3)
    outs = (o0, o1, o2, o3)

    def attend(k_ref, v_ref):
        sums = jnp.zeros((rows, SIDE), F32)

        def score(h):
            heads = jnp.concatenate([q[:, h * HD : (h + 1) * HD] for q in asked], axis=0)
            kv = slice(h // GROUP * HD, (h // GROUP + 1) * HD)
            return [dot_t(heads, k_ref[c, kv]) * SCALE for c in chunks]

        def weigh(scores):
            top = jnp.max(functools.reduce(jnp.maximum, scores), axis=1, keepdims=True)
            weights = [jnp.exp(s - top) for s in scores]
            total = jnp.sum(functools.reduce(jnp.add, weights), axis=1, keepdims=True)
            return [w.astype(BF16) for w in weights], total, top + jnp.log(total)

        def mix(h, weights, total):
            kv = slice(h // GROUP * HD, (h // GROUP + 1) * HD)
            parts = [dot(w, v_ref[c, kv]) for c, w in zip(chunks, weights)]
            mixture = (functools.reduce(jnp.add, parts) / total).astype(BF16)
            for o, out in enumerate(outs):
                out[:, h * HD : (h + 1) * HD] = mixture[requests * o : requests * (o + 1)]

        scores, weighed = {0: score(0)}, {}
        for h in range(HEADS + 1):
            if h + 1 < HEADS:
                scores[h + 1] = score(h + 1)
            if h < HEADS:
                *weighed[h], log_sum = weigh(scores.pop(h))
                sums = jnp.where(lax.rem(lane, HEADS) == h, log_sum, sums)
            if h:
                mix(h - 1, *weighed.pop(h - 1))

        hi, mid, lo = three_parts(sums)
        side = jnp.where(lane < HEADS, hi, jnp.where(lane < 2 * HEADS, mid, lo)).astype(BF16)
        for o, out in enumerate(outs):
            out[:, BLOCK:] = side[requests * o : requests * (o + 1)]

    @pl.when(core == 0)
    def _():
        attend(kv_mine, kv_other)

    @pl.when(core == 1)
    def _():
        attend(kv_other, kv_mine)


def join_kernel(got_ref, own_ref, where_ref, *refs):
    *served, out_hbm, out_ref, sems = refs
    entries = where_ref.shape[0]
    requests = served[0].shape[0]
    cells = got_ref.shape[0] * CAP
    pool = own_ref.shape[0]
    lane = iota((entries, 128), 1)
    where = where_ref[:, 0:1]
    pick = jnp.where(where == lane.astype(F32), 1.0, 0.0).astype(BF16)
    far, near = pick[:, :cells], pick[:, cells : cells + pool]
    side = dot(far, got_ref[:, :, QCOLS:ROW].reshape(cells, SIDE)) + dot(near, own_ref[:, QCOLS:ROW])
    sums = side + pltpu.roll(side, SIDE - QH, 1) + pltpu.roll(side, SIDE - 2 * QH, 1)
    sums = jnp.where(where >= 0.0, sums, VERY_LOW)
    turn = my_turn()
    sent = []

    def bring(o):
        cols = pl.ds(pl.multiple_of((turn ^ o) * BLOCK, 128), BLOCK)
        got = got_ref[:, :, cols].reshape(cells, BLOCK)
        return dot(far, got) + dot(near, own_ref[:, cols])

    def shares(o):
        moved = pltpu.roll(sums, lax.rem(SIDE - (turn ^ o) * HEADS, SIDE), 1)
        pre = served[o][:, BLOCK:].astype(F32)
        pre = pre + pltpu.roll(pre, SIDE - HEADS, 1) + pltpu.roll(pre, SIDE - 2 * HEADS, 1)
        logs = [moved[requests * j : requests * (j + 1)] for j in range(MAXP)]
        top = functools.reduce(jnp.maximum, logs, pre)
        parts = [jnp.exp(x - top) for x in (*logs, pre)]
        total = functools.reduce(jnp.add, parts)
        return [x / total for x in parts]

    weights = [shares(o) for o in range(SHARE)]
    rows = bring(0)
    for o in range(SHARE):
        ahead = bring(o + 1) if o + 1 < SHARE else None
        *parts, part = weights[o]
        at = pl.multiple_of((turn ^ o) * BLOCK, 128)
        for h in range(HEADS):
            here = slice(h * HD, (h + 1) * HD)
            mixture = part[:, h : h + 1] * served[o][:, here].astype(F32)
            for j in range(MAXP):
                mixture = mixture + parts[j][:, h : h + 1] * rows[requests * j : requests * (j + 1), here]
            out_ref[:, pl.ds(pl.multiple_of(at + h * HD, 128), HD)] = mixture.astype(BF16)
        rows = ahead
        cols = pl.ds(at, BLOCK)
        sent += load((out_ref.at[:, cols],), (out_hbm.at[:, cols],), sems.at[pl.ds(o, 1)])
    for copy in sent:
        copy.wait()


def call(kernel, out_shape, flops, *args, in_hbm=(), out_hbm=(), scratch=(), room=24 << 20):
    args = [
        pltpu.with_memory_space_constraint(x, pltpu.HBM) if i in in_hbm else x
        for i, x in enumerate(args)
    ]
    specs = [
        [pl.BlockSpec(memory_space=pl.ANY if i in hbm else pltpu.VMEM) for i in range(n)]
        for n, hbm in ((len(args), in_hbm), (len(out_shape), out_hbm))
    ]
    return pl.pallas_call(
        kernel,
        out_shape=[jax.ShapeDtypeStruct(s, d) for s, d in out_shape],
        in_specs=specs[0],
        out_specs=specs[1],
        scratch_shapes=list(scratch),
        compiler_params=pltpu.CompilerParams(vmem_limit_bytes=room),
        cost_estimate=pl.CostEstimate(flops=flops, bytes_accessed=1 << 22, transcendentals=0),
    )(*args)


def like(x):
    return pltpu.VMEM(x.shape, x.dtype)


def semaphores(*shape):
    return pltpu.SemaphoreType.DMA(shape)


def route(queries, tables, lengths, places, prefix_keys, prefix_values, devices, pool):
    requests, depth = queries.shape[0], prefix_keys.shape[0]
    shape = (devices, CAP, ROW + depth // 4 // CAP * KV)
    args = (queries, tables, lengths, places)
    return call(
        functools.partial(route_kernel, pool),
        [(shape, BF16), ((requests * MAXP, 128), F32)],
        10**8,
        *args,
        prefix_keys,
        prefix_values,
        in_hbm=range(6),
        scratch=(
            *map(like, args),
            pltpu.VMEM((depth, KV), BF16),
            semaphores(5),
        ),
    )


def home(queries, where, pool):
    return call(
        home_kernel,
        [((pool, ROW), BF16)] + [((queries.shape[0], BLOCK), BF16)] * SHARE,
        10**8,
        queries,
        where,
        in_hbm=(0,),
        scratch=(like(queries), semaphores(1)),
    )


def pages(got, local, suffix_keys, suffix_values):
    suffix_keys = pltpu.with_memory_space_constraint(suffix_keys, pltpu.VMEM)
    shape = (got.shape[0], CAP, ROW)
    return call(
        pages_kernel,
        [(shape, BF16), (local.shape, BF16)],
        10**9,
        got,
        local,
        suffix_keys,
        suffix_values,
        in_hbm=(3,),
        scratch=(like(suffix_values), semaphores(CHUNKS)),
    )


def prefix(asked, kv_mine, kv_other):
    shape = (asked[0].shape[0], BLOCK + SIDE)
    return call(
        prefix_kernel, [(shape, BF16)] * SHARE, 10**9, *asked, kv_mine, kv_other
    )


def join(back, own, where, served):
    shape = (served[0].shape[0], QCOLS)
    (out,) = call(
        join_kernel,
        [(shape, BF16)],
        10**8,
        back,
        own,
        where,
        *served,
        out_hbm=(0,),
        scratch=(pltpu.VMEM(shape, BF16), semaphores(SHARE)),
    )
    return out


def body(
    queries, page_table, suffix_len, place, suffix_keys, suffix_values, prefix_keys, prefix_values
):
    pool = suffix_keys.shape[0]
    devices = lax.axis_size("blk")
    group = lax.axis_size("grp")
    lengths, places = suffix_len.reshape(1, -1), place.reshape(-1, 128)
    send, where = route(
        queries, page_table.T, lengths, places, prefix_keys, prefix_values, devices, pool
    )
    flip = lambda x, bits: lax.ppermute(x, "grp", [(i, i ^ bits) for i in range(group)])
    turned = lambda xs: [flip(x, 4 * o) if o else x for o, x in enumerate(xs)]
    exchange = lambda x: lax.all_to_all(x, "blk", split_axis=0, concat_axis=0, tiled=True)
    got = exchange(send)
    local, *asked = home(queries, where, pool)
    asked = turned(asked)
    local, *asked = lax.optimization_barrier((local, *asked))
    answer, own = pages(got, local, suffix_keys, suffix_values)
    back = exchange(answer)
    part, own = lax.optimization_barrier((got[:, :, ROW:], own))
    part = part.reshape(-1, KV)
    pairs = [(i, i ^ (devices // 2)) for i in range(devices)]
    both = [
        (g * devices + i, (g ^ 2) * devices + j) for g in range(group) for i, j in pairs
    ]
    around = [
        flip(part, 2), lax.ppermute(part, "blk", pairs), lax.ppermute(part, ("grp", "blk"), both)
    ]
    kv_mine = jnp.concatenate([part, *around], axis=0)
    served = prefix(asked, kv_mine, flip(kv_mine, 1))
    return join(back, own, where, turned(served))


def solution(mesh):
    return jax.shard_map(
        body,
        mesh=mesh,
        in_specs=(
            P(("grp", "blk"), None),
            P(("grp", "blk"), None),
            P(("grp", "blk")),
            P("grp"),
            P(("grp", "blk"), None, None),
            P(("grp", "blk"), None, None),
            P("blk", None),
            P("blk", None),
        ),
        out_specs=P(("grp", "blk"), None),
        check_vma=False,
    )
```

```python
import functools
import math

import jax
import jax.numpy as jnp
from jax import lax
from jax.experimental import pallas as pl
from jax.experimental.pallas import tpu as pltpu
from jax.sharding import PartitionSpec as P

QH = 40
KVH = 8
HD = 128
PAGE = 16
MAXP = 4
CAP = 2
GROUP = QH // KVH
QCOLS = QH * HD
SIDE = 128
ROW = QCOLS + SIDE
SHARE = 4
HEADS = QH // SHARE
BLOCK = HEADS * HD
KV = KVH // SHARE * HD
CHUNKS = 4
CHUNK = QCOLS // CHUNKS
TOKENS_AT = 64
SCALE = HD ** (-0.5)
SCALE_2 = SCALE * math.log2(math.e)
VERY_LOW = -1e30
F32 = jnp.float32
BF16 = jnp.bfloat16


def iota(shape, axis):
    return lax.broadcasted_iota(jnp.int32, shape, axis)


def dot(a, b):
    return lax.dot_general(a, b, (((1,), (0,)), ((), ())), preferred_element_type=F32)


def dot_t(a, b):
    return lax.dot_general(a, b, (((1,), (1,)), ((), ())), preferred_element_type=F32)


def three_parts(x):
    hi = x.astype(BF16).astype(F32)
    mid = (x - hi).astype(BF16).astype(F32)
    lo = (x - hi - mid).astype(BF16).astype(F32)
    return hi, mid, lo


def load(refs, scratch, sems):
    copies = [
        pltpu.make_async_copy(ref, buf, sems.at[i])
        for i, (ref, buf) in enumerate(zip(refs, scratch, strict=True))
    ]
    for copy in copies:
        copy.start()
    return copies


def my_turn():
    return lax.div(lax.axis_index("grp"), 4)


def route_kernel(
    pool, q_hbm, table_hbm, len_hbm, place_hbm, pk_hbm, pv_hbm, send_ref, where_ref,
    q_ref, table_ref, len_ref, place_ref, rows_ref, sems,
):
    requests = q_ref.shape[0]
    entries = requests * MAXP
    devices = send_ref.shape[0]
    cells = devices * CAP
    mine = lax.axis_index("blk")
    group = lax.axis_index("grp")
    turn = my_turn()
    kv_at = pl.ds(pl.multiple_of(turn * KV, KV), KV)

    def fetch_rows(source):
        return pltpu.make_async_copy(source.at[:, kv_at], rows_ref, sems.at[4])

    @pl.when(lax.rem(group, 2) == 0)
    def _():
        fetch_rows(pk_hbm).start()

    @pl.when(lax.rem(group, 2) == 1)
    def _():
        fetch_rows(pv_hbm).start()

    copies = load(
        (place_hbm, table_hbm, len_hbm, q_hbm), (place_ref, table_ref, len_ref, q_ref), sems
    )
    fetch_rows(pk_hbm).wait()
    depth = rows_ref.shape[0]
    shape = (cells, depth)
    cell = iota(shape, 0)
    each = depth // 4 // CAP
    first = depth // 2 * lax.rem(lax.div(group, 2), 2) + depth // 4 * lax.div(cell, cells // 2)
    for p in range(each):
        one = iota(shape, 1) == first + each * lax.rem(cell, CAP) + p
        rows = dot(jnp.where(one, 1.0, 0.0).astype(BF16), rows_ref[...]).astype(BF16)
        send_ref[:, :, ROW + KV * p : ROW + KV * (p + 1)] = rows.reshape(devices, CAP, KV)

    base = group * (devices * pool)
    square = iota((requests, requests), 0) == iota((requests, requests), 1)

    def column(row):
        row = jnp.broadcast_to(row, (requests, requests)).astype(F32)
        return jnp.sum(jnp.where(square, row, 0.0), axis=1, keepdims=True)

    for copy in copies[:3]:
        copy.wait()
    table = table_ref[...] - base
    page = jnp.concatenate([column(table[j : j + 1]) for j in range(MAXP)], axis=0)
    place = (place_ref[...] - base).astype(F32)
    lane = iota((entries, 128), 1).astype(F32)
    found = jnp.zeros((entries, 128), F32)
    for k in range(place.shape[0]):
        found = found + jnp.where(page == lane + 128.0 * k, place[k : k + 1, :], 0.0)
    physical = jnp.sum(found, axis=1, keepdims=True)
    holder = jnp.floor((physical + 0.5) * (1.0 / pool))
    slot = physical - holder * pool
    length = column(len_ref[...])
    tokens = jnp.concatenate(
        [jnp.clip(length - PAGE * j, 0.0, PAGE) for j in range(MAXP)], axis=0
    )
    used = tokens > 0.0
    at_home = holder == mine.astype(F32)
    remote = jnp.where(used & jnp.logical_not(at_home), 1.0, 0.0)
    member = jnp.where(holder == lane, remote, 0.0)
    below = jnp.where(iota((entries, entries), 1) < iota((entries, entries), 0), 1.0, 0.0)
    before = dot(below.astype(BF16), member.astype(BF16))
    rank = jnp.sum(before * member, axis=1, keepdims=True)
    where = jnp.where(remote > 0.0, holder * CAP + rank, cells + slot)
    where = jnp.where(used, where, -1.0)
    where_ref[...] = jnp.where(lane < TOKENS_AT, where, tokens)
    pick = jnp.where(where == lane, 1.0, 0.0).T[:cells]
    facts = jnp.where(lane == 0.0, slot, jnp.where(lane == 1.0, tokens, 0.0))
    side = dot(pick.astype(BF16), facts.astype(BF16)).astype(BF16)
    send_ref[:, :, QCOLS:ROW] = side.reshape(devices, CAP, SIDE)
    picked = over_entries(pick, requests)
    copies[3].wait()
    for c in range(CHUNKS):
        begin = c * CHUNK
        rows = dot(picked, q_ref[:, begin : begin + CHUNK]).astype(BF16)
        send_ref[:, :, begin : begin + CHUNK] = rows.reshape(devices, CAP, CHUNK)


def over_entries(pick, requests):
    parts = [pick[:, requests * j : requests * (j + 1)] for j in range(MAXP)]
    return functools.reduce(jnp.add, parts).astype(BF16)


def home_kernel(q_hbm, where_ref, local_ref, s0, s1, s2, s3, q_ref, sems):
    copies = load((q_hbm,), (q_ref,), sems)
    requests = q_ref.shape[0]
    entries = requests * MAXP
    pool = local_ref.shape[0]
    cells = CAP * lax.axis_size("blk")
    where, tokens = where_ref[:, 0:1], where_ref[:, TOKENS_AT : TOKENS_AT + 1]
    lane = iota((entries, 128), 1).astype(F32)
    pick = jnp.where(where == lane, 1.0, 0.0).T[cells : cells + pool]
    facts = jnp.where(lane == 0.0, where - cells, jnp.where(lane == 1.0, tokens, 0.0))
    local_ref[:, QCOLS:ROW] = dot(pick.astype(BF16), facts.astype(BF16)).astype(BF16)
    picked = over_entries(pick, requests)
    copies[0].wait()
    for c in range(CHUNKS):
        cols = slice(c * CHUNK, (c + 1) * CHUNK)
        local_ref[:, cols] = dot(picked, q_ref[:, cols]).astype(BF16)
    turn = my_turn()
    for o, ref in enumerate((s0, s1, s2, s3)):
        at = pl.multiple_of((turn ^ o) * BLOCK, BLOCK)
        ref[...] = q_ref[:, pl.ds(at, BLOCK)]


def pages_kernel(
    got_ref, local_ref, k_ref, v_hbm, answer_ref, own_ref, v_ref, chunk_sems,
):
    devices = got_ref.shape[0]
    cells = devices * CAP
    pool = k_ref.shape[0]
    step = 16
    pair = 2 * HD
    every = slice(None)
    chunks = []
    for c in range(CHUNKS):
        kv_at = (every, every, pl.ds(c * pair, pair))
        chunks.append(
            load(
                (v_hbm.at[kv_at],), (v_ref.at[kv_at],), chunk_sems.at[pl.ds(c, 1)]
            )
        )
    wide = (step, step * PAGE)
    column = iota(wide, 1)
    same = lax.div(column, PAGE) == iota(wide, 0)
    token = lax.rem(column, PAGE).astype(F32)
    side_lane = iota((step, SIDE), 1)
    lane = iota((cells, 128), 1).astype(F32)
    plain = got_ref[:, :, QCOLS:ROW].reshape(cells, SIDE)
    facts = plain.astype(F32)
    pick = jnp.where((facts[:, 0:1] == lane) & (facts[:, 1:2] > 0.0), 1.0, 0.0)
    fetch = pick.T[:pool].astype(BF16)
    pick = pick[:, :pool].astype(BF16)
    tokens = (dot(fetch, plain) + local_ref[:, QCOLS:ROW].astype(F32))[:, 1:2]
    sums = [jnp.zeros((step, SIDE), F32) for _ in range(pool // step)]
    masks = []
    for g in range(pool // step):
        bias = jnp.where(same & (token < tokens[step * g : step * (g + 1)]), 0.0, VERY_LOW)
        masks.append(jnp.concatenate([bias] * (2 * GROUP), axis=0))
    nothing = jnp.zeros((step * GROUP, HD), BF16)
    spans = [slice(step * g, step * (g + 1)) for g in range(pool // step)]

    def score(c, g, rows):
        span = spans[g]
        one, two = (
            jnp.concatenate(
                [rows[span, (GROUP * k + i) * HD : (GROUP * k + i + 1) * HD] for i in range(GROUP)],
                axis=0,
            )
            for k in range(2)
        )
        heads = jnp.concatenate(
            [jnp.concatenate([one, nothing], axis=1), jnp.concatenate([nothing, two], axis=1)], axis=0
        )
        keys = k_ref[span, :, c * pair : (c + 1) * pair].reshape(step * PAGE, pair)
        return dot_t(heads, keys) + masks[g]

    def weigh(scores):
        top = jnp.max(scores, axis=1, keepdims=True)
        weights = jnp.exp2((scores - top) * SCALE_2)
        total = jnp.sum(weights, axis=1, keepdims=True)
        return weights.astype(BF16), total, top * SCALE + jnp.log(total)

    def mix(c, g, weights, total, log_sum):
        span = spans[g]
        values = v_ref[span, :, c * pair : (c + 1) * pair].reshape(step * PAGE, pair)
        mixture = dot(weights, values) / total
        for i in range(2 * GROUP):
            here = slice(step * i, step * (i + 1))
            part = mixture[here, :HD] if i < GROUP else mixture[here, HD:]
            at = c * CHUNK + i * HD
            own_ref[span, at : at + HD] = part.astype(BF16)
            mine = lax.rem(side_lane, QH) == c * 2 * GROUP + i
            sums[g] = jnp.where(mine, log_sum[here], sums[g])

    def ask(c):
        cols = slice(c * CHUNK, (c + 1) * CHUNK)
        asked = got_ref[:, :, cols].reshape(cells, CHUNK)
        return (dot(fetch, asked) + local_ref[:, cols].astype(F32)).astype(BF16)

    steps = [(c, g) for c in range(CHUNKS) for g in range(len(spans))]
    rows = {c: ask(c) for c in range(CHUNKS)}
    scores = {s: score(*s, rows[s[0]]) for s in steps[:2]}
    weighed = {}
    for n, s in enumerate(steps + [None]):
        if n + 2 < len(steps):
            t = steps[n + 2]
            scores[t] = score(*t, rows[t[0]])
        if s is not None:
            weighed[s] = weigh(scores.pop(s))
        if n == 1:
            for copy in chunks[0] + chunks[1]:
                copy.wait()
        if n == 7:
            for copy in chunks[2] + chunks[3]:
                copy.wait()
        if n >= 1:
            mix(*steps[n - 1], *weighed.pop(steps[n - 1]))
    for g in range(pool // step):
        hi, mid, lo = three_parts(sums[g])
        side = jnp.where(side_lane < QH, hi, jnp.where(side_lane < 2 * QH, mid, lo))
        own_ref[step * g : step * (g + 1), QCOLS:ROW] = side.astype(BF16)
    for c in range(0, QCOLS, 640):
        cols = slice(c, c + 640)
        rows = dot(pick, own_ref[:, cols]).astype(BF16)
        answer_ref[:, :, cols] = rows.reshape(devices, CAP, 640)
    rows = dot(pick, own_ref[:, QCOLS:ROW]).astype(BF16)
    answer_ref[:, :, QCOLS:ROW] = rows.reshape(devices, CAP, SIDE)


def prefix_kernel(q0, q1, q2, q3, kv_mine, kv_other, o0, o1, o2, o3):
    requests = q0.shape[0]
    rows = requests * SHARE
    step = 256
    chunks = [slice(c, c + step) for c in range(0, kv_mine.shape[0], step)]
    core = lax.rem(lax.axis_index("grp"), 2)
    lane = iota((rows, SIDE), 1)
    asked = (q0, q1, q2, q3)
    outs = (o0, o1, o2, o3)

    def attend(k_ref, v_ref):
        sums = jnp.zeros((rows, SIDE), F32)

        def score(h):
            heads = jnp.concatenate([q[:, h * HD : (h + 1) * HD] for q in asked], axis=0)
            kv = slice(h // GROUP * HD, (h // GROUP + 1) * HD)
            return [dot_t(heads, k_ref[c, kv]) for c in chunks]

        def weigh(scores):
            top = jnp.max(functools.reduce(jnp.maximum, scores), axis=1, keepdims=True)
            weights = [jnp.exp2((s - top) * SCALE_2) for s in scores]
            total = jnp.sum(functools.reduce(jnp.add, weights), axis=1, keepdims=True)
            return [w.astype(BF16) for w in weights], total, top * SCALE + jnp.log(total)

        def mix(h, weights, total):
            kv = slice(h // GROUP * HD, (h // GROUP + 1) * HD)
            parts = [dot(w, v_ref[c, kv]) for c, w in zip(chunks, weights)]
            mixture = (functools.reduce(jnp.add, parts) / total).astype(BF16)
            for o, out in enumerate(outs):
                out[:, h * HD : (h + 1) * HD] = mixture[requests * o : requests * (o + 1)]

        scores, weighed = {0: score(0)}, {}
        for h in range(HEADS + 1):
            if h + 1 < HEADS:
                scores[h + 1] = score(h + 1)
            if h < HEADS:
                *weighed[h], log_sum = weigh(scores.pop(h))
                sums = jnp.where(lax.rem(lane, HEADS) == h, log_sum, sums)
            if h:
                mix(h - 1, *weighed.pop(h - 1))

        hi, mid, lo = three_parts(sums)
        side = jnp.where(lane < HEADS, hi, jnp.where(lane < 2 * HEADS, mid, lo)).astype(BF16)
        for o, out in enumerate(outs):
            out[:, BLOCK:] = side[requests * o : requests * (o + 1)]

    @pl.when(core == 0)
    def _():
        attend(kv_mine, kv_other)

    @pl.when(core == 1)
    def _():
        attend(kv_other, kv_mine)


def join_kernel(got_ref, own_ref, where_ref, *refs):
    *served, out_hbm, out_ref, sems = refs
    entries = where_ref.shape[0]
    requests = served[0].shape[0]
    cells = got_ref.shape[0] * CAP
    pool = own_ref.shape[0]
    lane = iota((entries, 128), 1)
    where = where_ref[:, 0:1]
    pick = jnp.where(where == lane.astype(F32), 1.0, 0.0).astype(BF16)
    far, near = pick[:, :cells], pick[:, cells : cells + pool]
    side = dot(far, got_ref[:, :, QCOLS:ROW].reshape(cells, SIDE)) + dot(near, own_ref[:, QCOLS:ROW])
    sums = side + pltpu.roll(side, SIDE - QH, 1) + pltpu.roll(side, SIDE - 2 * QH, 1)
    sums = jnp.where(where >= 0.0, sums, VERY_LOW)
    turn = my_turn()
    sent = []

    def bring(o):
        cols = pl.ds(pl.multiple_of((turn ^ o) * BLOCK, 128), BLOCK)
        got = got_ref[:, :, cols].reshape(cells, BLOCK)
        return dot(far, got) + dot(near, own_ref[:, cols])

    def shares(o):
        moved = pltpu.roll(sums, lax.rem(SIDE - (turn ^ o) * HEADS, SIDE), 1)
        pre = served[o][:, BLOCK:].astype(F32)
        pre = pre + pltpu.roll(pre, SIDE - HEADS, 1) + pltpu.roll(pre, SIDE - 2 * HEADS, 1)
        logs = [moved[requests * j : requests * (j + 1)] for j in range(MAXP)]
        top = functools.reduce(jnp.maximum, logs, pre)
        parts = [jnp.exp(x - top) for x in (*logs, pre)]
        total = functools.reduce(jnp.add, parts)
        return [x / total for x in parts]

    weights = [shares(o) for o in range(SHARE)]
    rows = bring(0)
    for o in range(SHARE):
        ahead = bring(o + 1) if o + 1 < SHARE else None
        *parts, part = weights[o]
        at = pl.multiple_of((turn ^ o) * BLOCK, 128)
        for h in range(HEADS):
            here = slice(h * HD, (h + 1) * HD)
            mixture = part[:, h : h + 1] * served[o][:, here].astype(F32)
            for j in range(MAXP):
                mixture = mixture + parts[j][:, h : h + 1] * rows[requests * j : requests * (j + 1), here]
            out_ref[:, pl.ds(pl.multiple_of(at + h * HD, 128), HD)] = mixture.astype(BF16)
        rows = ahead
        cols = pl.ds(at, BLOCK)
        sent += load((out_ref.at[:, cols],), (out_hbm.at[:, cols],), sems.at[pl.ds(o, 1)])
    for copy in sent:
        copy.wait()


def call(kernel, out_shape, flops, *args, in_hbm=(), out_hbm=(), scratch=(), room=24 << 20):
    args = [
        pltpu.with_memory_space_constraint(x, pltpu.HBM) if i in in_hbm else x
        for i, x in enumerate(args)
    ]
    specs = [
        [pl.BlockSpec(memory_space=pl.ANY if i in hbm else pltpu.VMEM) for i in range(n)]
        for n, hbm in ((len(args), in_hbm), (len(out_shape), out_hbm))
    ]
    return pl.pallas_call(
        kernel,
        out_shape=[jax.ShapeDtypeStruct(s, d) for s, d in out_shape],
        in_specs=specs[0],
        out_specs=specs[1],
        scratch_shapes=list(scratch),
        compiler_params=pltpu.CompilerParams(vmem_limit_bytes=room),
        cost_estimate=pl.CostEstimate(flops=flops, bytes_accessed=1 << 22, transcendentals=0),
    )(*args)


def like(x):
    return pltpu.VMEM(x.shape, x.dtype)


def semaphores(*shape):
    return pltpu.SemaphoreType.DMA(shape)


def route(queries, tables, lengths, places, prefix_keys, prefix_values, devices, pool):
    requests, depth = queries.shape[0], prefix_keys.shape[0]
    shape = (devices, CAP, ROW + depth // 4 // CAP * KV)
    args = (queries, tables, lengths, places)
    return call(
        functools.partial(route_kernel, pool),
        [(shape, BF16), ((requests * MAXP, 128), F32)],
        10**8,
        *args,
        prefix_keys,
        prefix_values,
        in_hbm=range(6),
        scratch=(
            *map(like, args),
            pltpu.VMEM((depth, KV), BF16),
            semaphores(5),
        ),
    )


def home(queries, where, pool):
    return call(
        home_kernel,
        [((pool, ROW), BF16)] + [((queries.shape[0], BLOCK), BF16)] * SHARE,
        10**8,
        queries,
        where,
        in_hbm=(0,),
        scratch=(like(queries), semaphores(1)),
    )


def pages(got, local, suffix_keys, suffix_values):
    suffix_keys = pltpu.with_memory_space_constraint(suffix_keys, pltpu.VMEM)
    shape = (got.shape[0], CAP, ROW)
    return call(
        pages_kernel,
        [(shape, BF16), (local.shape, BF16)],
        10**9,
        got,
        local,
        suffix_keys,
        suffix_values,
        in_hbm=(3,),
        scratch=(like(suffix_values), semaphores(CHUNKS)),
    )


def prefix(asked, kv_mine, kv_other):
    shape = (asked[0].shape[0], BLOCK + SIDE)
    return call(
        prefix_kernel, [(shape, BF16)] * SHARE, 10**9, *asked, kv_mine, kv_other
    )


def join(back, own, where, served):
    shape = (served[0].shape[0], QCOLS)
    (out,) = call(
        join_kernel,
        [(shape, BF16)],
        10**8,
        back,
        own,
        where,
        *served,
        out_hbm=(0,),
        scratch=(pltpu.VMEM(shape, BF16), semaphores(SHARE)),
    )
    return out


def body(
    queries, page_table, suffix_len, place, suffix_keys, suffix_values, prefix_keys, prefix_values
):
    pool = suffix_keys.shape[0]
    devices = lax.axis_size("blk")
    group = lax.axis_size("grp")
    lengths, places = suffix_len.reshape(1, -1), place.reshape(-1, 128)
    send, where = route(
        queries, page_table.T, lengths, places, prefix_keys, prefix_values, devices, pool
    )
    flip = lambda x, bits: lax.ppermute(x, "grp", [(i, i ^ bits) for i in range(group)])
    turned = lambda xs: [flip(x, 4 * o) if o else x for o, x in enumerate(xs)]
    exchange = lambda x: lax.all_to_all(x, "blk", split_axis=0, concat_axis=0, tiled=True)
    got = exchange(send)
    local, *asked = home(queries, where, pool)
    asked = turned(asked)
    local, *asked = lax.optimization_barrier((local, *asked))
    answer, own = pages(got, local, suffix_keys, suffix_values)
    back = exchange(answer)
    part, own = lax.optimization_barrier((got[:, :, ROW:], own))
    part = part.reshape(-1, KV)
    pairs = [(i, i ^ (devices // 2)) for i in range(devices)]
    both = [
        (g * devices + i, (g ^ 2) * devices + j) for g in range(group) for i, j in pairs
    ]
    around = [
        flip(part, 2), lax.ppermute(part, "blk", pairs), lax.ppermute(part, ("grp", "blk"), both)
    ]
    kv_mine = jnp.concatenate([part, *around], axis=0)
    served = prefix(asked, kv_mine, flip(kv_mine, 1))
    return join(back, own, where, turned(served))


def solution(mesh):
    return jax.shard_map(
        body,
        mesh=mesh,
        in_specs=(
            P(("grp", "blk"), None),
            P(("grp", "blk"), None),
            P(("grp", "blk")),
            P("grp"),
            P(("grp", "blk"), None, None),
            P(("grp", "blk"), None, None),
            P("blk", None),
            P("blk", None),
        ),
        out_specs=P(("grp", "blk"), None),
        check_vma=False,
    )
```

```python
import functools
import math

import jax
import jax.numpy as jnp
from jax import lax
from jax.experimental import pallas as pl
from jax.experimental.pallas import tpu as pltpu
from jax.sharding import PartitionSpec as P

QH = 40
KVH = 8
HD = 128
PAGE = 16
MAXP = 4
CAP = 2
GROUP = QH // KVH
QCOLS = QH * HD
SIDE = 128
ROW = QCOLS + SIDE
SHARE = 4
HEADS = QH // SHARE
BLOCK = HEADS * HD
KV = KVH // SHARE * HD
CHUNKS = 4
CHUNK = QCOLS // CHUNKS
TOKENS_AT = 64
SCALE = HD ** (-0.5)
SCALE_2 = SCALE * math.log2(math.e)
VERY_LOW = -1e30
F32 = jnp.float32
BF16 = jnp.bfloat16


def iota(shape, axis):
    return lax.broadcasted_iota(jnp.int32, shape, axis)


def dot(a, b):
    return lax.dot_general(a, b, (((1,), (0,)), ((), ())), preferred_element_type=F32)


def dot_t(a, b):
    return lax.dot_general(a, b, (((1,), (1,)), ((), ())), preferred_element_type=F32)


def three_parts(x):
    hi = x.astype(BF16).astype(F32)
    mid = (x - hi).astype(BF16).astype(F32)
    lo = (x - hi - mid).astype(BF16).astype(F32)
    return hi, mid, lo


def load(refs, scratch, sems):
    copies = [
        pltpu.make_async_copy(ref, buf, sems.at[i])
        for i, (ref, buf) in enumerate(zip(refs, scratch, strict=True))
    ]
    for copy in copies:
        copy.start()
    return copies


def my_turn():
    return lax.div(lax.axis_index("grp"), 4)


def route_kernel(
    pool, q_hbm, table_hbm, len_hbm, place_hbm, pk_hbm, pv_hbm, send_ref, where_ref,
    q_ref, table_ref, len_ref, place_ref, rows_ref, sems,
):
    requests = q_ref.shape[0]
    entries = requests * MAXP
    devices = send_ref.shape[0]
    cells = devices * CAP
    mine = lax.axis_index("blk")
    group = lax.axis_index("grp")
    turn = my_turn()
    kv_at = pl.ds(pl.multiple_of(turn * KV, KV), KV)

    def fetch_rows(source):
        return pltpu.make_async_copy(source.at[:, kv_at], rows_ref, sems.at[4])

    @pl.when(lax.rem(group, 2) == 0)
    def _():
        fetch_rows(pk_hbm).start()

    @pl.when(lax.rem(group, 2) == 1)
    def _():
        fetch_rows(pv_hbm).start()

    copies = load(
        (place_hbm, table_hbm, len_hbm, q_hbm), (place_ref, table_ref, len_ref, q_ref), sems
    )
    fetch_rows(pk_hbm).wait()
    depth = rows_ref.shape[0]
    shape = (cells, depth)
    cell = iota(shape, 0)
    each = depth // 4 // CAP
    first = depth // 2 * lax.rem(lax.div(group, 2), 2) + depth // 4 * (1 - lax.div(cell, cells // 2))
    for p in range(each):
        one = iota(shape, 1) == first + each * lax.rem(cell, CAP) + p
        rows = dot(jnp.where(one, 1.0, 0.0).astype(BF16), rows_ref[...]).astype(BF16)
        send_ref[:, :, ROW + KV * p : ROW + KV * (p + 1)] = rows.reshape(devices, CAP, KV)

    base = group * (devices * pool)
    square = iota((requests, requests), 0) == iota((requests, requests), 1)

    def column(row):
        row = jnp.broadcast_to(row, (requests, requests)).astype(F32)
        return jnp.sum(jnp.where(square, row, 0.0), axis=1, keepdims=True)

    for copy in copies[:3]:
        copy.wait()
    table = table_ref[...] - base
    page = jnp.concatenate([column(table[j : j + 1]) for j in range(MAXP)], axis=0)
    place = (place_ref[...] - base).astype(F32)
    lane = iota((entries, 128), 1).astype(F32)
    found = jnp.zeros((entries, 128), F32)
    for k in range(place.shape[0]):
        found = found + jnp.where(page == lane + 128.0 * k, place[k : k + 1, :], 0.0)
    physical = jnp.sum(found, axis=1, keepdims=True)
    holder = jnp.floor((physical + 0.5) * (1.0 / pool))
    slot = physical - holder * pool
    length = column(len_ref[...])
    tokens = jnp.concatenate(
        [jnp.clip(length - PAGE * j, 0.0, PAGE) for j in range(MAXP)], axis=0
    )
    used = tokens > 0.0
    at_home = holder == mine.astype(F32)
    remote = jnp.where(used & jnp.logical_not(at_home), 1.0, 0.0)
    member = jnp.where(holder == lane, remote, 0.0)
    below = jnp.where(iota((entries, entries), 1) < iota((entries, entries), 0), 1.0, 0.0)
    before = dot(below.astype(BF16), member.astype(BF16))
    rank = jnp.sum(before * member, axis=1, keepdims=True)
    where = jnp.where(remote > 0.0, (devices - 1 - holder) * CAP + rank, cells + slot)
    where = jnp.where(used, where, -1.0)
    where_ref[...] = jnp.where(lane < TOKENS_AT, where, tokens)
    pick = jnp.where(where == lane, 1.0, 0.0).T[:cells]
    facts = jnp.where(lane == 0.0, slot, jnp.where(lane == 1.0, tokens, 0.0))
    side = dot(pick.astype(BF16), facts.astype(BF16)).astype(BF16)
    send_ref[:, :, QCOLS:ROW] = side.reshape(devices, CAP, SIDE)
    picked = over_entries(pick, requests)
    copies[3].wait()
    for c in range(CHUNKS):
        begin = c * CHUNK
        rows = dot(picked, q_ref[:, begin : begin + CHUNK]).astype(BF16)
        send_ref[:, :, begin : begin + CHUNK] = rows.reshape(devices, CAP, CHUNK)


def over_entries(pick, requests):
    parts = [pick[:, requests * j : requests * (j + 1)] for j in range(MAXP)]
    return functools.reduce(jnp.add, parts).astype(BF16)


def home_kernel(q_hbm, where_ref, local_ref, s0, s1, s2, s3, q_ref, sems):
    copies = load((q_hbm,), (q_ref,), sems)
    requests = q_ref.shape[0]
    entries = requests * MAXP
    pool = local_ref.shape[0]
    cells = CAP * lax.axis_size("blk")
    where, tokens = where_ref[:, 0:1], where_ref[:, TOKENS_AT : TOKENS_AT + 1]
    lane = iota((entries, 128), 1).astype(F32)
    pick = jnp.where(where == lane, 1.0, 0.0).T[cells : cells + pool]
    facts = jnp.where(lane == 0.0, where - cells, jnp.where(lane == 1.0, tokens, 0.0))
    local_ref[:, QCOLS:ROW] = dot(pick.astype(BF16), facts.astype(BF16)).astype(BF16)
    picked = over_entries(pick, requests)
    copies[0].wait()
    for c in range(CHUNKS):
        cols = slice(c * CHUNK, (c + 1) * CHUNK)
        local_ref[:, cols] = dot(picked, q_ref[:, cols]).astype(BF16)
    turn = my_turn()
    for o, ref in enumerate((s0, s1, s2, s3)):
        at = pl.multiple_of((turn ^ o) * BLOCK, BLOCK)
        ref[...] = q_ref[:, pl.ds(at, BLOCK)]


def pages_kernel(
    got_ref, local_ref, k_ref, v_hbm, answer_ref, own_ref, v_ref, chunk_sems,
):
    devices = got_ref.shape[0]
    cells = devices * CAP
    pool = k_ref.shape[0]
    step = 16
    pair = 2 * HD
    every = slice(None)
    chunks = []
    for c in range(CHUNKS):
        kv_at = (every, every, pl.ds(c * pair, pair))
        chunks.append(
            load(
                (v_hbm.at[kv_at],), (v_ref.at[kv_at],), chunk_sems.at[pl.ds(c, 1)]
            )
        )
    wide = (step, step * PAGE)
    column = iota(wide, 1)
    same = lax.div(column, PAGE) == iota(wide, 0)
    token = lax.rem(column, PAGE).astype(F32)
    side_lane = iota((step, SIDE), 1)
    lane = iota((cells, 128), 1).astype(F32)
    plain = got_ref[:, :, QCOLS:ROW].reshape(cells, SIDE)
    facts = plain.astype(F32)
    pick = jnp.where((facts[:, 0:1] == lane) & (facts[:, 1:2] > 0.0), 1.0, 0.0)
    fetch = pick.T[:pool].astype(BF16)
    pick = pick[:, :pool].astype(BF16)
    tokens = (dot(fetch, plain) + local_ref[:, QCOLS:ROW].astype(F32))[:, 1:2]
    sums = [jnp.zeros((step, SIDE), F32) for _ in range(pool // step)]
    masks = []
    for g in range(pool // step):
        bias = jnp.where(same & (token < tokens[step * g : step * (g + 1)]), 0.0, VERY_LOW)
        masks.append(jnp.concatenate([bias] * (2 * GROUP), axis=0))
    nothing = jnp.zeros((step * GROUP, HD), BF16)
    spans = [slice(step * g, step * (g + 1)) for g in range(pool // step)]

    def score(c, g, rows):
        span = spans[g]
        one, two = (
            jnp.concatenate(
                [rows[span, (GROUP * k + i) * HD : (GROUP * k + i + 1) * HD] for i in range(GROUP)],
                axis=0,
            )
            for k in range(2)
        )
        heads = jnp.concatenate(
            [jnp.concatenate([one, nothing], axis=1), jnp.concatenate([nothing, two], axis=1)], axis=0
        )
        keys = k_ref[span, :, c * pair : (c + 1) * pair].reshape(step * PAGE, pair)
        return dot_t(heads, keys) + masks[g]

    def weigh(scores):
        top = jnp.max(scores, axis=1, keepdims=True)
        weights = jnp.exp2((scores - top) * SCALE_2)
        total = jnp.sum(weights, axis=1, keepdims=True)
        return weights.astype(BF16), total, top * SCALE + jnp.log(total)

    def mix(c, g, weights, total, log_sum):
        span = spans[g]
        values = v_ref[span, :, c * pair : (c + 1) * pair].reshape(step * PAGE, pair)
        mixture = dot(weights, values) / total
        for i in range(2 * GROUP):
            here = slice(step * i, step * (i + 1))
            part = mixture[here, :HD] if i < GROUP else mixture[here, HD:]
            at = c * CHUNK + i * HD
            own_ref[span, at : at + HD] = part.astype(BF16)
            mine = lax.rem(side_lane, QH) == c * 2 * GROUP + i
            sums[g] = jnp.where(mine, log_sum[here], sums[g])

    def ask(c):
        cols = slice(c * CHUNK, (c + 1) * CHUNK)
        asked = got_ref[:, :, cols].reshape(cells, CHUNK)
        return (dot(fetch, asked) + local_ref[:, cols].astype(F32)).astype(BF16)

    steps = [(c, g) for c in range(CHUNKS) for g in range(len(spans))]
    rows = {c: ask(c) for c in range(CHUNKS)}
    scores = {s: score(*s, rows[s[0]]) for s in steps[:2]}
    weighed = {}
    for n, s in enumerate(steps + [None]):
        if n + 2 < len(steps):
            t = steps[n + 2]
            scores[t] = score(*t, rows[t[0]])
        if s is not None:
            weighed[s] = weigh(scores.pop(s))
        if n == 1:
            for copy in chunks[0] + chunks[1]:
                copy.wait()
        if n == 7:
            for copy in chunks[2] + chunks[3]:
                copy.wait()
        if n >= 1:
            mix(*steps[n - 1], *weighed.pop(steps[n - 1]))
    for g in range(pool // step):
        hi, mid, lo = three_parts(sums[g])
        side = jnp.where(side_lane < QH, hi, jnp.where(side_lane < 2 * QH, mid, lo))
        own_ref[step * g : step * (g + 1), QCOLS:ROW] = side.astype(BF16)
    for c in range(0, QCOLS, 640):
        cols = slice(c, c + 640)
        rows = dot(pick, own_ref[:, cols]).astype(BF16)
        answer_ref[:, :, cols] = rows.reshape(devices, CAP, 640)
    rows = dot(pick, own_ref[:, QCOLS:ROW]).astype(BF16)
    answer_ref[:, :, QCOLS:ROW] = rows.reshape(devices, CAP, SIDE)


def prefix_kernel(q0, q1, q2, q3, kv_mine, kv_other, o0, o1, o2, o3):
    requests = q0.shape[0]
    rows = requests * SHARE
    step = 256
    chunks = [slice(c, c + step) for c in range(0, kv_mine.shape[0], step)]
    core = lax.rem(lax.axis_index("grp"), 2)
    lane = iota((rows, SIDE), 1)
    asked = (q0, q1, q2, q3)
    outs = (o0, o1, o2, o3)

    def attend(k_ref, v_ref):
        sums = jnp.zeros((rows, SIDE), F32)

        def score(h):
            heads = jnp.concatenate([q[:, h * HD : (h + 1) * HD] for q in asked], axis=0)
            kv = slice(h // GROUP * HD, (h // GROUP + 1) * HD)
            return [dot_t(heads, k_ref[c, kv]) for c in chunks]

        def weigh(scores):
            top = jnp.max(functools.reduce(jnp.maximum, scores), axis=1, keepdims=True)
            weights = [jnp.exp2((s - top) * SCALE_2) for s in scores]
            total = jnp.sum(functools.reduce(jnp.add, weights), axis=1, keepdims=True)
            return [w.astype(BF16) for w in weights], total, top * SCALE + jnp.log(total)

        def mix(h, weights, total):
            kv = slice(h // GROUP * HD, (h // GROUP + 1) * HD)
            parts = [dot(w, v_ref[c, kv]) for c, w in zip(chunks, weights)]
            mixture = (functools.reduce(jnp.add, parts) / total).astype(BF16)
            for o, out in enumerate(outs):
                out[:, h * HD : (h + 1) * HD] = mixture[requests * o : requests * (o + 1)]

        scores, weighed = {0: score(0)}, {}
        for h in range(HEADS + 1):
            if h + 1 < HEADS:
                scores[h + 1] = score(h + 1)
            if h < HEADS:
                *weighed[h], log_sum = weigh(scores.pop(h))
                sums = jnp.where(lax.rem(lane, HEADS) == h, log_sum, sums)
            if h:
                mix(h - 1, *weighed.pop(h - 1))

        hi, mid, lo = three_parts(sums)
        side = jnp.where(lane < HEADS, hi, jnp.where(lane < 2 * HEADS, mid, lo)).astype(BF16)
        for o, out in enumerate(outs):
            out[:, BLOCK:] = side[requests * o : requests * (o + 1)]

    @pl.when(core == 0)
    def _():
        attend(kv_mine, kv_other)

    @pl.when(core == 1)
    def _():
        attend(kv_other, kv_mine)


def join_kernel(got_ref, own_ref, where_ref, *refs):
    *served, out_hbm, out_ref, sems = refs
    entries = where_ref.shape[0]
    requests = served[0].shape[0]
    cells = got_ref.shape[0] * CAP
    pool = own_ref.shape[0]
    lane = iota((entries, 128), 1)
    where = where_ref[:, 0:1]
    pick = jnp.where(where == lane.astype(F32), 1.0, 0.0).astype(BF16)
    far, near = pick[:, :cells], pick[:, cells : cells + pool]
    side = dot(far, got_ref[:, :, QCOLS:ROW].reshape(cells, SIDE)) + dot(near, own_ref[:, QCOLS:ROW])
    sums = side + pltpu.roll(side, SIDE - QH, 1) + pltpu.roll(side, SIDE - 2 * QH, 1)
    sums = jnp.where(where >= 0.0, sums, VERY_LOW)
    turn = my_turn()
    sent = []

    def bring(o):
        cols = pl.ds(pl.multiple_of((turn ^ o) * BLOCK, 128), BLOCK)
        got = got_ref[:, :, cols].reshape(cells, BLOCK)
        return dot(far, got) + dot(near, own_ref[:, cols])

    def shares(o):
        moved = pltpu.roll(sums, lax.rem(SIDE - (turn ^ o) * HEADS, SIDE), 1)
        pre = served[o][:, BLOCK:].astype(F32)
        pre = pre + pltpu.roll(pre, SIDE - HEADS, 1) + pltpu.roll(pre, SIDE - 2 * HEADS, 1)
        logs = [moved[requests * j : requests * (j + 1)] for j in range(MAXP)]
        top = functools.reduce(jnp.maximum, logs, pre)
        parts = [jnp.exp(x - top) for x in (*logs, pre)]
        total = functools.reduce(jnp.add, parts)
        return [x / total for x in parts]

    weights = [shares(o) for o in range(SHARE)]
    rows = bring(0)
    for o in range(SHARE):
        ahead = bring(o + 1) if o + 1 < SHARE else None
        *parts, part = weights[o]
        at = pl.multiple_of((turn ^ o) * BLOCK, 128)
        for h in range(HEADS):
            here = slice(h * HD, (h + 1) * HD)
            mixture = part[:, h : h + 1] * served[o][:, here].astype(F32)
            for j in range(MAXP):
                mixture = mixture + parts[j][:, h : h + 1] * rows[requests * j : requests * (j + 1), here]
            out_ref[:, pl.ds(pl.multiple_of(at + h * HD, 128), HD)] = mixture.astype(BF16)
        rows = ahead
        cols = pl.ds(at, BLOCK)
        sent += load((out_ref.at[:, cols],), (out_hbm.at[:, cols],), sems.at[pl.ds(o, 1)])
    for copy in sent:
        copy.wait()


def call(kernel, out_shape, flops, *args, in_hbm=(), out_hbm=(), scratch=(), room=24 << 20):
    args = [
        pltpu.with_memory_space_constraint(x, pltpu.HBM) if i in in_hbm else x
        for i, x in enumerate(args)
    ]
    specs = [
        [pl.BlockSpec(memory_space=pl.ANY if i in hbm else pltpu.VMEM) for i in range(n)]
        for n, hbm in ((len(args), in_hbm), (len(out_shape), out_hbm))
    ]
    return pl.pallas_call(
        kernel,
        out_shape=[jax.ShapeDtypeStruct(s, d) for s, d in out_shape],
        in_specs=specs[0],
        out_specs=specs[1],
        scratch_shapes=list(scratch),
        compiler_params=pltpu.CompilerParams(vmem_limit_bytes=room),
        cost_estimate=pl.CostEstimate(flops=flops, bytes_accessed=1 << 22, transcendentals=0),
    )(*args)


def like(x):
    return pltpu.VMEM(x.shape, x.dtype)


def semaphores(*shape):
    return pltpu.SemaphoreType.DMA(shape)


def route(queries, tables, lengths, places, prefix_keys, prefix_values, devices, pool):
    requests, depth = queries.shape[0], prefix_keys.shape[0]
    shape = (devices, CAP, ROW + depth // 4 // CAP * KV)
    args = (queries, tables, lengths, places)
    return call(
        functools.partial(route_kernel, pool),
        [(shape, BF16), ((requests * MAXP, 128), F32)],
        10**8,
        *args,
        prefix_keys,
        prefix_values,
        in_hbm=range(6),
        scratch=(
            *map(like, args),
            pltpu.VMEM((depth, KV), BF16),
            semaphores(5),
        ),
    )


def home(queries, where, pool):
    return call(
        home_kernel,
        [((pool, ROW), BF16)] + [((queries.shape[0], BLOCK), BF16)] * SHARE,
        10**8,
        queries,
        where,
        in_hbm=(0,),
        scratch=(like(queries), semaphores(1)),
    )


def pages(got, local, suffix_keys, suffix_values):
    suffix_keys = pltpu.with_memory_space_constraint(suffix_keys, pltpu.VMEM)
    shape = (got.shape[0], CAP, ROW)
    return call(
        pages_kernel,
        [(shape, BF16), (local.shape, BF16)],
        10**9,
        got,
        local,
        suffix_keys,
        suffix_values,
        in_hbm=(3,),
        scratch=(like(suffix_values), semaphores(CHUNKS)),
    )


def prefix(asked, kv_mine, kv_other):
    shape = (asked[0].shape[0], BLOCK + SIDE)
    return call(
        prefix_kernel, [(shape, BF16)] * SHARE, 10**9, *asked, kv_mine, kv_other
    )


def join(back, own, where, served):
    shape = (served[0].shape[0], QCOLS)
    (out,) = call(
        join_kernel,
        [(shape, BF16)],
        10**8,
        back,
        own,
        where,
        *served,
        out_hbm=(0,),
        scratch=(pltpu.VMEM(shape, BF16), semaphores(SHARE)),
    )
    return out


def body(
    queries, page_table, suffix_len, place, suffix_keys, suffix_values, prefix_keys, prefix_values
):
    pool = suffix_keys.shape[0]
    devices = lax.axis_size("blk")
    group = lax.axis_size("grp")
    lengths, places = suffix_len.reshape(1, -1), place.reshape(-1, 128)
    send, where = route(
        queries, page_table.T, lengths, places, prefix_keys, prefix_values, devices, pool
    )
    flip = lambda x, bits: lax.ppermute(x, "grp", [(i, i ^ bits) for i in range(group)])
    turned = lambda xs: [flip(x, 4 * o) if o else x for o, x in enumerate(xs)]
    descending = [list(range(devices))[::-1]]
    exchange = lambda x: lax.all_to_all(
        x, "blk", split_axis=0, concat_axis=0, tiled=True, axis_index_groups=descending
    )
    got = exchange(send)
    local, *asked = home(queries, where, pool)
    asked = turned(asked)
    local, *asked = lax.optimization_barrier((local, *asked))
    answer, own = pages(got, local, suffix_keys, suffix_values)
    back = exchange(answer)
    part, own = lax.optimization_barrier((got[:, :, ROW:], own))
    part = part.reshape(-1, KV)
    pairs = [(i, i ^ (devices // 2)) for i in range(devices)]
    both = [
        (g * devices + i, (g ^ 2) * devices + j) for g in range(group) for i, j in pairs
    ]
    around = [
        flip(part, 2), lax.ppermute(part, "blk", pairs), lax.ppermute(part, ("grp", "blk"), both)
    ]
    kv_mine = jnp.concatenate([part, *around], axis=0)
    served = prefix(asked, kv_mine, flip(kv_mine, 1))
    return join(back, own, where, turned(served))


def solution(mesh):
    return jax.shard_map(
        body,
        mesh=mesh,
        in_specs=(
            P(("grp", "blk"), None),
            P(("grp", "blk"), None),
            P(("grp", "blk")),
            P("grp"),
            P(("grp", "blk"), None, None),
            P(("grp", "blk"), None, None),
            P("blk", None),
            P("blk", None),
        ),
        out_specs=P(("grp", "blk"), None),
        check_vma=False,
    )
```

```python
import functools
import math

import jax
import jax.numpy as jnp
from jax import lax
from jax.experimental import pallas as pl
from jax.experimental.pallas import tpu as pltpu
from jax.sharding import PartitionSpec as P

QH = 40
KVH = 8
HD = 128
PAGE = 16
MAXP = 4
CAP = 2
GROUP = QH // KVH
QCOLS = QH * HD
SIDE = 128
ROW = QCOLS + SIDE
SHARE = 4
HEADS = QH // SHARE
BLOCK = HEADS * HD
KV = KVH // SHARE * HD
CHUNKS = 4
CHUNK = QCOLS // CHUNKS
TOKENS_AT = 64
SCALE = HD ** (-0.5)
SCALE_2 = SCALE * math.log2(math.e)
VERY_LOW = -1e30
F32 = jnp.float32
BF16 = jnp.bfloat16


def iota(shape, axis):
    return lax.broadcasted_iota(jnp.int32, shape, axis)


def dot(a, b):
    return lax.dot_general(a, b, (((1,), (0,)), ((), ())), preferred_element_type=F32)


def dot_t(a, b):
    return lax.dot_general(a, b, (((1,), (1,)), ((), ())), preferred_element_type=F32)


def three_parts(x):
    hi = x.astype(BF16).astype(F32)
    mid = (x - hi).astype(BF16).astype(F32)
    lo = (x - hi - mid).astype(BF16).astype(F32)
    return hi, mid, lo


def load(refs, scratch, sems):
    copies = [
        pltpu.make_async_copy(ref, buf, sems.at[i])
        for i, (ref, buf) in enumerate(zip(refs, scratch, strict=True))
    ]
    for copy in copies:
        copy.start()
    return copies


def my_turn():
    return lax.div(lax.axis_index("grp"), 4)


def route_kernel(
    pool, q_hbm, table_hbm, len_hbm, place_hbm, pk_hbm, pv_hbm, send_ref, where_ref,
    q_ref, table_ref, len_ref, place_ref, rows_ref, sems,
):
    requests = q_ref.shape[0]
    entries = requests * MAXP
    devices = send_ref.shape[0]
    cells = devices * CAP
    mine = lax.axis_index("blk")
    group = lax.axis_index("grp")
    turn = my_turn()
    kv_at = pl.ds(pl.multiple_of(turn * KV, KV), KV)

    def fetch_rows(source):
        return pltpu.make_async_copy(source.at[:, kv_at], rows_ref, sems.at[4])

    @pl.when(lax.rem(group, 2) == 0)
    def _():
        fetch_rows(pk_hbm).start()

    @pl.when(lax.rem(group, 2) == 1)
    def _():
        fetch_rows(pv_hbm).start()

    copies = load(
        (place_hbm, table_hbm, len_hbm, q_hbm), (place_ref, table_ref, len_ref, q_ref), sems
    )
    fetch_rows(pk_hbm).wait()
    depth = rows_ref.shape[0]
    shape = (cells, depth)
    cell = iota(shape, 0)
    each = depth // 4 // CAP
    first = depth // 2 * lax.rem(lax.div(group, 2), 2) + depth // 4 * (1 - lax.div(cell, cells // 2))
    for p in range(each):
        one = iota(shape, 1) == first + each * lax.rem(cell, CAP) + p
        rows = dot(jnp.where(one, 1.0, 0.0).astype(BF16), rows_ref[...]).astype(BF16)
        send_ref[:, :, ROW + KV * p : ROW + KV * (p + 1)] = rows.reshape(devices, CAP, KV)

    base = group * (devices * pool)
    square = iota((requests, requests), 0) == iota((requests, requests), 1)

    def column(row):
        row = jnp.broadcast_to(row, (requests, requests)).astype(F32)
        return jnp.sum(jnp.where(square, row, 0.0), axis=1, keepdims=True)

    for copy in copies[:3]:
        copy.wait()
    table = table_ref[...] - base
    page = jnp.concatenate([column(table[j : j + 1]) for j in range(MAXP)], axis=0)
    place = (place_ref[...] - base).astype(F32)
    lane = iota((entries, 128), 1).astype(F32)
    found = jnp.zeros((entries, 128), F32)
    for k in range(place.shape[0]):
        found = found + jnp.where(page == lane + 128.0 * k, place[k : k + 1, :], 0.0)
    physical = jnp.sum(found, axis=1, keepdims=True)
    holder = jnp.floor((physical + 0.5) * (1.0 / pool))
    slot = physical - holder * pool
    length = column(len_ref[...])
    tokens = jnp.concatenate(
        [jnp.clip(length - PAGE * j, 0.0, PAGE) for j in range(MAXP)], axis=0
    )
    used = tokens > 0.0
    at_home = holder == mine.astype(F32)
    remote = jnp.where(used & jnp.logical_not(at_home), 1.0, 0.0)
    member = jnp.where(holder == lane, remote, 0.0)
    below = jnp.where(iota((entries, entries), 1) < iota((entries, entries), 0), 1.0, 0.0)
    before = dot(below.astype(BF16), member.astype(BF16))
    rank = jnp.sum(before * member, axis=1, keepdims=True)
    where = jnp.where(remote > 0.0, (devices - 1 - holder) * CAP + rank, cells + slot)
    where = jnp.where(used, where, -1.0)
    where_ref[...] = jnp.where(lane < TOKENS_AT, where, tokens)
    pick = jnp.where(where == lane, 1.0, 0.0).T[:cells]
    facts = jnp.where(lane == 0.0, slot, jnp.where(lane == 1.0, tokens, 0.0))
    side = dot(pick.astype(BF16), facts.astype(BF16)).astype(BF16)
    send_ref[:, :, QCOLS:ROW] = side.reshape(devices, CAP, SIDE)
    picked = over_entries(pick, requests)
    copies[3].wait()
    for c in range(CHUNKS):
        begin = c * CHUNK
        rows = dot(picked, q_ref[:, begin : begin + CHUNK]).astype(BF16)
        send_ref[:, :, begin : begin + CHUNK] = rows.reshape(devices, CAP, CHUNK)


def over_entries(pick, requests):
    parts = [pick[:, requests * j : requests * (j + 1)] for j in range(MAXP)]
    return functools.reduce(jnp.add, parts).astype(BF16)


def home_kernel(q_hbm, where_ref, local_ref, s0, s1, s2, s3, q_ref, sems):
    copies = load((q_hbm,), (q_ref,), sems)
    requests = q_ref.shape[0]
    entries = requests * MAXP
    pool = local_ref.shape[0]
    cells = CAP * lax.axis_size("blk")
    where, tokens = where_ref[:, 0:1], where_ref[:, TOKENS_AT : TOKENS_AT + 1]
    lane = iota((entries, 128), 1).astype(F32)
    pick = jnp.where(where == lane, 1.0, 0.0).T[cells : cells + pool]
    facts = jnp.where(lane == 0.0, where - cells, jnp.where(lane == 1.0, tokens, 0.0))
    local_ref[:, QCOLS:ROW] = dot(pick.astype(BF16), facts.astype(BF16)).astype(BF16)
    picked = over_entries(pick, requests)
    copies[0].wait()
    for c in range(CHUNKS):
        cols = slice(c * CHUNK, (c + 1) * CHUNK)
        local_ref[:, cols] = dot(picked, q_ref[:, cols]).astype(BF16)
    turn = my_turn()
    for o, ref in enumerate((s0, s1, s2, s3)):
        at = pl.multiple_of((turn ^ o) * BLOCK, BLOCK)
        ref[...] = q_ref[:, pl.ds(at, BLOCK)]


def pages_kernel(
    got_ref, local_ref, k_ref, v_hbm, answer_ref, own_ref, v_ref, chunk_sems,
):
    devices = got_ref.shape[0]
    cells = devices * CAP
    pool = k_ref.shape[0]
    step = 16
    pair = 2 * HD
    every = slice(None)
    chunks = []
    for c in range(CHUNKS):
        kv_at = (every, every, pl.ds(c * pair, pair))
        chunks.append(
            load(
                (v_hbm.at[kv_at],), (v_ref.at[kv_at],), chunk_sems.at[pl.ds(c, 1)]
            )
        )
    wide = (step, step * PAGE)
    column = iota(wide, 1)
    same = lax.div(column, PAGE) == iota(wide, 0)
    token = lax.rem(column, PAGE).astype(F32)
    side_lane = iota((step, SIDE), 1)
    lane = iota((cells, 128), 1).astype(F32)
    plain = got_ref[:, :, QCOLS:ROW].reshape(cells, SIDE)
    facts = plain.astype(F32)
    pick = jnp.where((facts[:, 0:1] == lane) & (facts[:, 1:2] > 0.0), 1.0, 0.0)
    fetch = pick.T[:pool].astype(BF16)
    pick = pick[:, :pool].astype(BF16)
    tokens = (dot(fetch, plain) + local_ref[:, QCOLS:ROW].astype(F32))[:, 1:2]
    sums = [jnp.zeros((step, SIDE), F32) for _ in range(pool // step)]
    masks = []
    for g in range(pool // step):
        bias = jnp.where(same & (token < tokens[step * g : step * (g + 1)]), 0.0, VERY_LOW)
        masks.append(jnp.concatenate([bias] * (2 * GROUP), axis=0))
    nothing = jnp.zeros((step * GROUP, HD), BF16)
    spans = [slice(step * g, step * (g + 1)) for g in range(pool // step)]

    def score(c, g, rows):
        span = spans[g]
        one, two = (
            jnp.concatenate(
                [rows[span, (GROUP * k + i) * HD : (GROUP * k + i + 1) * HD] for i in range(GROUP)],
                axis=0,
            )
            for k in range(2)
        )
        heads = jnp.concatenate(
            [jnp.concatenate([one, nothing], axis=1), jnp.concatenate([nothing, two], axis=1)], axis=0
        )
        keys = k_ref[span, :, c * pair : (c + 1) * pair].reshape(step * PAGE, pair)
        return dot_t(heads, keys) + masks[g]

    def weigh(scores):
        top = jnp.max(scores, axis=1, keepdims=True)
        weights = jnp.exp2((scores - top) * SCALE_2)
        total = jnp.sum(weights, axis=1, keepdims=True)
        return weights.astype(BF16), total, top * SCALE + jnp.log(total)

    def mix(c, g, weights, total, log_sum):
        span = spans[g]
        values = v_ref[span, :, c * pair : (c + 1) * pair].reshape(step * PAGE, pair)
        mixture = dot(weights, values) / total
        for i in range(2 * GROUP):
            here = slice(step * i, step * (i + 1))
            part = mixture[here, :HD] if i < GROUP else mixture[here, HD:]
            at = c * CHUNK + i * HD
            own_ref[span, at : at + HD] = part.astype(BF16)
            mine = lax.rem(side_lane, QH) == c * 2 * GROUP + i
            sums[g] = jnp.where(mine, log_sum[here], sums[g])

    def ask(c):
        cols = slice(c * CHUNK, (c + 1) * CHUNK)
        asked = got_ref[:, :, cols].reshape(cells, CHUNK)
        return (dot(fetch, asked) + local_ref[:, cols].astype(F32)).astype(BF16)

    steps = [(c, g) for c in range(CHUNKS) for g in range(len(spans))]
    rows = {c: ask(c) for c in range(CHUNKS)}
    scores = {s: score(*s, rows[s[0]]) for s in steps[:2]}
    weighed = {}
    for n, s in enumerate(steps + [None]):
        if n + 2 < len(steps):
            t = steps[n + 2]
            scores[t] = score(*t, rows[t[0]])
        if s is not None:
            weighed[s] = weigh(scores.pop(s))
        if n == 1:
            for copy in chunks[0] + chunks[1]:
                copy.wait()
        if n == 7:
            for copy in chunks[2] + chunks[3]:
                copy.wait()
        if n >= 1:
            mix(*steps[n - 1], *weighed.pop(steps[n - 1]))
    for g in range(pool // step):
        hi, mid, lo = three_parts(sums[g])
        side = jnp.where(side_lane < QH, hi, jnp.where(side_lane < 2 * QH, mid, lo))
        own_ref[step * g : step * (g + 1), QCOLS:ROW] = side.astype(BF16)
    for c in range(0, QCOLS, 640):
        cols = slice(c, c + 640)
        rows = dot(pick, own_ref[:, cols]).astype(BF16)
        answer_ref[:, :, cols] = rows.reshape(devices, CAP, 640)
    rows = dot(pick, own_ref[:, QCOLS:ROW]).astype(BF16)
    answer_ref[:, :, QCOLS:ROW] = rows.reshape(devices, CAP, SIDE)


def prefix_kernel(q0, q1, q2, q3, mine_a, mine_b, other_a, other_b, o0, o1, o2, o3):
    requests = q0.shape[0]
    rows = requests * SHARE
    step = 256
    chunks = [
        (i, slice(c, c + step))
        for i, x in enumerate((mine_a, mine_b))
        for c in range(0, x.shape[0], step)
    ]
    core = lax.rem(lax.axis_index("grp"), 2)
    lane = iota((rows, SIDE), 1)
    asked = (q0, q1, q2, q3)
    outs = (o0, o1, o2, o3)

    def attend(k_refs, v_refs):
        sums = jnp.zeros((rows, SIDE), F32)

        def score(h):
            heads = jnp.concatenate([q[:, h * HD : (h + 1) * HD] for q in asked], axis=0)
            kv = slice(h // GROUP * HD, (h // GROUP + 1) * HD)
            return [dot_t(heads, k_refs[i][c, kv]) for i, c in chunks]

        def weigh(scores):
            top = jnp.max(functools.reduce(jnp.maximum, scores), axis=1, keepdims=True)
            weights = [jnp.exp2((s - top) * SCALE_2) for s in scores]
            total = jnp.sum(functools.reduce(jnp.add, weights), axis=1, keepdims=True)
            return [w.astype(BF16) for w in weights], total, top * SCALE + jnp.log(total)

        def mix(h, weights, total):
            kv = slice(h // GROUP * HD, (h // GROUP + 1) * HD)
            parts = [dot(w, v_refs[i][c, kv]) for (i, c), w in zip(chunks, weights)]
            mixture = (functools.reduce(jnp.add, parts) / total).astype(BF16)
            for o, out in enumerate(outs):
                out[:, h * HD : (h + 1) * HD] = mixture[requests * o : requests * (o + 1)]

        scores, weighed = {0: score(0)}, {}
        for h in range(HEADS + 1):
            if h + 1 < HEADS:
                scores[h + 1] = score(h + 1)
            if h < HEADS:
                *weighed[h], log_sum = weigh(scores.pop(h))
                sums = jnp.where(lax.rem(lane, HEADS) == h, log_sum, sums)
            if h:
                mix(h - 1, *weighed.pop(h - 1))

        hi, mid, lo = three_parts(sums)
        side = jnp.where(lane < HEADS, hi, jnp.where(lane < 2 * HEADS, mid, lo)).astype(BF16)
        for o, out in enumerate(outs):
            out[:, BLOCK:] = side[requests * o : requests * (o + 1)]

    @pl.when(core == 0)
    def _():
        attend((mine_a, mine_b), (other_a, other_b))

    @pl.when(core == 1)
    def _():
        attend((other_a, other_b), (mine_a, mine_b))


def join_kernel(got_ref, own_ref, where_ref, *refs):
    *served, out_hbm, out_ref, sems = refs
    entries = where_ref.shape[0]
    requests = served[0].shape[0]
    cells = got_ref.shape[0] * CAP
    pool = own_ref.shape[0]
    lane = iota((entries, 128), 1)
    where = where_ref[:, 0:1]
    pick = jnp.where(where == lane.astype(F32), 1.0, 0.0).astype(BF16)
    far, near = pick[:, :cells], pick[:, cells : cells + pool]
    side = dot(far, got_ref[:, :, QCOLS:ROW].reshape(cells, SIDE)) + dot(near, own_ref[:, QCOLS:ROW])
    sums = side + pltpu.roll(side, SIDE - QH, 1) + pltpu.roll(side, SIDE - 2 * QH, 1)
    sums = jnp.where(where >= 0.0, sums, VERY_LOW)
    turn = my_turn()
    sent = []

    def bring(o):
        cols = pl.ds(pl.multiple_of((turn ^ o) * BLOCK, 128), BLOCK)
        got = got_ref[:, :, cols].reshape(cells, BLOCK)
        return dot(far, got) + dot(near, own_ref[:, cols])

    def shares(o):
        moved = pltpu.roll(sums, lax.rem(SIDE - (turn ^ o) * HEADS, SIDE), 1)
        pre = served[o][:, BLOCK:].astype(F32)
        pre = pre + pltpu.roll(pre, SIDE - HEADS, 1) + pltpu.roll(pre, SIDE - 2 * HEADS, 1)
        logs = [moved[requests * j : requests * (j + 1)] for j in range(MAXP)]
        top = functools.reduce(jnp.maximum, logs, pre)
        parts = [jnp.exp(x - top) for x in (*logs, pre)]
        total = functools.reduce(jnp.add, parts)
        return [x / total for x in parts]

    weights = [shares(o) for o in range(SHARE)]
    rows = bring(0)
    for o in range(SHARE):
        ahead = bring(o + 1) if o + 1 < SHARE else None
        *parts, part = weights[o]
        at = pl.multiple_of((turn ^ o) * BLOCK, 128)
        for h in range(HEADS):
            here = slice(h * HD, (h + 1) * HD)
            mixture = part[:, h : h + 1] * served[o][:, here].astype(F32)
            for j in range(MAXP):
                mixture = mixture + parts[j][:, h : h + 1] * rows[requests * j : requests * (j + 1), here]
            out_ref[:, pl.ds(pl.multiple_of(at + h * HD, 128), HD)] = mixture.astype(BF16)
        rows = ahead
        cols = pl.ds(at, BLOCK)
        sent += load((out_ref.at[:, cols],), (out_hbm.at[:, cols],), sems.at[pl.ds(o, 1)])
    for copy in sent:
        copy.wait()


def call(kernel, out_shape, flops, *args, in_hbm=(), out_hbm=(), scratch=(), room=24 << 20):
    args = [
        pltpu.with_memory_space_constraint(x, pltpu.HBM) if i in in_hbm else x
        for i, x in enumerate(args)
    ]
    specs = [
        [pl.BlockSpec(memory_space=pl.ANY if i in hbm else pltpu.VMEM) for i in range(n)]
        for n, hbm in ((len(args), in_hbm), (len(out_shape), out_hbm))
    ]
    return pl.pallas_call(
        kernel,
        out_shape=[jax.ShapeDtypeStruct(s, d) for s, d in out_shape],
        in_specs=specs[0],
        out_specs=specs[1],
        scratch_shapes=list(scratch),
        compiler_params=pltpu.CompilerParams(vmem_limit_bytes=room),
        cost_estimate=pl.CostEstimate(flops=flops, bytes_accessed=1 << 22, transcendentals=0),
    )(*args)


def like(x):
    return pltpu.VMEM(x.shape, x.dtype)


def semaphores(*shape):
    return pltpu.SemaphoreType.DMA(shape)


def route(queries, tables, lengths, places, prefix_keys, prefix_values, devices, pool):
    requests, depth = queries.shape[0], prefix_keys.shape[0]
    shape = (devices, CAP, ROW + depth // 4 // CAP * KV)
    args = (queries, tables, lengths, places)
    return call(
        functools.partial(route_kernel, pool),
        [(shape, BF16), ((requests * MAXP, 128), F32)],
        10**8,
        *args,
        prefix_keys,
        prefix_values,
        in_hbm=range(6),
        scratch=(
            *map(like, args),
            pltpu.VMEM((depth, KV), BF16),
            semaphores(5),
        ),
    )


def home(queries, where, pool):
    return call(
        home_kernel,
        [((pool, ROW), BF16)] + [((queries.shape[0], BLOCK), BF16)] * SHARE,
        10**8,
        queries,
        where,
        in_hbm=(0,),
        scratch=(like(queries), semaphores(1)),
    )


def pages(got, local, suffix_keys, suffix_values):
    suffix_keys = pltpu.with_memory_space_constraint(suffix_keys, pltpu.VMEM)
    shape = (got.shape[0], CAP, ROW)
    return call(
        pages_kernel,
        [(shape, BF16), (local.shape, BF16)],
        10**9,
        got,
        local,
        suffix_keys,
        suffix_values,
        in_hbm=(3,),
        scratch=(like(suffix_values), semaphores(CHUNKS)),
    )


def prefix(asked, *kv):
    shape = (asked[0].shape[0], BLOCK + SIDE)
    return call(
        prefix_kernel, [(shape, BF16)] * SHARE, 10**9, *asked, *kv
    )


def join(back, own, where, served):
    shape = (served[0].shape[0], QCOLS)
    (out,) = call(
        join_kernel,
        [(shape, BF16)],
        10**8,
        back,
        own,
        where,
        *served,
        out_hbm=(0,),
        scratch=(pltpu.VMEM(shape, BF16), semaphores(SHARE)),
    )
    return out


def body(
    queries, page_table, suffix_len, place, suffix_keys, suffix_values, prefix_keys, prefix_values
):
    pool = suffix_keys.shape[0]
    devices = lax.axis_size("blk")
    group = lax.axis_size("grp")
    lengths, places = suffix_len.reshape(1, -1), place.reshape(-1, 128)
    send, where = route(
        queries, page_table.T, lengths, places, prefix_keys, prefix_values, devices, pool
    )
    flip = lambda x, bits: lax.ppermute(x, "grp", [(i, i ^ bits) for i in range(group)])
    turned = lambda xs: [flip(x, 4 * o) if o else x for o, x in enumerate(xs)]
    descending = [list(range(devices))[::-1]]
    exchange = lambda x: lax.all_to_all(
        x, "blk", split_axis=0, concat_axis=0, tiled=True, axis_index_groups=descending
    )
    got = exchange(send)
    local, *asked = home(queries, where, pool)
    asked = turned(asked)
    local, *asked = lax.optimization_barrier((local, *asked))
    answer, own = pages(got, local, suffix_keys, suffix_values)
    back = exchange(answer)
    part, own = lax.optimization_barrier((got[:, :, ROW:], own))
    part = part.reshape(-1, KV)
    pairs = [(i, i ^ (devices // 2)) for i in range(devices)]
    both = [
        (g * devices + i, (g ^ 2) * devices + j) for g in range(group) for i, j in pairs
    ]
    around = [
        flip(part, 2), lax.ppermute(part, "blk", pairs), lax.ppermute(part, ("grp", "blk"), both)
    ]
    rest = jnp.concatenate(around, axis=0)
    served = prefix(asked, part, rest, flip(part, 1), flip(rest, 1))
    return join(back, own, where, turned(served))


def solution(mesh):
    return jax.shard_map(
        body,
        mesh=mesh,
        in_specs=(
            P(("grp", "blk"), None),
            P(("grp", "blk"), None),
            P(("grp", "blk")),
            P("grp"),
            P(("grp", "blk"), None, None),
            P(("grp", "blk"), None, None),
            P("blk", None),
            P("blk", None),
        ),
        out_specs=P(("grp", "blk"), None),
        check_vma=False,
    )
```
